128 devices in a mesh: seq: 2 (over core), ctx: 16 (over x, y), tp: 4 (over z).
Axes of the slice: x: 4, y: 4, z: 4, core: 2. Of those that a mesh axis runs over, the one named last changes fastest.
Arguments:
- tokens: bfloat16 [2, 4096, 1088], P('seq', 'ctx'), may hold values from -6 to 6
- cotangent: bfloat16 [2, 4096, 1088], P('seq', 'ctx'), may hold values from -6 to 6
- block_place: int32 [16], replicated, may hold values from 0 to 15, each once
- head_count: int32 [4], replicated, may hold values from 1 to 5, as said below
- ln1_gain: bfloat16 [1088], replicated, may hold values from 0.5 to 1.5
- ln1_bias: bfloat16 [1088], replicated, may hold values from -0.625 to 0.625
- w_qkv: bfloat16 [1088, 3840], P(None, 'tp'), may hold values from -0.1875 to 0.1875
- b_qv: bfloat16 [2560], P('tp'), may hold values from -0.3125 to 0.3125
- w_out: bfloat16 [1280, 1088], P('tp'), may hold values from -3 to 3
- b_out: bfloat16 [1088], replicated, may hold values from -0.625 to 0.625
- ln2_gain: bfloat16 [1088], replicated, may hold values from 0.5 to 1.5
- ln2_bias: bfloat16 [1088], replicated, may hold values from -0.625 to 0.625
- w_up: bfloat16 [1088, 4352], P(None, 'tp'), may hold values from -0.1875 to 0.1875
- b_up: bfloat16 [4352], P('tp'), may hold values from -3 to 3
- w_down: bfloat16 [4352, 1088], P('tp'), may hold values from -0.09375 to 0.09375
- b_down: bfloat16 [1088], replicated, may hold values from -0.625 to 0.625
Outputs:
- output: bfloat16 [2, 4096, 1088], P('seq', 'ctx')
- tokens_grad: float32 [2, 4096, 1088], P('seq', 'ctx')
- ln1_gain_grad: float32 [1088], replicated
- ln1_bias_grad: float32 [1088], replicated
- w_qkv_grad: float32 [1088, 3840], P(None, 'tp')
- b_qv_grad: float32 [2560], P('tp')
- w_out_grad: float32 [1280, 1088], P('tp')
- b_out_grad: float32 [1088], replicated
- ln2_gain_grad: float32 [1088], replicated
- ln2_bias_grad: float32 [1088], replicated
- w_up_grad: float32 [1088, 4352], P(None, 'tp')
- b_up_grad: float32 [4352], P('tp')
- w_down_grad: float32 [4352, 1088], P('tp')
- b_down_grad: float32 [1088], replicated
The draws below stay inside these ranges and needn't reach their ends.
Inputs may be any that keep to these rules, and one draw needn't show every extreme that they name: `block_place`: each block number appears once. `head_count`: live slots sum to 17; some index holds 5.
All inputs are finite; a program needn't handle non-finite values.
Results may differ from the reference program's by a relative error of at most 0.025.
Values may be sent and summed in bfloat16 or wider, within the bound.
A program may use at most 128 MiB of HBM per device.

```python
import jax
import jax.numpy as jnp
import numpy as np
from jax import lax

D = 1088
HEADS = 17
HD = 64
FF = 4352
HSLOT = 5
TOK = 256
SEQS = 2
LENGTH = 4096
SLOTS = 20
N_CTX = 16
N_TP = 4


def compositions(remaining, part_count, upper):
    if part_count == 0:
        return [[]] if remaining == 0 else []
    results = []
    for leading in range(1, upper + 1):
        for remainder in compositions(remaining - leading, part_count - 1, upper):
            results.append([leading] + remainder)
    return results


def draw_head_count(key, part):
    key = jax.random.fold_in(key, 7)
    options_table = jnp.asarray(np.array(compositions(HEADS - HSLOT, N_TP - 1, HSLOT), dtype=np.int32).reshape(-1, N_TP - 1))
    pick_key, place_key = jax.random.split(key)
    chosen = options_table[jax.random.randint(pick_key, (), 0, options_table.shape[0])]
    full_at = jax.random.randint(place_key, (), 0, N_TP)
    shard_ids = jnp.arange(N_TP)
    lower_pick = chosen[jnp.clip(shard_ids, 0, N_TP - 2)]
    upper_pick = chosen[jnp.clip(shard_ids - 1, 0, N_TP - 2)]
    return jnp.where(shard_ids < full_at, lower_pick, jnp.where(shard_ids == full_at, HSLOT, upper_pick)).astype(jnp.int32)


def block_levels(own_key, dims, shards, least, top_value):
    def one(dim, shards_of):
        draws = jax.random.uniform(jax.random.fold_in(jax.random.fold_in(own_key, 6), dim), (shards_of,), jnp.float32, least / len(shards), top_value / len(shards))
        return jnp.repeat(jnp.exp(draws), dims[dim] // shards_of).reshape((-1,) + (1,) * (len(dims) - dim - 1))

    level = one(*shards[0])
    for cut in shards[1:]:
        level = level * one(*cut)
    return level


def normal_values(stream_key, dims, spread, limit, pieces=(), kind=jnp.bfloat16):
    gain = block_levels(stream_key, dims, pieces, -0.22, 0.18) if pieces else 1.0
    drawn = jax.random.normal(stream_key, dims, jnp.float32) * spread * gain
    return jnp.minimum(jnp.maximum(drawn, -limit), limit).astype(kind)


def setup_inputs(seed: int = 0) -> dict:
    keys = jax.random.split(jax.random.key(seed), 17)
    tokens = normal_values(keys[0], (SEQS, LENGTH, D), 1.0, 6.0, ((0, 2), (1, 16)))
    cotangent = normal_values(keys[1], (SEQS, LENGTH, D), 1.0, 6.0, ((0, 2), (1, 16)))
    block_place = jax.random.permutation(keys[2], N_CTX).astype(jnp.int32)
    head_count = draw_head_count(jax.random.fold_in(keys[16], 71), 0)
    ln1_gain = jnp.clip(1.0 + 0.1 * jax.random.normal(keys[4], (D,), jnp.float32), 0.5, 1.5).astype(jnp.bfloat16)
    ln1_bias = normal_values(keys[5], (D,), 0.1, 0.625)
    w_qkv = normal_values(keys[6], (D, SLOTS * 3 * HD), D ** -0.5, 0.1875, ((1, 4),))
    b_qv = normal_values(keys[7], (SLOTS * 2 * HD,), 0.05, 0.3125, ((0, 4),))
    w_out = normal_values(keys[8], (SLOTS * HD, D), (max(1, HEADS * HD * HD // (4 * TOK * N_CTX))) ** -0.5, 3.0, ((0, 4),))
    b_out = normal_values(keys[9], (D,), 0.1, 0.625)
    ln2_gain = jnp.clip(1.0 + 0.1 * jax.random.normal(keys[10], (D,), jnp.float32), 0.5, 1.5).astype(jnp.bfloat16)
    ln2_bias = normal_values(keys[11], (D,), 0.1, 0.625)
    w_up = normal_values(keys[12], (D, FF), D ** -0.5, 0.1875, ((1, 4),))
    b_up = normal_values(keys[13], (FF,), 0.5, 3.0, ((0, 4),))
    w_down = normal_values(keys[14], (FF, D), FF ** -0.5, 0.09375, ((0, 4),))
    b_down = normal_values(keys[15], (D,), 0.1, 0.625)
    return {"tokens": tokens, "cotangent": cotangent, "block_place": block_place, "head_count": head_count, "ln1_gain": ln1_gain, "ln1_bias": ln1_bias, "w_qkv": w_qkv, "b_qv": b_qv, "w_out": w_out, "b_out": b_out, "ln2_gain": ln2_gain, "ln2_bias": ln2_bias, "w_up": w_up, "b_up": b_up, "w_down": w_down, "b_down": b_down}


@jax.custom_vjp
def low(v):
    return lax.optimization_barrier(v.astype(jnp.bfloat16)).astype(jnp.float32)

@jax.custom_vjp
def low_back(v):
    return v

def low_keep(v):
    return (low(v), None)

def low_pass(kept, grad):
    return (grad,)

def back_keep(v):
    return (v, None)

def back_low(kept, grad):
    return (low(grad),)
low.defvjp(low_keep, low_pass)
low_back.defvjp(back_keep, back_low)
EPSILON = 1e-05
NEGATIVE = -1e+30
HIGHEST_PRECISION = lax.Precision.HIGHEST

def matmul(left, right):
    return jnp.dot(left, right, precision=HIGHEST_PRECISION, preferred_element_type=jnp.float32)

def layer_norm(values, norm_gain, norm_bias):
    row_mean = lax.optimization_barrier(jnp.mean(values, axis=-1, keepdims=True))
    centered = values - row_mean
    variance = lax.optimization_barrier(jnp.mean(centered * centered, axis=-1, keepdims=True))
    return centered * lax.rsqrt(variance + EPSILON) * norm_gain + norm_bias

def sequence_forward(inputs, positions, live_slots, params):
    ln1_gain, ln1_bias, w_qkv, b_qv, w_out, b_out, ln2_gain, ln2_bias, w_up, b_up, w_down, b_down = params
    length = inputs.shape[0]
    slot_count = live_slots.shape[0]
    score_scale = HD ** (-0.5)
    normed = low(layer_norm(inputs, ln1_gain, ln1_bias))
    projected = matmul(normed, w_qkv).reshape(length, slot_count, 3, HD)
    bias_pair = b_qv.reshape(slot_count, 2, HD)
    queries = low(low_back(projected[:, :, 0] + bias_pair[:, 0]))
    key_rows = low(low_back(projected[:, :, 1]))
    value_rows = low(low_back(projected[:, :, 2] + bias_pair[:, 1]))
    block_rows = min(512, length)
    block_count = length // block_rows

    def attend(block_pair):
        block_queries, block_positions = block_pair
        scores = jnp.einsum('qse,kse->sqk', block_queries, key_rows, precision=HIGHEST_PRECISION) * score_scale
        scores = low_back(scores)
        allowed = positions[None, None, :] <= block_positions[None, :, None]
        scores = jnp.where(allowed, scores, NEGATIVE)
        row_top = lax.optimization_barrier(jnp.max(scores, axis=-1, keepdims=True))
        weights = jnp.exp(scores - row_top)
        weights = weights / lax.optimization_barrier(jnp.sum(weights, axis=-1, keepdims=True))
        return jnp.einsum('sqk,kse->qse', low(weights), value_rows, precision=HIGHEST_PRECISION)
    attended = lax.map(jax.checkpoint(attend), (queries.reshape(block_count, block_rows, slot_count, HD), positions.reshape(block_count, block_rows)))
    attended = attended.reshape(length, slot_count, HD) * live_slots[None, :, None]
    attended = low(low_back(attended)).reshape(length, slot_count * HD)
    residual = inputs + low_back(matmul(attended, w_out) + b_out)
    normed2 = low(layer_norm(residual, ln2_gain, ln2_bias))
    hidden = low_back(matmul(normed2, w_up) + b_up)
    activated = low(jax.nn.gelu(hidden, approximate=False))
    return residual + matmul(activated, w_down) + b_down

def reference(tokens, cotangent, block_place, head_count, ln1_gain, ln1_bias, w_qkv, b_qv, w_out, b_out, ln2_gain, ln2_bias, w_up, b_up, w_down, b_down):
    slot_ids = jnp.arange(N_TP * HSLOT, dtype=jnp.int32)
    live_slots = (slot_ids % HSLOT < head_count[slot_ids // HSLOT]).astype(jnp.float32)
    row_ids = jnp.arange(TOK * N_CTX, dtype=jnp.int32)
    positions = block_place[row_ids // TOK] * TOK + row_ids % TOK
    params = tuple((argument.astype(jnp.float32) for argument in (ln1_gain, ln1_bias, w_qkv, b_qv, w_out, b_out, ln2_gain, ln2_bias, w_up, b_up, w_down, b_down)))

    def forward(inputs, weight_set):
        return lax.map(lambda sequence: sequence_forward(sequence, positions, live_slots, weight_set), inputs)
    outputs, pullback = jax.vjp(forward, tokens.astype(jnp.float32), params)
    tokens_grad, weight_grads = pullback(cotangent.astype(jnp.float32))
    grad_ln1_gain, grad_ln1_bias, grad_w_qkv, grad_b_qv, grad_w_out, grad_b_out, grad_ln2_gain, grad_ln2_bias, grad_w_up, grad_b_up, grad_w_down, grad_b_down = weight_grads
    return (outputs.astype(jnp.bfloat16), tokens_grad, grad_ln1_gain, grad_ln1_bias, grad_w_qkv, grad_b_qv, grad_w_out, grad_b_out, grad_ln2_gain, grad_ln2_bias, grad_w_up, grad_b_up, grad_w_down, grad_b_down)
```

```python
import functools

import jax
import jax.numpy as jnp
from jax import lax
from jax.experimental import pallas as pl
from jax.experimental.pallas import tpu as pltpu
from jax.sharding import PartitionSpec as P

HD = 64
HSLOT = 5
D = 1088
TOK = 256
N_CTX = 16
N_TP = 4
SPLIT = 3
STEP = 80
SHARE = 96
HALF = SHARE // 2
PIECE = TOK + HALF
ROWS = N_CTX * SHARE
GROUP = 128
WORK = HSLOT * SPLIT
COLS = HSLOT * 3 * HD
FLAT = 3584
HALF_FLAT = FLAT // 2
EPSILON = 1e-05
NEGATIVE = -1e30
BF = jnp.bfloat16
F32 = jnp.float32
MESH = pl.DeviceIdType.MESH
VMEM_LIMIT = 56 * 2**20

VM = pl.BlockSpec(memory_space=pltpu.VMEM)
SM = pl.BlockSpec(memory_space=pltpu.SMEM)
HB = pl.BlockSpec(memory_space=pl.ANY)


def dot(a, b):
    return jnp.dot(a, b, preferred_element_type=F32)


def dot_nt(a, b):
    return lax.dot_general(a, b, (((1,), (1,)), ((), ())), preferred_element_type=F32)


def dot_tn(a, b):
    return lax.dot_general(a, b, (((0,), (0,)), ((), ())), preferred_element_type=F32)


def pack(rows):
    return jnp.concatenate([rows[:HALF], rows[HALF:]], axis=1)


def unpack(packed):
    return jnp.concatenate([packed[:, :HD], packed[:, HD:]], axis=0)


def normalize(values):
    centered = values - jnp.mean(values, axis=-1, keepdims=True)
    inverse = lax.rsqrt(jnp.mean(centered * centered, axis=-1, keepdims=True) + EPSILON)
    return centered * inverse, inverse


def norm_backward(grad_out, normal, inverse, gain):
    grad_normal = grad_out * gain
    grad_mean = jnp.mean(grad_normal, axis=-1, keepdims=True)
    grad_along = jnp.mean(grad_normal * normal, axis=-1, keepdims=True)
    return inverse * (grad_normal - grad_mean - normal * grad_along)


def row_sum(values):
    return jnp.sum(values, axis=0, keepdims=True)


def local_call(body, outs, args, specs=None, scratch=(), flops=0):
    moved = sum(a.size * a.dtype.itemsize for a in args)
    return pl.pallas_call(
        body,
        out_shape=tuple(jax.ShapeDtypeStruct(shape, dtype) for shape, dtype in outs),
        in_specs=specs or [VM] * len(args),
        out_specs=tuple(VM for _ in outs),
        scratch_shapes=list(scratch),
        compiler_params=pltpu.CompilerParams(vmem_limit_bytes=VMEM_LIMIT),
        cost_estimate=pl.CostEstimate(flops=flops, bytes_accessed=moved, transcendentals=0),
    )(*args)


def project_body(tok, vecs, w, send, normed_out):
    normal, _ = normalize(tok[...].astype(F32))
    normed = (normal * vecs[0:1, :] + vecs[1:2, :]).astype(BF)
    normed_out[...] = normed
    projected = (dot(normed, w[...]) + vecs[7:8, :COLS]).astype(BF)
    for s in range(HSLOT):
        base = 3 * HD * s
        pair = projected[:, base + HD : base + 3 * HD]
        queries = projected[:, base : base + HD] * jnp.asarray(HD**-0.5, BF)
        for j in range(SPLIT):
            send[SPLIT * s + j, :TOK, :] = pair
            send[SPLIT * s + j, TOK:, :] = pack(queries[STEP * j : STEP * j + SHARE])
    send[WORK] = jnp.zeros((PIECE, 2 * HD), BF)


def join_shares(shares):
    return jnp.concatenate([shares[0], shares[1][16:], shares[2][16:]], axis=0)


def out_project_body(pieces, w, attended, part):
    heads = []
    for s in range(HSLOT):
        heads.append(join_shares([unpack(pieces[SPLIT * s + j]) for j in range(SPLIT)]))
    rows = jnp.concatenate(heads, axis=1)
    attended[...] = rows
    part[...] = dot(rows, w[...]).astype(BF)


def mlp_body(tok, cot, attn, vecs, w_up, w_down, mlp, gn2, gw_up, gw_down, sums):
    residual = tok[...].astype(F32) + (attn[...].astype(F32) + vecs[4:5, :])
    normal, _ = normalize(residual)
    normed = (normal * vecs[2:3, :] + vecs[3:4, :]).astype(BF)
    hidden = dot(normed, w_up[...]) + vecs[6:7, :]
    cdf = 0.5 * (1.0 + lax.erf(hidden * (0.5**0.5)))
    activated = (hidden * cdf).astype(BF)
    mlp[...] = dot(activated, w_down[...]).astype(BF)
    cot_low = cot[...]
    grad_act = dot_nt(cot_low, w_down[...])
    slope = cdf + hidden * jnp.exp(-0.5 * hidden * hidden) * 0.3989422804014327
    grad_hidden = (grad_act * slope).astype(BF)
    gn2[...] = dot_nt(grad_hidden, w_up[...]).astype(BF)
    gw_down[...] = dot_tn(activated, cot_low).astype(BF)
    gw_up[...] = dot_tn(normed, grad_hidden).astype(BF)
    sums[...] = jnp.zeros_like(sums)
    sums[0:1, :] = row_sum(grad_hidden.astype(F32))
    sums[1:2, :] = row_sum(cot_low.astype(F32))


def middle_body(
    tok, cot, attn, mlp, gn2, vecs, w_out, attended, output, grad_res, gw_out, send, sums
):
    residual = tok[...].astype(F32) + (attn[...].astype(F32) + vecs[4:5, :])
    output[...] = (residual + (mlp[...].astype(F32) + vecs[5:6, :])).astype(BF)
    normal, inverse = normalize(residual)
    grad_norm = gn2[...].astype(F32)
    grad = cot[...].astype(F32) + norm_backward(grad_norm, normal, inverse, vecs[2:3, :])
    grad_res[...] = grad
    grad_low = grad.astype(BF)
    gw_out[...] = dot_tn(attended[...], grad_low).astype(BF)
    live = vecs[8:9, : HSLOT * HD]
    grad_att = (dot_nt(grad_low, w_out[...]) * live).astype(BF)
    for s in range(HSLOT):
        head = grad_att[:, HD * s : HD * (s + 1)]
        for j in range(SPLIT):
            share = head[STEP * j : STEP * j + SHARE]
            if j:
                share = jnp.concatenate([jnp.zeros((16, HD), BF), share[16:]], axis=0)
            send[SPLIT * s + j] = pack(share)
    send[WORK] = jnp.zeros((HALF, 2 * HD), BF)
    sums[...] = jnp.zeros_like(sums)
    sums[0:1, :] = row_sum(grad_norm * normal)
    sums[1:2, :] = row_sum(grad_norm)
    sums[2:3, :] = row_sum(grad_low.astype(F32))


def project_back_body(pieces, normed, w, gw_qkv, gn1, sums):
    columns = []
    for s in range(HSLOT):
        mine = [pieces[SPLIT * s + j] for j in range(SPLIT)]
        pair = mine[0][:TOK].astype(F32)
        for piece in mine[1:]:
            pair = pair + piece[:TOK].astype(F32)
        columns.append(join_shares([unpack(piece[TOK:]) for piece in mine]))
        columns.append(pair.astype(BF))
    grads = jnp.concatenate(columns, axis=1)
    gw_qkv[:, :COLS] = dot_tn(normed[...], grads).astype(BF)
    gw_qkv[:, COLS:] = jnp.zeros((D, D - COLS), BF)
    gn1[...] = dot_nt(grads, w[...]).astype(BF)
    sums[...] = jnp.zeros_like(sums)
    sums[0:1, :COLS] = row_sum(grads.astype(F32))


def last_body(tok, gn1, grad_res, vecs, grad_tok, sums):
    normal, inverse = normalize(tok[...].astype(F32))
    grad_norm = gn1[...].astype(F32)
    grad_tok[...] = grad_res[...] + norm_backward(grad_norm, normal, inverse, vecs[0:1, :])
    sums[...] = jnp.zeros_like(sums)
    sums[0:1, :] = row_sum(grad_norm * normal)
    sums[1:2, :] = row_sum(grad_norm)


def group_keys(first):
    low = first // SHARE
    high = (first + GROUP - 1) // SHARE
    return low * TOK, (high + 1) * TOK


def allowed_keys(first, row_offset):
    low, high = group_keys(first)
    row = first + lax.broadcasted_iota(jnp.int32, (1, GROUP), 1)
    place = jnp.full((1, GROUP), low // TOK, jnp.int32)
    for p in range(low // TOK + 1, high // TOK):
        place = place + (row >= p * SHARE).astype(jnp.int32)
    position = place * (TOK - SHARE) + row + row_offset
    key = low + lax.broadcasted_iota(jnp.int32, (high - low, GROUP), 0)
    return key <= position


def attend_body(order, info, pieces, send, keys, keys_t, queries, out_t, lse):
    for p in range(N_CTX):
        owner = order[p]
        pair = pieces[owner, :TOK, :]
        keys[p * TOK : (p + 1) * TOK, :] = pair
        keys_t[:, p * TOK : (p + 1) * TOK] = pair.T
        rows = unpack(pieces[owner, TOK:, :])
        queries[p * SHARE : (p + 1) * SHARE, :] = jnp.concatenate(
            [rows, jnp.zeros((SHARE, HD), BF)], axis=1
        )
    live = info[1].astype(F32)
    for first in range(0, ROWS, GROUP):
        low, high = group_keys(first)
        block = queries[first : first + GROUP, :]
        edge = jnp.where(
            allowed_keys(first, info[0]), dot_nt(keys[low:high, :], block), NEGATIVE
        )
        top = jnp.max(edge, axis=0, keepdims=True)
        if low:
            body = dot_nt(keys[:low, :], block)
            top = jnp.maximum(top, jnp.max(body, axis=0, keepdims=True))
        weights = jnp.exp(edge - top)
        total = jnp.sum(weights, axis=0, keepdims=True)
        mixed = dot(keys_t[HD:, low:high], weights.astype(BF))
        if low:
            weights = jnp.exp(body - top)
            total = total + jnp.sum(weights, axis=0, keepdims=True)
            mixed = mixed + dot(keys_t[HD:, :low], weights.astype(BF))
        out_t[:, first : first + GROUP] = mixed / total * live
        lse[:, first : first + GROUP] = top + jnp.log(total)
    for p in range(N_CTX):
        rows = out_t[:, p * SHARE : (p + 1) * SHARE].T.astype(BF)
        send[order[p]] = pack(rows)


def attend_back_body(
    order, info, pieces, keys, keys_t, queries, out_t, lse, send, grads, grad_q, dots
):
    for p in range(N_CTX):
        rows = unpack(pieces[order[p]])
        grads[p * SHARE : (p + 1) * SHARE, :] = jnp.concatenate(
            [jnp.zeros((SHARE, HD), BF), rows], axis=1
        )
    for first in range(0, ROWS, GROUP):
        turned = grads[first : first + GROUP, :].astype(F32).T
        dots[:, first : first + GROUP] = jnp.sum(
            turned[HD:, :] * out_t[:, first : first + GROUP], axis=0, keepdims=True
        )

    def inner(acc):
        acc[...] = jnp.zeros_like(acc)
        for first in range(0, ROWS, GROUP):
            low, high = group_keys(first)
            span = slice(first, first + GROUP)
            both = jnp.concatenate([queries[span, :], grads[span, :]], axis=0)
            grad_block = jnp.zeros((HD, GROUP), F32)
            for start, stop in ((0, low), (low, high)):
                if start == stop:
                    continue
                scores = dot_nt(keys[start:stop, :], both)
                weights = jnp.exp(scores[:, :GROUP] - lse[:, span])
                if start == low:
                    weights = jnp.where(allowed_keys(first, info[0]), weights, 0.0)
                grad_scores = (weights * (scores[:, GROUP:] - dots[:, span])).astype(BF)
                pair = jnp.concatenate([grad_scores, weights.astype(BF)], axis=1)
                acc[start:stop, :] += dot(pair, both)
                grad_block = grad_block + dot(keys_t[:HD, start:stop], grad_scores)
            grad_q[:, span] = grad_block * (HD**-0.5)
        for p in range(N_CTX):
            owner = order[p]
            send[owner, :TOK, :] = acc[p * TOK : (p + 1) * TOK, :].astype(BF)
            rows = grad_q[:, p * SHARE : (p + 1) * SHARE].T.astype(BF)
            send[owner, TOK:, :] = pack(rows)

    pl.run_scoped(inner, pltpu.VMEM((N_CTX * TOK, 2 * HD), F32))


def greet(peers):
    barrier = pltpu.get_barrier_semaphore()
    for peer in peers:
        pl.semaphore_signal(barrier, inc=1, device_id=peer, device_id_type=MESH)
    pl.semaphore_wait(barrier, len(peers))


def when(condition, action):
    if condition is True:
        action()
    else:
        pl.when(condition)(action)


def exchange_body(to_workers, src, dst, send_sem, recv_sem, local_sem):
    me = lax.axis_index("ctx")
    greet([{"ctx": lax.rem(me + k, N_CTX)} for k in range(1, N_CTX)])

    def copy(k, peer):
        return pltpu.make_async_remote_copy(
            src_ref=src.at[peer],
            dst_ref=dst.at[me],
            send_sem=send_sem.at[k],
            recv_sem=recv_sem.at[k],
            device_id={"ctx": peer},
            device_id_type=MESH,
        )

    def arrival(k, peer):
        return pltpu.make_async_remote_copy(
            src_ref=src.at[peer],
            dst_ref=dst.at[peer],
            send_sem=send_sem.at[k],
            recv_sem=recv_sem.at[k],
            device_id={"ctx": peer},
            device_id_type=MESH,
        )

    works = me < WORK
    for k in range(1, N_CTX):
        peer = lax.rem(me + k, N_CTX)
        when(peer < WORK if to_workers else works, copy(k, peer).start)
    own = pltpu.make_async_copy(src.at[me], dst.at[me], local_sem)
    when(works, own.start)
    when(works, own.wait)
    for k in range(1, N_CTX):
        peer = lax.rem(me + N_CTX - k, N_CTX)
        when(works if to_workers else peer < WORK, arrival(k, peer).wait_recv)
    for k in range(1, N_CTX):
        peer = lax.rem(me + k, N_CTX)
        when(peer < WORK if to_workers else works, copy(k, peer).wait_send)


def exchange(to_workers, collective_id, src):
    return pl.pallas_call(
        functools.partial(exchange_body, to_workers),
        out_shape=jax.ShapeDtypeStruct(src.shape, src.dtype),
        in_specs=[HB],
        out_specs=HB,
        scratch_shapes=[
            pltpu.SemaphoreType.DMA((N_CTX,)),
            pltpu.SemaphoreType.DMA((N_CTX,)),
            pltpu.SemaphoreType.DMA,
        ],
        compiler_params=pltpu.CompilerParams(collective_id=collective_id, has_side_effects=True),
    )(src)


def tp_sum_body(count, *refs):
    parts, totals = refs[:count], refs[count : 2 * count]
    held, send_sem, recv_sem = refs[2 * count :]
    me = lax.axis_index("tp")
    share = TOK // N_TP

    def rows(index):
        return pl.ds(pl.multiple_of(index * share, share), share)

    greet([{"tp": lax.rem(me + k, N_TP)} for k in range(1, N_TP)])
    copies = []
    for i in range(count):
        for k in range(1, N_TP):
            peer = lax.rem(me + k, N_TP)
            copies.append(
                pltpu.make_async_remote_copy(
                    src_ref=parts[i].at[rows(peer), :],
                    dst_ref=held.at[i, k - 1],
                    send_sem=send_sem.at[0, i, k - 1],
                    recv_sem=recv_sem.at[0, i, k - 1],
                    device_id={"tp": peer},
                    device_id_type=MESH,
                )
            )
            copies[-1].start()
    shared = []
    for i in range(count):
        for k in range(1, N_TP):
            copies[i * (N_TP - 1) + k - 1].wait_recv()
        total = parts[i][rows(me), :].astype(F32)
        for k in range(1, N_TP):
            total = total + held[i, k - 1].astype(F32)
        totals[i][rows(me), :] = total.astype(BF)
        for k in range(1, N_TP):
            peer = lax.rem(me + k, N_TP)
            shared.append(
                pltpu.make_async_remote_copy(
                    src_ref=totals[i].at[rows(me), :],
                    dst_ref=totals[i].at[rows(me), :],
                    send_sem=send_sem.at[1, i, k - 1],
                    recv_sem=recv_sem.at[1, i, k - 1],
                    device_id={"tp": peer},
                    device_id_type=MESH,
                )
            )
            shared[-1].start()
    for i in range(count):
        for k in range(1, N_TP):
            peer = lax.rem(me + N_TP - k, N_TP)
            pltpu.make_async_remote_copy(
                src_ref=totals[i].at[rows(peer), :],
                dst_ref=totals[i].at[rows(peer), :],
                send_sem=send_sem.at[1, i, k - 1],
                recv_sem=recv_sem.at[1, i, k - 1],
                device_id={"tp": peer},
                device_id_type=MESH,
            ).wait_recv()
    for copy in copies + shared:
        copy.wait_send()


def tp_sum(collective_id, *parts):
    count = len(parts)
    return pl.pallas_call(
        functools.partial(tp_sum_body, count),
        out_shape=tuple(jax.ShapeDtypeStruct(p.shape, p.dtype) for p in parts),
        in_specs=[VM] * count,
        out_specs=(VM,) * count,
        scratch_shapes=[
            pltpu.VMEM((count, N_TP - 1, TOK // N_TP, D), BF),
            pltpu.SemaphoreType.DMA((2, count, N_TP - 1)),
            pltpu.SemaphoreType.DMA((2, count, N_TP - 1)),
        ],
        compiler_params=pltpu.CompilerParams(
            collective_id=collective_id, has_side_effects=True, vmem_limit_bytes=VMEM_LIMIT
        ),
    )(*parts)


QUARTER = HALF_FLAT // 4
SIXTEENTH = HALF_FLAT // 16
CUT = 512
VEC_ROW = 704
VEC_ROWS = 144


def weight_sum_body(
    up, down, w_out, w_qkv, vec, out, own, got, got_vec, a1, b1, a2, b2, sa, sb,
    first_send, first_recv, first_local, ring_send, ring_recv, last_send, last_recv,
):
    core = lax.axis_index("seq")
    ctx = lax.axis_index("ctx")
    x, y = ctx // 4, lax.rem(ctx, 4)
    base = core * HALF_FLAT
    partner = {"seq": 1 - core}

    def along_x(k):
        return lax.rem(x + k, 4)

    def along_y(k):
        return lax.rem(y + k, 4)

    def at_x(place):
        return {"ctx": place * 4 + y}

    def at_y(place):
        return {"ctx": x * 4 + place}

    greet(
        [partner]
        + [at_x(along_x(k)) for k in range(1, 4)]
        + [at_y(along_y(k)) for k in range(1, 4)]
    )

    def remote(src, dst, send, recv, device):
        return pltpu.make_async_remote_copy(
            src_ref=src, dst_ref=dst, send_sem=send, recv_sem=recv,
            device_id=device, device_id_type=MESH,
        )

    def rows(start, size):
        return pl.ds(pl.multiple_of(start, 16), size)

    halves = (
        ((up, 0, D, 0), (down, 0, VEC_ROW, D)),
        ((down, VEC_ROW, D - VEC_ROW, 0), (w_out, 0, 320, 384), (w_qkv, 0, D, VEC_ROW)),
    )

    def keep(i, segment):
        ref, start, size, to = segment
        return pltpu.make_async_copy(
            ref.at[pl.ds(start, size), :], own.at[pl.ds(to, size), :], first_local.at[i]
        )

    def give(i, segment):
        ref, start, size, to = segment
        return remote(
            ref.at[pl.ds(start, size), :], got.at[pl.ds(to, size), :],
            first_send.at[i], first_recv.at[i], partner,
        )

    give_vec = remote(vec, got_vec, first_send.at[3], first_recv.at[3], partner)

    for mine in range(2):

        @pl.when(core == mine)
        def _():
            for i, segment in enumerate(halves[1 - mine]):
                give(i, segment).start()
            if mine == 0:
                give_vec.start()
            for i, segment in enumerate(halves[mine]):
                keep(i, segment).start()
            for i, segment in enumerate(halves[mine]):
                keep(i, segment).wait()
                give(i, segment).wait_recv()
            if mine == 1:
                give_vec.wait_recv()
            for i, segment in enumerate(halves[1 - mine]):
                give(i, segment).wait_send()
            if mine == 0:
                give_vec.wait_send()

    def add_rows(i, carry):
        span = rows(i * SIXTEENTH, SIXTEENTH)
        own[span, :] = (own[span, :].astype(F32) + got[span, :].astype(F32)).astype(BF)
        return carry

    lax.fori_loop(0, 16, add_rows, 0)

    @pl.when(core == 1)
    def _():
        own[VEC_ROW : VEC_ROW + VEC_ROWS, D - HD :] = (
            vec[...].astype(F32) + got_vec[...].astype(F32)
        ).astype(BF)

    left, right = slice(0, CUT), slice(CUT, D)

    def sem(stage, part, k):
        return ring_send.at[stage, part, k - 1], ring_recv.at[stage, part, k - 1]

    def stage_start(stage, copy_a, copy_b):
        started = []
        for k in (2, 1, 3):
            started += [copy_a(k, *sem(stage, 0, k)), copy_b(k, *sem(stage, 1, k))]
        for copy in started:
            copy.start()
        return started

    def quarter_sum(k0, src, columns, place, size, held):
        total = src[rows(place * size, size), columns].astype(F32)
        for k in range(3):
            total = total + held[k].astype(F32)
        return total.astype(BF)

    started = stage_start(
        0,
        lambda k, s, r: remote(
            own.at[rows(along_x(k) * QUARTER, QUARTER), left], a1.at[k - 1], s, r, at_x(along_x(k))
        ),
        lambda k, s, r: remote(
            own.at[rows(along_y(k) * QUARTER, QUARTER), right], b1.at[k - 1], s, r, at_y(along_y(k))
        ),
    )
    for copy in started:
        copy.wait_recv()
    sa[...] = quarter_sum(0, own, left, x, QUARTER, a1)
    sb[...] = quarter_sum(0, own, right, y, QUARTER, b1)
    pending = started
    started = stage_start(
        1,
        lambda k, s, r: remote(
            sa.at[rows(along_y(k) * SIXTEENTH, SIXTEENTH), :], a2.at[k - 1], s, r, at_y(along_y(k))
        ),
        lambda k, s, r: remote(
            sb.at[rows(along_x(k) * SIXTEENTH, SIXTEENTH), :], b2.at[k - 1], s, r, at_x(along_x(k))
        ),
    )
    for copy in started:
        copy.wait_recv()
    pending += started

    def piece_a(px, py):
        return out.at[rows(base + px * QUARTER + py * SIXTEENTH, SIXTEENTH), left]

    def piece_b(px, py):
        return out.at[rows(base + py * QUARTER + px * SIXTEENTH, SIXTEENTH), right]

    piece_a(x, y)[...] = quarter_sum(0, sa, slice(0, CUT), y, SIXTEENTH, a2)
    piece_b(x, y)[...] = quarter_sum(0, sb, slice(0, D - CUT), x, SIXTEENTH, b2)

    pending += stage_start(
        2,
        lambda k, s, r: remote(piece_a(x, y), piece_a(x, y), s, r, at_y(along_y(k))),
        lambda k, s, r: remote(piece_b(x, y), piece_b(x, y), s, r, at_x(along_x(k))),
    )
    for k in range(1, 4):
        there = along_y(4 - k)
        remote(piece_a(x, there), piece_a(x, there), *sem(2, 0, k), at_y(there)).wait_recv()
        there = along_x(4 - k)
        remote(piece_b(there, y), piece_b(there, y), *sem(2, 1, k), at_x(there)).wait_recv()

    def band_a(px):
        return out.at[rows(base + px * QUARTER, QUARTER), left]

    def band_b(py):
        return out.at[rows(base + py * QUARTER, QUARTER), right]

    pending += stage_start(
        3,
        lambda k, s, r: remote(band_a(x), band_a(x), s, r, at_x(along_x(k))),
        lambda k, s, r: remote(band_b(y), band_b(y), s, r, at_y(along_y(k))),
    )
    for k in range(1, 4):
        there = along_x(4 - k)
        remote(band_a(there), band_a(there), *sem(3, 0, k), at_x(there)).wait_recv()
        there = along_y(4 - k)
        remote(band_b(there), band_b(there), *sem(3, 1, k), at_y(there)).wait_recv()

    mine = out.at[rows(base, HALF_FLAT), :]
    theirs = out.at[rows(HALF_FLAT - base, HALF_FLAT), :]
    last = remote(mine, mine, last_send, last_recv, partner)
    last.start()
    remote(theirs, theirs, last_send, last_recv, partner).wait_recv()
    last.wait_send()
    for copy in pending:
        copy.wait_send()


def weight_sum(collective_id, up, down, w_out, w_qkv, vec):
    dma = pltpu.SemaphoreType.DMA
    return pl.pallas_call(
        weight_sum_body,
        out_shape=jax.ShapeDtypeStruct((FLAT, D), BF),
        in_specs=[HB, HB, HB, HB, VM],
        out_specs=VM,
        scratch_shapes=[
            pltpu.VMEM((HALF_FLAT, D), BF),
            pltpu.VMEM((HALF_FLAT, D), BF),
            pltpu.VMEM((VEC_ROWS, HD), BF),
            pltpu.VMEM((3, QUARTER, CUT), BF),
            pltpu.VMEM((3, QUARTER, D - CUT), BF),
            pltpu.VMEM((3, SIXTEENTH, CUT), BF),
            pltpu.VMEM((3, SIXTEENTH, D - CUT), BF),
            pltpu.VMEM((QUARTER, CUT), BF),
            pltpu.VMEM((QUARTER, D - CUT), BF),
            dma((4,)), dma((4,)), dma((3,)),
            dma((4, 2, 3)), dma((4, 2, 3)),
            dma, dma,
        ],
        compiler_params=pltpu.CompilerParams(
            collective_id=collective_id, has_side_effects=True, vmem_limit_bytes=VMEM_LIMIT
        ),
    )(up, down, w_out, w_qkv, vec)


def on_device(
    tokens, cotangent, block_place, head_count, ln1_gain, ln1_bias, w_qkv, b_qv, w_out, b_out,
    ln2_gain, ln2_bias, w_up, b_up, w_down, b_down,
):
    tok, cot = tokens[0], cotangent[0]
    ctx = lax.axis_index("ctx")
    live_count = head_count[lax.axis_index("tp")]
    order = jnp.argsort(block_place).astype(jnp.int32)
    head_live = (ctx // SPLIT < live_count).astype(jnp.int32)
    info = jnp.stack([lax.rem(ctx, SPLIT) * STEP, head_live]).astype(jnp.int32)

    def widen(row):
        row = row.astype(F32)
        return jnp.pad(row, (0, D - row.shape[0]))

    bias_pair = b_qv.reshape(HSLOT, 2, HD).astype(F32)
    bias_row = jnp.stack(
        [bias_pair[:, 0], jnp.zeros((HSLOT, HD), F32), bias_pair[:, 1]], axis=1
    ).reshape(COLS)
    live_row = (jnp.arange(HSLOT * HD) // HD < live_count).astype(F32)
    vecs = jnp.stack(
        [
            widen(v)
            for v in (
                ln1_gain, ln1_bias, ln2_gain, ln2_bias, b_out, b_down, b_up, bias_row, live_row
            )
        ]
    )

    send1, normed1 = local_call(
        project_body, [((N_CTX, PIECE, 2 * HD), BF), ((TOK, D), BF)], [tok, vecs, w_qkv]
    )
    pieces1 = exchange(True, 1, send1)
    send2, keys, keys_t, queries, out_t, lse = local_call(
        attend_body,
        [
            ((N_CTX, HALF, 2 * HD), BF),
            ((N_CTX * TOK, 2 * HD), BF),
            ((2 * HD, N_CTX * TOK), BF),
            ((ROWS, 2 * HD), BF),
            ((HD, ROWS), F32),
            ((1, ROWS), F32),
        ],
        [order, info, pieces1],
        specs=[SM, SM, VM],
    )
    pieces2 = exchange(False, 2, send2)
    attended, attn_part = local_call(
        out_project_body, [((TOK, HSLOT * HD), BF), ((TOK, D), BF)], [pieces2, w_out]
    )
    (attn,) = tp_sum(3, attn_part)
    mlp_part, gn2_part, gw_up, gw_down, sums_mlp = local_call(
        mlp_body,
        [((TOK, D), BF), ((TOK, D), BF), ((D, D), BF), ((D, D), BF), ((8, D), F32)],
        [tok, cot, attn, vecs, w_up, w_down],
    )
    mlp, gn2 = tp_sum(4, mlp_part, gn2_part)
    output, grad_res, gw_out, send3, sums_mid = local_call(
        middle_body,
        [
            ((TOK, D), BF),
            ((TOK, D), F32),
            ((HSLOT * HD, D), BF),
            ((N_CTX, HALF, 2 * HD), BF),
            ((8, D), F32),
        ],
        [tok, cot, attn, mlp, gn2, vecs, w_out, attended],
    )
    pieces3 = exchange(True, 5, send3)
    (send4,) = local_call(
        attend_back_body,
        [((N_CTX, PIECE, 2 * HD), BF)],
        [order, info, pieces3, keys, keys_t, queries, out_t, lse],
        specs=[SM, SM] + [VM] * 6,
        scratch=[
            pltpu.VMEM((ROWS, 2 * HD), BF),
            pltpu.VMEM((HD, ROWS), F32),
            pltpu.VMEM((1, ROWS), F32),
        ],
    )
    pieces4 = exchange(False, 6, send4)
    gw_qkv, gn1_part, sums_qkv = local_call(
        project_back_body,
        [((D, D), BF), ((TOK, D), BF), ((8, D), F32)],
        [pieces4, normed1, w_qkv],
    )
    (gn1,) = tp_sum(7, gn1_part)
    grad_tok, sums_last = local_call(
        last_body, [((TOK, D), F32), ((8, D), F32)], [tok, gn1, grad_res, vecs]
    )
    vec = jnp.concatenate(
        [sums_last[:2], sums_mid[:3], sums_mlp[:2], sums_qkv[:1]], axis=0
    ).astype(BF)
    vec = jnp.pad(vec.reshape(8 * D // HD, HD), ((0, VEC_ROWS - 8 * D // HD), (0, 0)))
    flat = weight_sum(8, gw_up, gw_down, gw_out, gw_qkv, vec)
    top = 2 * D + HSLOT * HD
    g = flat[top : top + 8 * D // HD, D - HD :].reshape(8, D).astype(F32)
    g_bqv = g[7, :COLS].reshape(HSLOT, 3, HD)
    return (
        output[None],
        grad_tok[None],
        g[0],
        g[1],
        flat[top:, :COLS].astype(F32),
        jnp.stack([g_bqv[:, 0], g_bqv[:, 2]], axis=1).reshape(HSLOT * 2 * HD),
        flat[2 * D : top].astype(F32),
        g[4],
        g[2],
        g[3],
        flat[:D].astype(F32),
        g[5],
        flat[D : 2 * D].astype(F32),
        g[6],
    )


def solution(mesh):
    in_specs = (
        P("seq", "ctx", None), P("seq", "ctx", None), P(), P(), P(), P(), P(None, "tp"), P("tp"),
        P("tp", None), P(), P(), P(), P(None, "tp"), P("tp"), P("tp", None), P(),
    )
    out_specs = (
        P("seq", "ctx", None), P("seq", "ctx", None), P(), P(), P(None, "tp"), P("tp"),
        P("tp", None), P(), P(), P(), P(None, "tp"), P("tp"), P("tp", None), P(),
    )
    return jax.shard_map(
        on_device, mesh=mesh, in_specs=in_specs, out_specs=out_specs, check_vma=False
    )
```

```python
import functools

import jax
import jax.numpy as jnp
from jax import lax
from jax.experimental import pallas as pl
from jax.experimental.pallas import tpu as pltpu
from jax.sharding import PartitionSpec as P

HD = 64
HSLOT = 5
D = 1088
TOK = 256
N_CTX = 16
N_TP = 4
SPLIT = 3
STEP = 80
SHARE = 96
HALF = SHARE // 2
PIECE = TOK + HALF
ROWS = N_CTX * SHARE
GROUP = 128
WORK = HSLOT * SPLIT
COLS = HSLOT * 3 * HD
FIRST = 1024
REST = D - FIRST
SECOND = 768
CUT = 512
EPSILON = 1e-05
NEGATIVE = -1e30
BF = jnp.bfloat16
F32 = jnp.float32
MESH = pl.DeviceIdType.MESH
VMEM_LIMIT = 56 * 2**20

VM = pl.BlockSpec(memory_space=pltpu.VMEM)
SM = pl.BlockSpec(memory_space=pltpu.SMEM)
HB = pl.BlockSpec(memory_space=pl.ANY)


def dot(a, b):
    return jnp.dot(a, b, preferred_element_type=F32)


def dot_nt(a, b):
    return lax.dot_general(a, b, (((1,), (1,)), ((), ())), preferred_element_type=F32)


def dot_tn(a, b):
    return lax.dot_general(a, b, (((0,), (0,)), ((), ())), preferred_element_type=F32)


def pack(rows):
    return jnp.concatenate([rows[:HALF], rows[HALF:]], axis=1)


def unpack(packed):
    return jnp.concatenate([packed[:, :HD], packed[:, HD:]], axis=0)


def normalize(values):
    centered = values - jnp.mean(values, axis=-1, keepdims=True)
    inverse = lax.rsqrt(jnp.mean(centered * centered, axis=-1, keepdims=True) + EPSILON)
    return centered * inverse, inverse


def norm_backward(grad_out, normal, inverse, gain):
    grad_normal = grad_out * gain
    grad_mean = jnp.mean(grad_normal, axis=-1, keepdims=True)
    grad_along = jnp.mean(grad_normal * normal, axis=-1, keepdims=True)
    return inverse * (grad_normal - grad_mean - normal * grad_along)


def row_sum(values):
    return jnp.sum(values, axis=0, keepdims=True)


def local_call(body, outs, args, specs=None, scratch=(), flops=0):
    moved = sum(a.size * a.dtype.itemsize for a in args)
    return pl.pallas_call(
        body,
        out_shape=tuple(jax.ShapeDtypeStruct(shape, dtype) for shape, dtype in outs),
        in_specs=specs or [VM] * len(args),
        out_specs=tuple(VM for _ in outs),
        scratch_shapes=list(scratch),
        compiler_params=pltpu.CompilerParams(vmem_limit_bytes=VMEM_LIMIT),
        cost_estimate=pl.CostEstimate(flops=flops, bytes_accessed=moved, transcendentals=0),
    )(*args)


def project_body(tok_t, cot_t, vecs_low, w_t, send, normed_out, tok, cot, vecs):
    tok[...] = tok_t[...].T
    cot[...] = cot_t[...].T
    vecs[...] = vecs_low[...].astype(F32)
    normal, _ = normalize(tok[...].astype(F32))
    normed = (normal * vecs[0:1, :] + vecs[1:2, :]).astype(BF)
    normed_out[...] = normed
    projected = dot_nt(normed, w_t[...])
    upper = lax.broadcasted_iota(jnp.int32, (1, 2 * HD), 1) >= HD
    for s in range(HSLOT):
        base = 3 * HD * s
        bias = vecs[7:8, 2 * HD * s : 2 * HD * (s + 1)]
        pair = projected[:, base + HD : base + 3 * HD] + jnp.where(upper, bias, 0.0)
        pair = pair.astype(BF)
        queries = (projected[:, base : base + HD] + bias[:, :HD]).astype(BF)
        queries = queries * jnp.asarray(HD**-0.5, BF)
        for j in range(SPLIT):
            send[SPLIT * s + j, :TOK, :] = pair
            send[SPLIT * s + j, TOK:, :] = pack(queries[STEP * j : STEP * j + SHARE])
    send[WORK] = jnp.zeros((PIECE, 2 * HD), BF)


def join_shares(shares):
    return jnp.concatenate([shares[0], shares[1][16:], shares[2][16:]], axis=0)


def out_project_body(pieces, w, attended, part):
    heads = []
    for s in range(HSLOT):
        heads.append(join_shares([unpack(pieces[SPLIT * s + j]) for j in range(SPLIT)]))
    rows = jnp.concatenate(heads, axis=1)
    attended[...] = rows
    part[...] = dot(rows, w[...]).astype(BF)


def mlp_body(tok, cot, attn, vecs, w_up, w_down, mlp, gn2, gw_up, gw_down, sums):
    residual = tok[...].astype(F32) + (attn[...].astype(F32) + vecs[4:5, :])
    normal, _ = normalize(residual)
    normed = (normal * vecs[2:3, :] + vecs[3:4, :]).astype(BF)
    hidden = dot(normed, w_up[...]) + vecs[6:7, :]
    cdf = 0.5 * (1.0 + lax.erf(hidden * (0.5**0.5)))
    activated = (hidden * cdf).astype(BF)
    mlp[...] = dot(activated, w_down[...]).astype(BF)
    cot_low = cot[...]
    grad_act = dot_nt(cot_low, w_down[...])
    slope = cdf + hidden * jnp.exp(-0.5 * hidden * hidden) * 0.3989422804014327
    grad_hidden = (grad_act * slope).astype(BF)
    gn2[...] = dot_nt(grad_hidden, w_up[...]).astype(BF)
    gw_down[...] = dot_tn(activated, cot_low).astype(BF)
    gw_up[...] = dot_tn(normed, grad_hidden).astype(BF)
    sums[...] = jnp.zeros_like(sums)
    sums[0:1, :] = row_sum(grad_hidden.astype(F32))
    sums[1:2, :] = row_sum(cot_low.astype(F32))


def middle_body(
    head_count, tok, cot, attn, mlp, gn2, vecs, w_out, attended,
    output_t, grad_res, gw_out, send, sums,
):
    residual = tok[...].astype(F32) + (attn[...].astype(F32) + vecs[4:5, :])
    output_t[...] = (residual + (mlp[...].astype(F32) + vecs[5:6, :])).astype(BF).T
    normal, inverse = normalize(residual)
    grad_norm = gn2[...].astype(F32)
    grad = cot[...].astype(F32) + norm_backward(grad_norm, normal, inverse, vecs[2:3, :])
    grad_res[...] = grad
    grad_low = grad.astype(BF)
    gw_out[...] = dot_tn(attended[...], grad_low).astype(BF)
    live_lanes = head_count[lax.axis_index("tp")] * HD
    lane = lax.broadcasted_iota(jnp.int32, (1, HSLOT * HD), 1)
    live = (lane < live_lanes).astype(F32)
    grad_att = (dot_nt(grad_low, w_out[...]) * live).astype(BF)
    for s in range(HSLOT):
        head = grad_att[:, HD * s : HD * (s + 1)]
        for j in range(SPLIT):
            share = head[STEP * j : STEP * j + SHARE]
            if j:
                share = jnp.concatenate([jnp.zeros((16, HD), BF), share[16:]], axis=0)
            send[SPLIT * s + j] = pack(share)
    send[WORK] = jnp.zeros((HALF, 2 * HD), BF)
    sums[...] = jnp.zeros_like(sums)
    sums[0:1, :] = row_sum(grad_norm * normal)
    sums[1:2, :] = row_sum(grad_norm)
    sums[2:3, :] = row_sum(grad_low.astype(F32))


def project_back_body(pieces, tok, normed, w_t, sums_mid, sums_mlp, gw_qkv_t, gn1, vec):
    columns, biases = [], []
    for s in range(HSLOT):
        mine = [pieces[SPLIT * s + j] for j in range(SPLIT)]
        pair = mine[0][:TOK].astype(F32)
        for piece in mine[1:]:
            pair = pair + piece[:TOK].astype(F32)
        pair = pair.astype(BF)
        queries = join_shares([unpack(piece[TOK:]) for piece in mine])
        columns += [queries, pair]
        biases += [row_sum(queries.astype(F32)), row_sum(pair.astype(F32))[:, HD:]]
    grads = jnp.concatenate(columns, axis=1)
    gw_qkv_t[...] = dot_tn(grads, normed[...]).astype(BF)
    part = dot(grads, w_t[...])
    gn1[...] = part.astype(BF)
    normal, _ = normalize(tok[...].astype(F32))
    vec[0:1, :] = row_sum(part * normal)
    vec[1:2, :] = row_sum(part)
    vec[2:5, :] = sums_mid[0:3, :]
    vec[5:7, :] = sums_mlp[0:2, :]
    vec[7:8, : HSLOT * 2 * HD] = jnp.concatenate(biases, axis=1)
    vec[7:8, HSLOT * 2 * HD :] = jnp.zeros((1, D - HSLOT * 2 * HD), F32)
    vec[8:, :] = jnp.zeros((8, D), F32)


def group_keys(first):
    low = first // SHARE
    high = (first + GROUP - 1) // SHARE
    return low * TOK, (high + 1) * TOK


def allowed_keys(first, row_offset):
    low, high = group_keys(first)
    row = first + lax.broadcasted_iota(jnp.int32, (1, GROUP), 1)
    place = jnp.full((1, GROUP), low // TOK, jnp.int32)
    for p in range(low // TOK + 1, high // TOK):
        place = place + (row >= p * SHARE).astype(jnp.int32)
    position = place * (TOK - SHARE) + row + row_offset
    key = low + lax.broadcasted_iota(jnp.int32, (high - low, GROUP), 0)
    return key <= position


def place_order(block_place, order):
    for i in range(N_CTX):
        order[block_place[i]] = i


def attend_body(
    block_place, head_count, pieces, send, keys, keys_t, queries, out_t, lse, order
):
    place_order(block_place, order)
    ctx = lax.axis_index("ctx")
    row_offset = lax.rem(ctx, SPLIT) * STEP
    live = (ctx // SPLIT < head_count[lax.axis_index("tp")]).astype(F32)
    for p in range(N_CTX):
        owner = order[p]
        pair = pieces[owner, :TOK, :]
        keys[p * TOK : (p + 1) * TOK, :] = pair
        keys_t[:, p * TOK : (p + 1) * TOK] = pair.T
        rows = unpack(pieces[owner, TOK:, :])
        queries[p * SHARE : (p + 1) * SHARE, :] = jnp.concatenate(
            [rows, jnp.zeros((SHARE, HD), BF)], axis=1
        )
    for first in range(0, ROWS, GROUP):
        low, high = group_keys(first)
        block = queries[first : first + GROUP, :]
        edge = jnp.where(
            allowed_keys(first, row_offset), dot_nt(keys[low:high, :], block), NEGATIVE
        )
        top = jnp.max(edge, axis=0, keepdims=True)
        if low:
            body = dot_nt(keys[:low, :], block)
            top = jnp.maximum(top, jnp.max(body, axis=0, keepdims=True))
        weights = jnp.exp(edge - top)
        total = jnp.sum(weights, axis=0, keepdims=True)
        mixed = dot(keys_t[HD:, low:high], weights.astype(BF))
        if low:
            weights = jnp.exp(body - top)
            total = total + jnp.sum(weights, axis=0, keepdims=True)
            mixed = mixed + dot(keys_t[HD:, :low], weights.astype(BF))
        out_t[:, first : first + GROUP] = mixed / total * live
        lse[:, first : first + GROUP] = top + jnp.log(total)
    for p in range(N_CTX):
        rows = out_t[:, p * SHARE : (p + 1) * SHARE].T.astype(BF)
        send[order[p]] = pack(rows)


def attend_back_body(
    block_place, pieces, keys, keys_t, queries, out_t, lse, send, grads, grad_q, dots, order
):
    place_order(block_place, order)
    row_offset = lax.rem(lax.axis_index("ctx"), SPLIT) * STEP
    for p in range(N_CTX):
        rows = unpack(pieces[order[p]])
        grads[p * SHARE : (p + 1) * SHARE, :] = jnp.concatenate(
            [jnp.zeros((SHARE, HD), BF), rows], axis=1
        )
    for first in range(0, ROWS, GROUP):
        turned = grads[first : first + GROUP, :].astype(F32).T
        dots[:, first : first + GROUP] = jnp.sum(
            turned[HD:, :] * out_t[:, first : first + GROUP], axis=0, keepdims=True
        )

    def inner(acc):
        acc[...] = jnp.zeros_like(acc)
        for first in range(0, ROWS, GROUP):
            low, high = group_keys(first)
            span = slice(first, first + GROUP)
            both = jnp.concatenate([queries[span, :], grads[span, :]], axis=0)
            grad_block = jnp.zeros((HD, GROUP), F32)
            for start, stop in ((0, low), (low, high)):
                if start == stop:
                    continue
                scores = dot_nt(keys[start:stop, :], both)
                weights = jnp.exp(scores[:, :GROUP] - lse[:, span])
                if start == low:
                    weights = jnp.where(allowed_keys(first, row_offset), weights, 0.0)
                grad_scores = (weights * (scores[:, GROUP:] - dots[:, span])).astype(BF)
                pair = jnp.concatenate([grad_scores, weights.astype(BF)], axis=1)
                acc[start:stop, :] += dot(pair, both)
                grad_block = grad_block + dot(keys_t[:HD, start:stop], grad_scores)
            grad_q[:, span] = grad_block * (HD**-0.5)
        for p in range(N_CTX):
            owner = order[p]
            send[owner, :TOK, :] = acc[p * TOK : (p + 1) * TOK, :].astype(BF)
            rows = grad_q[:, p * SHARE : (p + 1) * SHARE].T.astype(BF)
            send[owner, TOK:, :] = pack(rows)

    pl.run_scoped(inner, pltpu.VMEM((N_CTX * TOK, 2 * HD), F32))


def greet(peers):
    barrier = pltpu.get_barrier_semaphore()
    for peer in peers:
        pl.semaphore_signal(barrier, inc=1, device_id=peer, device_id_type=MESH)
    pl.semaphore_wait(barrier, len(peers))


def when(condition, action):
    if condition is True:
        action()
    else:
        pl.when(condition)(action)


def exchange_body(to_workers, src, dst, send_sem, recv_sem, local_sem):
    me = lax.axis_index("ctx")
    greet([{"ctx": lax.rem(me + k, N_CTX)} for k in range(1, N_CTX)])

    def copy(k, peer):
        return pltpu.make_async_remote_copy(
            src_ref=src.at[peer],
            dst_ref=dst.at[me],
            send_sem=send_sem.at[k],
            recv_sem=recv_sem.at[k],
            device_id={"ctx": peer},
            device_id_type=MESH,
        )

    def arrival(k, peer):
        return pltpu.make_async_remote_copy(
            src_ref=src.at[peer],
            dst_ref=dst.at[peer],
            send_sem=send_sem.at[k],
            recv_sem=recv_sem.at[k],
            device_id={"ctx": peer},
            device_id_type=MESH,
        )

    works = me < WORK
    for k in range(1, N_CTX):
        peer = lax.rem(me + k, N_CTX)
        when(peer < WORK if to_workers else works, copy(k, peer).start)
    own = pltpu.make_async_copy(src.at[me], dst.at[me], local_sem)
    when(works, own.start)
    when(works, own.wait)
    for k in range(1, N_CTX):
        peer = lax.rem(me + N_CTX - k, N_CTX)
        when(works if to_workers else peer < WORK, arrival(k, peer).wait_recv)
    for k in range(1, N_CTX):
        peer = lax.rem(me + k, N_CTX)
        when(peer < WORK if to_workers else works, copy(k, peer).wait_send)


def exchange(to_workers, collective_id, src):
    return pl.pallas_call(
        functools.partial(exchange_body, to_workers),
        out_shape=jax.ShapeDtypeStruct(src.shape, src.dtype),
        in_specs=[HB],
        out_specs=HB,
        scratch_shapes=[
            pltpu.SemaphoreType.DMA((N_CTX,)),
            pltpu.SemaphoreType.DMA((N_CTX,)),
            pltpu.SemaphoreType.DMA,
        ],
        compiler_params=pltpu.CompilerParams(collective_id=collective_id, has_side_effects=True),
    )(src)


def remote(src, dst, send, recv, device):
    return pltpu.make_async_remote_copy(
        src_ref=src,
        dst_ref=dst,
        send_sem=send,
        recv_sem=recv,
        device_id=device,
        device_id_type=MESH,
    )


def rows(start, size):
    return pl.ds(pl.multiple_of(start, 16), size)


def tp_steps(parts, totals, held, send_sem, recv_sem, pending):
    me = lax.axis_index("tp")
    share = TOK // N_TP
    count = len(parts)
    started = {}
    for i in range(count):
        for k in (2, 1, 3):
            peer = lax.rem(me + k, N_TP)
            started[i, k] = remote(
                parts[i].at[rows(peer * share, share), :], held.at[i, k - 1],
                send_sem.at[0, i, k - 1], recv_sem.at[0, i, k - 1], {"tp": peer},
            )
            started[i, k].start()
    pending += started.values()
    yield
    own = rows(me * share, share)
    for i in range(count):
        total = parts[i][own, :].astype(F32)
        for k in range(1, N_TP):
            started[i, k].wait_recv()
            total = total + held[i, k - 1].astype(F32)
        totals[i][own, :] = total.astype(BF)
        for k in (2, 1, 3):
            copy = remote(
                totals[i].at[own, :], totals[i].at[own, :],
                send_sem.at[1, i, k - 1], recv_sem.at[1, i, k - 1],
                {"tp": lax.rem(me + k, N_TP)},
            )
            copy.start()
            pending.append(copy)
    yield
    for i in range(count):
        for k in range(1, N_TP):
            peer = lax.rem(me + N_TP - k, N_TP)
            there = totals[i].at[rows(peer * share, share), :]
            remote(
                there, there, send_sem.at[1, i, k - 1], recv_sem.at[1, i, k - 1], {"tp": peer}
            ).wait_recv()


def tp_scratch(count):
    return [
        pltpu.VMEM((count, N_TP - 1, TOK // N_TP, D), BF),
        pltpu.SemaphoreType.DMA((2, count, N_TP - 1)),
        pltpu.SemaphoreType.DMA((2, count, N_TP - 1)),
    ]


def tp_peers():
    me = lax.axis_index("tp")
    return [{"tp": lax.rem(me + k, N_TP)} for k in range(1, N_TP)]


class Plane:
    def __init__(self):
        ctx = lax.axis_index("ctx")
        self.core = lax.axis_index("seq")
        self.partner = {"seq": 1 - self.core}
        self.x, self.y = ctx // 4, lax.rem(ctx, 4)

    def x_of(self, k):
        return lax.rem(self.x + k, 4)

    def y_of(self, k):
        return lax.rem(self.y + k, 4)

    def at_x(self, place):
        return {"ctx": place * 4 + self.y}

    def at_y(self, place):
        return {"ctx": self.x * 4 + place}

    def peers(self):
        return (
            [self.partner]
            + [self.at_x(self.x_of(k)) for k in range(1, 4)]
            + [self.at_y(self.y_of(k)) for k in range(1, 4)]
        )


LEFT, RIGHT = slice(0, CUT), slice(CUT, D)


def reduce_steps(plane, half, segments, held, sems, result, pending, late=None):
    own, got, a1, b1, a2, b2, sa, sb = held
    first_send, first_recv, first_local, ring_send, ring_recv = sems
    red_a, red_b = result
    quarter, part = half // 4, half // 16

    def keep(i, segment):
        ref, start, size, to = segment
        return pltpu.make_async_copy(
            ref.at[pl.ds(start, size), :], own.at[pl.ds(to, size), :], first_local.at[i]
        )

    def give(i, segment):
        ref, start, size, to = segment
        return remote(
            ref.at[pl.ds(start, size), :], got.at[pl.ds(to, size), :],
            first_send.at[i], first_recv.at[i], plane.partner,
        )

    for mine in range(2):

        @pl.when(plane.core == mine)
        def _():
            for i, segment in enumerate(segments[1 - mine]):
                give(i, segment).start()
            for i, segment in enumerate(segments[mine]):
                keep(i, segment).start()

    yield
    if late is not None:
        late()
    for mine in range(2):

        @pl.when(plane.core == mine)
        def _():
            for i, segment in enumerate(segments[mine]):
                keep(i, segment).wait()
                give(i, segment).wait_recv()
            for i, segment in enumerate(segments[1 - mine]):
                give(i, segment).wait_send()

    def add_rows(i, carry):
        span = rows(i * part, part)
        own[span, :] = (own[span, :].astype(F32) + got[span, :].astype(F32)).astype(BF)
        return carry

    lax.fori_loop(0, 16, add_rows, 0)

    def stage(number, copy_a, copy_b):
        started = []
        for k in (2, 1, 3):
            started += [
                copy_a(k, ring_send.at[number, 0, k - 1], ring_recv.at[number, 0, k - 1]),
                copy_b(k, ring_send.at[number, 1, k - 1], ring_recv.at[number, 1, k - 1]),
            ]
        for copy in started:
            copy.start()
        pending.extend(started)
        return started

    def total(src, columns, place, size, arrived):
        value = src[rows(place * size, size), columns].astype(F32)
        for k in range(3):
            value = value + arrived[k].astype(F32)
        return value.astype(BF)

    x_of, y_of = plane.x_of, plane.y_of
    started = stage(
        0,
        lambda k, s, r: remote(
            own.at[rows(x_of(k) * quarter, quarter), LEFT], a1.at[k - 1], s, r,
            plane.at_x(x_of(k)),
        ),
        lambda k, s, r: remote(
            own.at[rows(y_of(k) * quarter, quarter), RIGHT], b1.at[k - 1], s, r,
            plane.at_y(y_of(k)),
        ),
    )
    yield
    for copy in started:
        copy.wait_recv()
    sa[...] = total(own, LEFT, plane.x, quarter, a1)
    sb[...] = total(own, RIGHT, plane.y, quarter, b1)
    started = stage(
        1,
        lambda k, s, r: remote(
            sa.at[rows(y_of(k) * part, part), :], a2.at[k - 1], s, r, plane.at_y(y_of(k))
        ),
        lambda k, s, r: remote(
            sb.at[rows(x_of(k) * part, part), :], b2.at[k - 1], s, r, plane.at_x(x_of(k))
        ),
    )
    yield
    for copy in started:
        copy.wait_recv()
    red_a[...] = total(sa, slice(0, CUT), plane.y, part, a2)
    red_b[...] = total(sb, slice(0, D - CUT), plane.x, part, b2)


def reduce_scratch(half, segments):
    dma = pltpu.SemaphoreType.DMA
    quarter, part = half // 4, half // 16
    return [
        pltpu.VMEM((half, D), BF),
        pltpu.VMEM((half, D), BF),
        pltpu.VMEM((3, quarter, CUT), BF),
        pltpu.VMEM((3, quarter, D - CUT), BF),
        pltpu.VMEM((3, part, CUT), BF),
        pltpu.VMEM((3, part, D - CUT), BF),
        pltpu.VMEM((quarter, CUT), BF),
        pltpu.VMEM((quarter, D - CUT), BF),
        dma((segments,)), dma((segments,)), dma((segments,)), dma((2, 2, 3)), dma((2, 2, 3)),
    ]


def reduced_shapes(half):
    return [((half // 16, CUT), BF), ((half // 16, D - CUT), BF)]


def spread_steps(plane, half, reduced, full, sems, pending):
    red_a, red_b = reduced
    ring_send, ring_recv, last_send, last_recv = sems
    quarter, part = half // 4, half // 16
    base = plane.core * half
    x, y, x_of, y_of = plane.x, plane.y, plane.x_of, plane.y_of

    def piece_a(px, py):
        return full.at[rows(base + px * quarter + py * part, part), LEFT]

    def piece_b(px, py):
        return full.at[rows(base + py * quarter + px * part, part), RIGHT]

    def band_a(px):
        return full.at[rows(base + px * quarter, quarter), LEFT]

    def band_b(py):
        return full.at[rows(base + py * quarter, quarter), RIGHT]

    def sem(number, side, k):
        return ring_send.at[number, side, k - 1], ring_recv.at[number, side, k - 1]

    def start(copy):
        copy.start()
        pending.append(copy)

    piece_a(x, y)[...] = red_a[...]
    piece_b(x, y)[...] = red_b[...]
    for k in (2, 1, 3):
        start(remote(red_a, piece_a(x, y), *sem(0, 0, k), plane.at_y(y_of(k))))
        start(remote(red_b, piece_b(x, y), *sem(0, 1, k), plane.at_x(x_of(k))))
    yield
    for k in range(1, 4):
        there = y_of(4 - k)
        remote(red_a, piece_a(x, there), *sem(0, 0, k), plane.at_y(there)).wait_recv()
        there = x_of(4 - k)
        remote(red_b, piece_b(there, y), *sem(0, 1, k), plane.at_x(there)).wait_recv()
    for k in (2, 1, 3):
        start(remote(band_a(x), band_a(x), *sem(1, 0, k), plane.at_x(x_of(k))))
        start(remote(band_b(y), band_b(y), *sem(1, 1, k), plane.at_y(y_of(k))))
    yield
    for k in range(1, 4):
        there = x_of(4 - k)
        remote(band_a(there), band_a(there), *sem(1, 0, k), plane.at_x(there)).wait_recv()
        there = y_of(4 - k)
        remote(band_b(there), band_b(there), *sem(1, 1, k), plane.at_y(there)).wait_recv()
    mine = full.at[rows(base, half), :]
    theirs = full.at[rows(half - base, half), :]
    start(remote(mine, mine, last_send, last_recv, plane.partner))
    yield
    remote(theirs, theirs, last_send, last_recv, plane.partner).wait_recv()


def spread_scratch():
    dma = pltpu.SemaphoreType.DMA
    return [dma((2, 2, 3)), dma((2, 2, 3)), dma, dma]


def take_turns(*generators):
    waiting = list(generators)
    while waiting:
        for generator in list(waiting):
            try:
                next(generator)
            except StopIteration:
                waiting.remove(generator)


def comm_call(body, collective_id, outs, args, specs, out_specs, scratch):
    return pl.pallas_call(
        body,
        out_shape=tuple(jax.ShapeDtypeStruct(shape, dtype) for shape, dtype in outs),
        in_specs=specs,
        out_specs=tuple(out_specs),
        scratch_shapes=scratch,
        compiler_params=pltpu.CompilerParams(
            collective_id=collective_id, has_side_effects=True, vmem_limit_bytes=VMEM_LIMIT
        ),
    )(*args)


def attn_sum_body(part, total, *scratch):
    greet(tp_peers())
    pending = []
    take_turns(tp_steps([part], [total], *scratch, pending))
    for copy in pending:
        copy.wait_send()


def mlp_sum_body(gn2_part, mlp_part, up, down, gn2, mlp, red_a, red_b, *scratch):
    plane = Plane()
    greet(plane.peers() + tp_peers())
    pending = []
    tp, weights = scratch[:3], scratch[3:]
    segments = (((up, 0, FIRST, 0),), ((down, 0, FIRST, 0),))
    take_turns(
        reduce_steps(
            plane, FIRST, segments, weights[:8], weights[8:], (red_a, red_b), pending
        ),
        tp_steps([gn2_part, mlp_part], [gn2, mlp], *tp, pending),
    )
    for copy in pending:
        copy.wait_send()


VEC_AT = 2 * REST + HSLOT * HD + COLS


def project_sum_body(
    gn1_part, up, down, w_out, w_qkv_t, vec, red1_a, red1_b,
    gn1, full1, red_a, red_b,
    vec_parts, vec_low, vec_got, vec_send, vec_recv, *scratch,
):
    plane = Plane()
    greet(plane.peers() + tp_peers())
    pending = []
    tp, spread, weights = scratch[:3], scratch[3:7], scratch[7:]
    own, got = weights[:2]
    me = lax.axis_index("tp")

    vec_parts[me] = vec[...].astype(BF)
    for k in range(1, N_TP):
        copy = remote(
            vec_parts.at[me], vec_parts.at[me], vec_send.at[k], vec_recv.at[k],
            {"tp": lax.rem(me + k, N_TP)},
        )
        copy.start()
        pending.append(copy)

    @pl.when(plane.core == 1)
    def _():
        own[SECOND - 128 :, :] = jnp.zeros((128, D), BF)
        got[SECOND - 128 :, :] = jnp.zeros((128, D), BF)

    def add_vectors():
        for k in range(1, N_TP):
            there = vec_parts.at[lax.rem(me + N_TP - k, N_TP)]
            remote(there, there, vec_send.at[k], vec_recv.at[k], plane.partner).wait_recv()
        over_tp = vec_parts[0].astype(F32)
        for t in range(1, N_TP):
            over_tp = over_tp + vec_parts[t].astype(F32)
        row = lax.broadcasted_iota(jnp.int32, (16, 1), 0)
        vec_low[...] = jnp.where(row < 2, over_tp, vec[...]).astype(BF)
        copy = remote(vec_low, vec_got, vec_send.at[0], vec_recv.at[0], plane.partner)
        copy.start()
        copy.wait_recv()
        pending.append(copy)

        @pl.when(plane.core == 1)
        def _():
            own[SECOND - 128 : SECOND - 112, :] = vec_low[...]
            got[SECOND - 128 : SECOND - 112, :] = vec_got[...]

    segments = (
        (
            (up, FIRST, REST, 0),
            (down, FIRST, REST, REST),
            (w_out, 0, HSLOT * HD, 2 * REST),
            (w_qkv_t, 0, 320, 448),
        ),
        ((w_qkv_t, 320, 640, 0),),
    )
    take_turns(
        spread_steps(plane, FIRST, (red1_a, red1_b), full1, spread, pending),
        reduce_steps(
            plane, SECOND, segments, weights[:8], weights[8:], (red_a, red_b), pending,
            late=add_vectors,
        ),
        tp_steps([gn1_part], [gn1], *tp, pending),
    )
    for copy in pending:
        copy.wait_send()


def finish_body(
    tok, gn1, grad_res, vecs, full1, red_a, red_b,
    grad_tok_t, up_out, down_out, w_out_out, w_qkv_out, *rest,
):
    vec_outs, (full2, up, down, w_out, w_qkv, out_sem, *scratch) = rest[:8], rest[8:]
    plane = Plane()
    greet(plane.peers())
    pending = []
    spread = spread_steps(plane, SECOND, (red_a, red_b), full2, scratch, pending)
    next(spread)
    normal, inverse = normalize(tok[...].astype(F32))
    grad_norm = gn1[...].astype(F32)
    grad = grad_res[...] + norm_backward(grad_norm, normal, inverse, vecs[0:1, :])
    grad_tok_t[...] = grad.T
    next(spread)
    up[:FIRST, :] = full1[:FIRST, :].astype(F32)
    down[:FIRST, :] = full1[FIRST:, :].astype(F32)
    next(spread)
    for _ in spread:
        pass
    up[FIRST:, :] = full2[:REST, :].astype(F32)
    down[FIRST:, :] = full2[REST : 2 * REST, :].astype(F32)
    copies = [pltpu.make_async_copy(up, up_out, out_sem.at[0])]
    copies.append(pltpu.make_async_copy(down, down_out, out_sem.at[1]))
    for copy in copies:
        copy.start()
    top = 2 * REST + HSLOT * HD
    w_out[...] = full2[2 * REST : top, :].astype(F32)
    copies.append(pltpu.make_async_copy(w_out, w_out_out, out_sem.at[2]))
    copies[-1].start()
    w_qkv[...] = full2[top:VEC_AT, :].astype(F32)
    copies.append(pltpu.make_async_copy(w_qkv, w_qkv_out, out_sem.at[3]))
    copies[-1].start()
    vectors = full2[VEC_AT : VEC_AT + 16, :].astype(F32)
    for i, ref in enumerate(vec_outs):
        ref[...] = vectors[i, : ref.shape[0]]
    for copy in copies:
        copy.wait()
    for copy in pending:
        copy.wait_send()


def on_device(
    tokens, cotangent, block_place, head_count, ln1_gain, ln1_bias, w_qkv, b_qv, w_out, b_out,
    ln2_gain, ln2_bias, w_up, b_up, w_down, b_down,
):
    w_qkv_t = w_qkv.T
    vecs_low = jnp.concatenate(
        [
            ln1_gain, ln1_bias, ln2_gain, ln2_bias, b_out, b_down, b_up, b_qv,
            jnp.zeros((D - HSLOT * 2 * HD,), BF),
        ]
    ).reshape(8, D)
    send1, normed1, tok, cot, vecs = local_call(
        project_body,
        [
            ((N_CTX, PIECE, 2 * HD), BF),
            ((TOK, D), BF),
            ((TOK, D), BF),
            ((TOK, D), BF),
            ((8, D), F32),
        ],
        [tokens[0].T, cotangent[0].T, vecs_low, w_qkv_t],
    )
    pieces1 = exchange(True, 1, send1)
    send2, keys, keys_t, queries, out_t, lse = local_call(
        attend_body,
        [
            ((N_CTX, HALF, 2 * HD), BF),
            ((N_CTX * TOK, 2 * HD), BF),
            ((2 * HD, N_CTX * TOK), BF),
            ((ROWS, 2 * HD), BF),
            ((HD, ROWS), F32),
            ((1, ROWS), F32),
        ],
        [block_place, head_count, pieces1],
        specs=[SM, SM, VM],
        scratch=[pltpu.SMEM((N_CTX,), jnp.int32)],
    )
    pieces2 = exchange(False, 2, send2)
    attended, attn_part = local_call(
        out_project_body, [((TOK, HSLOT * HD), BF), ((TOK, D), BF)], [pieces2, w_out]
    )
    (attn,) = comm_call(
        attn_sum_body, 3, [((TOK, D), BF)], [attn_part], [VM], [VM], tp_scratch(1)
    )
    mlp_part, gn2_part, gw_up, gw_down, sums_mlp = local_call(
        mlp_body,
        [((TOK, D), BF), ((TOK, D), BF), ((D, D), BF), ((D, D), BF), ((8, D), F32)],
        [tok, cot, attn, vecs, w_up, w_down],
    )
    gn2, mlp, red1_a, red1_b = comm_call(
        mlp_sum_body,
        4,
        [((TOK, D), BF), ((TOK, D), BF)] + reduced_shapes(FIRST),
        [gn2_part, mlp_part, gw_up, gw_down],
        [VM, VM, HB, HB],
        [VM] * 4,
        tp_scratch(2) + reduce_scratch(FIRST, 1),
    )
    output_t, grad_res, gw_out, send3, sums_mid = local_call(
        middle_body,
        [
            ((D, TOK), BF),
            ((TOK, D), F32),
            ((HSLOT * HD, D), BF),
            ((N_CTX, HALF, 2 * HD), BF),
            ((8, D), F32),
        ],
        [head_count, tok, cot, attn, mlp, gn2, vecs, w_out, attended],
        specs=[SM] + [VM] * 8,
    )
    pieces3 = exchange(True, 5, send3)
    (send4,) = local_call(
        attend_back_body,
        [((N_CTX, PIECE, 2 * HD), BF)],
        [block_place, pieces3, keys, keys_t, queries, out_t, lse],
        specs=[SM] + [VM] * 6,
        scratch=[
            pltpu.VMEM((ROWS, 2 * HD), BF),
            pltpu.VMEM((HD, ROWS), F32),
            pltpu.VMEM((1, ROWS), F32),
            pltpu.SMEM((N_CTX,), jnp.int32),
        ],
    )
    pieces4 = exchange(False, 6, send4)
    gw_qkv_t, gn1_part, vec = local_call(
        project_back_body,
        [((COLS, D), BF), ((TOK, D), BF), ((16, D), F32)],
        [pieces4, tok, normed1, w_qkv_t, sums_mid, sums_mlp],
    )
    dma = pltpu.SemaphoreType.DMA
    gn1, full1, red2_a, red2_b = comm_call(
        project_sum_body,
        7,
        [((TOK, D), BF), ((2 * FIRST, D), BF)] + reduced_shapes(SECOND),
        [gn1_part, gw_up, gw_down, gw_out, gw_qkv_t, vec, red1_a, red1_b],
        [VM, HB, HB, HB, HB, VM, VM, VM],
        [VM] * 4,
        [
            pltpu.VMEM((N_TP, 16, D), BF),
            pltpu.VMEM((16, D), BF),
            pltpu.VMEM((16, D), BF),
            dma((N_TP,)),
            dma((N_TP,)),
        ]
        + tp_scratch(1)
        + spread_scratch()
        + reduce_scratch(SECOND, 4),
    )
    grad_tok_t, g_up, g_down, g_out, g_qkv_t, *g = comm_call(
        finish_body,
        8,
        [
            ((D, TOK), F32),
            ((D, D), F32),
            ((D, D), F32),
            ((HSLOT * HD, D), F32),
            ((COLS, D), F32),
        ]
        + [((D,), F32)] * 7
        + [((HSLOT * 2 * HD,), F32)],
        [tok, gn1, grad_res, vecs, full1, red2_a, red2_b],
        [VM] * 7,
        [VM, HB, HB, HB, HB] + [VM] * 8,
        [
            pltpu.VMEM((2 * SECOND, D), BF),
            pltpu.VMEM((D, D), F32),
            pltpu.VMEM((D, D), F32),
            pltpu.VMEM((HSLOT * HD, D), F32),
            pltpu.VMEM((COLS, D), F32),
            dma((4,)),
        ]
        + spread_scratch(),
    )
    return (
        output_t.T[None],
        grad_tok_t.T[None],
        g[0],
        g[1],
        g_qkv_t.T,
        g[7],
        g_out,
        g[4],
        g[2],
        g[3],
        g_up,
        g[5],
        g_down,
        g[6],
    )


def solution(mesh):
    in_specs = (
        P("seq", "ctx", None), P("seq", "ctx", None), P(), P(), P(), P(), P(None, "tp"), P("tp"),
        P("tp", None), P(), P(), P(), P(None, "tp"), P("tp"), P("tp", None), P(),
    )
    out_specs = (
        P("seq", "ctx", None), P("seq", "ctx", None), P(), P(), P(None, "tp"), P("tp"),
        P("tp", None), P(), P(), P(), P(None, "tp"), P("tp"), P("tp", None), P(),
    )
    return jax.shard_map(
        on_device, mesh=mesh, in_specs=in_specs, out_specs=out_specs, check_vma=False
    )
```

```python
import functools

import jax
import jax.numpy as jnp
from jax import lax
from jax.experimental import pallas as pl
from jax.experimental.pallas import tpu as pltpu
from jax.sharding import PartitionSpec as P

HD = 64
HSLOT = 5
D = 1088
TOK = 256
N_CTX = 16
N_TP = 4
SPLIT = 3
STEP = 80
SHARE = 96
HALF = SHARE // 2
PIECE = TOK + HALF
ROWS = N_CTX * SHARE
GROUP = 128
WORK = HSLOT * SPLIT
COLS = HSLOT * 3 * HD
FIRST = 1024
REST = D - FIRST
SECOND = 768
CUT = 512
EPSILON = 1e-05
NEGATIVE = -1e30
BF = jnp.bfloat16
F32 = jnp.float32
MESH = pl.DeviceIdType.MESH
VMEM_LIMIT = 56 * 2**20

VM = pl.BlockSpec(memory_space=pltpu.VMEM)
SM = pl.BlockSpec(memory_space=pltpu.SMEM)
HB = pl.BlockSpec(memory_space=pl.ANY)


def dot(a, b):
    return jnp.dot(a, b, preferred_element_type=F32)


def dot_nt(a, b):
    return lax.dot_general(a, b, (((1,), (1,)), ((), ())), preferred_element_type=F32)


def dot_tn(a, b):
    return lax.dot_general(a, b, (((0,), (0,)), ((), ())), preferred_element_type=F32)


def pack(rows):
    return jnp.concatenate([rows[:HALF], rows[HALF:]], axis=1)


def unpack(packed):
    return jnp.concatenate([packed[:, :HD], packed[:, HD:]], axis=0)


def normalize(values):
    centered = values - jnp.mean(values, axis=-1, keepdims=True)
    inverse = lax.rsqrt(jnp.mean(centered * centered, axis=-1, keepdims=True) + EPSILON)
    return centered * inverse, inverse


def norm_backward(grad_out, normal, inverse, gain):
    grad_normal = grad_out * gain
    grad_mean = jnp.mean(grad_normal, axis=-1, keepdims=True)
    grad_along = jnp.mean(grad_normal * normal, axis=-1, keepdims=True)
    return inverse * (grad_normal - grad_mean - normal * grad_along)


def row_sum(values):
    return jnp.sum(values, axis=0, keepdims=True)


def local_call(body, outs, args, specs=None, scratch=(), out_specs=None):
    moved = sum(a.size * a.dtype.itemsize for a in args)
    return pl.pallas_call(
        body,
        out_shape=tuple(jax.ShapeDtypeStruct(shape, dtype) for shape, dtype in outs),
        in_specs=specs or [VM] * len(args),
        out_specs=tuple(out_specs or [VM] * len(outs)),
        scratch_shapes=list(scratch),
        compiler_params=pltpu.CompilerParams(vmem_limit_bytes=VMEM_LIMIT),
        cost_estimate=pl.CostEstimate(flops=0, bytes_accessed=moved, transcendentals=0),
    )(*args)


def project_body(tok_t, cot_t, w_t, *rest):
    rows_in, (send, normed_out, tok, cot, vecs) = rest[:8], rest[8:]
    tok[...] = tok_t[...].T
    cot[...] = cot_t[...].T
    for i, ref in enumerate(rows_in):
        vecs[i : i + 1, : ref.shape[0]] = ref[...].astype(F32).reshape(1, ref.shape[0])
    normal, _ = normalize(tok[...].astype(F32))
    normed = (normal * vecs[0:1, :] + vecs[1:2, :]).astype(BF)
    normed_out[...] = normed
    projected = dot_nt(normed, w_t[...])
    upper = lax.broadcasted_iota(jnp.int32, (1, 2 * HD), 1) >= HD
    for s in range(HSLOT):
        base = 3 * HD * s
        bias = vecs[7:8, 2 * HD * s : 2 * HD * (s + 1)]
        pair = projected[:, base + HD : base + 3 * HD] + jnp.where(upper, bias, 0.0)
        pair = pair.astype(BF)
        queries = (projected[:, base : base + HD] + bias[:, :HD]).astype(BF)
        queries = queries * jnp.asarray(HD**-0.5, BF)
        for j in range(SPLIT):
            send[SPLIT * s + j, :TOK, :] = pair
            send[SPLIT * s + j, TOK:, :] = pack(queries[STEP * j : STEP * j + SHARE])
    send[WORK] = jnp.zeros((PIECE, 2 * HD), BF)


def join_shares(shares):
    return jnp.concatenate([shares[0], shares[1][16:], shares[2][16:]], axis=0)


def out_project_body(pieces, w, attended, part):
    heads = []
    for s in range(HSLOT):
        heads.append(join_shares([unpack(pieces[SPLIT * s + j]) for j in range(SPLIT)]))
    rows = jnp.concatenate(heads, axis=1)
    attended[...] = rows
    part[...] = dot(rows, w[...]).astype(BF)


def mlp_body(tok, cot, attn, vecs, w_up, w_down, mlp, gn2, gw_up, gw_down, sums):
    residual = tok[...].astype(F32) + (attn[...].astype(F32) + vecs[4:5, :])
    normal, _ = normalize(residual)
    normed = (normal * vecs[2:3, :] + vecs[3:4, :]).astype(BF)
    hidden = dot(normed, w_up[...]) + vecs[6:7, :]
    cdf = 0.5 * (1.0 + lax.erf(hidden * (0.5**0.5)))
    activated = (hidden * cdf).astype(BF)
    mlp[...] = dot(activated, w_down[...]).astype(BF)
    cot_low = cot[...]
    grad_act = dot_nt(cot_low, w_down[...])
    slope = cdf + hidden * jnp.exp(-0.5 * hidden * hidden) * 0.3989422804014327
    grad_hidden = (grad_act * slope).astype(BF)
    gn2[...] = dot_nt(grad_hidden, w_up[...]).astype(BF)
    gw_down[...] = dot_tn(activated, cot_low).astype(BF)
    gw_up[...] = dot_tn(normed, grad_hidden).astype(BF)
    sums[...] = jnp.zeros_like(sums)
    sums[0:1, :] = row_sum(grad_hidden.astype(F32))
    sums[1:2, :] = row_sum(cot_low.astype(F32))


def middle_body(
    head_count, tok, cot, attn, gn2, vecs, w_out, attended, grad_res, gw_out, send, sums
):
    residual = tok[...].astype(F32) + (attn[...].astype(F32) + vecs[4:5, :])
    normal, inverse = normalize(residual)
    grad_norm = gn2[...].astype(F32)
    grad = cot[...].astype(F32) + norm_backward(grad_norm, normal, inverse, vecs[2:3, :])
    grad_res[...] = grad
    grad_low = grad.astype(BF)
    gw_out[...] = dot_tn(attended[...], grad_low).astype(BF)
    live_lanes = head_count[lax.axis_index("tp")] * HD
    lane = lax.broadcasted_iota(jnp.int32, (1, HSLOT * HD), 1)
    live = (lane < live_lanes).astype(F32)
    grad_att = (dot_nt(grad_low, w_out[...]) * live).astype(BF)
    for s in range(HSLOT):
        head = grad_att[:, HD * s : HD * (s + 1)]
        for j in range(SPLIT):
            share = head[STEP * j : STEP * j + SHARE]
            if j:
                share = jnp.concatenate([jnp.zeros((16, HD), BF), share[16:]], axis=0)
            send[SPLIT * s + j] = pack(share)
    send[WORK] = jnp.zeros((HALF, 2 * HD), BF)
    sums[...] = jnp.zeros_like(sums)
    sums[0:1, :] = row_sum(grad_norm * normal)
    sums[1:2, :] = row_sum(grad_norm)
    sums[2:3, :] = row_sum(grad_low.astype(F32))


def project_back_body(pieces, tok, normed, w_t, sums_mid, sums_mlp, gw_qkv_t, gn1, vec):
    columns, biases = [], []
    for s in range(HSLOT):
        mine = [pieces[SPLIT * s + j] for j in range(SPLIT)]
        pair = mine[0][:TOK].astype(F32)
        for piece in mine[1:]:
            pair = pair + piece[:TOK].astype(F32)
        pair = pair.astype(BF)
        queries = join_shares([unpack(piece[TOK:]) for piece in mine])
        columns += [queries, pair]
        biases += [row_sum(queries.astype(F32)), row_sum(pair.astype(F32))[:, HD:]]
    grads = jnp.concatenate(columns, axis=1)
    gw_qkv_t[...] = dot_tn(grads, normed[...]).astype(BF)
    part = dot(grads, w_t[...])
    gn1[...] = part.astype(BF)
    normal, _ = normalize(tok[...].astype(F32))
    vec[0:1, :] = row_sum(part * normal)
    vec[1:2, :] = row_sum(part)
    vec[2:5, :] = sums_mid[0:3, :]
    vec[5:7, :] = sums_mlp[0:2, :]
    vec[7:8, : HSLOT * 2 * HD] = jnp.concatenate(biases, axis=1)
    vec[7:8, HSLOT * 2 * HD :] = jnp.zeros((1, D - HSLOT * 2 * HD), F32)
    vec[8:, :] = jnp.zeros((8, D), F32)


def group_keys(first):
    low = first // SHARE
    high = (first + GROUP - 1) // SHARE
    return low * TOK, (high + 1) * TOK


def allowed_keys(first, row_offset):
    low, high = group_keys(first)
    row = first + lax.broadcasted_iota(jnp.int32, (1, GROUP), 1)
    place = jnp.full((1, GROUP), low // TOK, jnp.int32)
    for p in range(low // TOK + 1, high // TOK):
        place = place + (row >= p * SHARE).astype(jnp.int32)
    position = place * (TOK - SHARE) + row + row_offset
    key = low + lax.broadcasted_iota(jnp.int32, (high - low, GROUP), 0)
    return key <= position


def attend_body(
    block_place, head_count, pieces, send, keys, keys_t, queries, out_t, lse, order
):
    for i in range(N_CTX):
        order[block_place[i]] = i
    ctx = lax.axis_index("ctx")
    row_offset = lax.rem(ctx, SPLIT) * STEP
    live = (ctx // SPLIT < head_count[lax.axis_index("tp")]).astype(F32)
    for p in range(N_CTX):
        owner = order[p]
        pair = pieces[owner, :TOK, :]
        keys[p * TOK : (p + 1) * TOK, :] = pair
        keys_t[:, p * TOK : (p + 1) * TOK] = pair.T
        rows = unpack(pieces[owner, TOK:, :])
        queries[p * SHARE : (p + 1) * SHARE, :] = jnp.concatenate(
            [rows, jnp.zeros((SHARE, HD), BF)], axis=1
        )
    for first in range(0, ROWS, GROUP):
        low, high = group_keys(first)
        block = queries[first : first + GROUP, :]
        edge = jnp.where(
            allowed_keys(first, row_offset), dot_nt(keys[low:high, :], block), NEGATIVE
        )
        top = jnp.max(edge, axis=0, keepdims=True)
        if low:
            body = dot_nt(keys[:low, :], block)
            top = jnp.maximum(top, jnp.max(body, axis=0, keepdims=True))
        weights = jnp.exp(edge - top)
        total = jnp.sum(weights, axis=0, keepdims=True)
        mixed = dot(keys_t[HD:, low:high], weights.astype(BF))
        if low:
            weights = jnp.exp(body - top)
            total = total + jnp.sum(weights, axis=0, keepdims=True)
            mixed = mixed + dot(keys_t[HD:, :low], weights.astype(BF))
        out_t[:, first : first + GROUP] = mixed / total * live
        lse[:, first : first + GROUP] = top + jnp.log(total)
    for p in range(N_CTX):
        rows = out_t[:, p * SHARE : (p + 1) * SHARE].T.astype(BF)
        send[order[p]] = pack(rows)


def greet(peers):
    barrier = pltpu.get_barrier_semaphore()
    for peer in peers:
        pl.semaphore_signal(barrier, inc=1, device_id=peer, device_id_type=MESH)
    pl.semaphore_wait(barrier, len(peers))


def remote(src, dst, send, recv, device):
    return pltpu.make_async_remote_copy(
        src_ref=src,
        dst_ref=dst,
        send_sem=send,
        recv_sem=recv,
        device_id=device,
        device_id_type=MESH,
    )


def rows(start, size):
    return pl.ds(pl.multiple_of(start, 16), size)


def tp_steps(parts, totals, held, send_sem, recv_sem, pending):
    me = lax.axis_index("tp")
    share = TOK // N_TP
    count = len(parts)
    started = {}
    for i in range(count):
        for k in (2, 1, 3):
            peer = lax.rem(me + k, N_TP)
            started[i, k] = remote(
                parts[i].at[rows(peer * share, share), :], held.at[i, k - 1],
                send_sem.at[0, i, k - 1], recv_sem.at[0, i, k - 1], {"tp": peer},
            )
            started[i, k].start()
    pending += started.values()
    yield
    own = rows(me * share, share)
    for i in range(count):
        total = parts[i][own, :].astype(F32)
        for k in range(1, N_TP):
            started[i, k].wait_recv()
            total = total + held[i, k - 1].astype(F32)
        totals[i][own, :] = total.astype(BF)
        for k in (2, 1, 3):
            copy = remote(
                totals[i].at[own, :], totals[i].at[own, :],
                send_sem.at[1, i, k - 1], recv_sem.at[1, i, k - 1],
                {"tp": lax.rem(me + k, N_TP)},
            )
            copy.start()
            pending.append(copy)
    yield
    for i in range(count):
        for k in range(1, N_TP):
            peer = lax.rem(me + N_TP - k, N_TP)
            there = totals[i].at[rows(peer * share, share), :]
            remote(
                there, there, send_sem.at[1, i, k - 1], recv_sem.at[1, i, k - 1], {"tp": peer}
            ).wait_recv()


def tp_scratch(count):
    return [
        pltpu.VMEM((count, N_TP - 1, TOK // N_TP, D), BF),
        pltpu.SemaphoreType.DMA((2, count, N_TP - 1)),
        pltpu.SemaphoreType.DMA((2, count, N_TP - 1)),
    ]


def tp_peers():
    me = lax.axis_index("tp")
    return [{"tp": lax.rem(me + k, N_TP)} for k in range(1, N_TP)]


class Plane:
    def __init__(self):
        ctx = lax.axis_index("ctx")
        self.core = lax.axis_index("seq")
        self.partner = {"seq": 1 - self.core}
        self.x, self.y = ctx // 4, lax.rem(ctx, 4)

    def x_of(self, k):
        return lax.rem(self.x + k, 4)

    def y_of(self, k):
        return lax.rem(self.y + k, 4)

    def at_x(self, place):
        return {"ctx": place * 4 + self.y}

    def at_y(self, place):
        return {"ctx": self.x * 4 + place}

    def peers(self):
        return (
            [self.partner]
            + [self.at_x(self.x_of(k)) for k in range(1, 4)]
            + [self.at_y(self.y_of(k)) for k in range(1, 4)]
        )


LEFT, RIGHT = slice(0, CUT), slice(CUT, D)


def ring_total(src, columns, place, size, arrived):
    value = src[rows(place * size, size), columns].astype(F32)
    for k in range(3):
        value = value + arrived[k].astype(F32)
    return value.astype(BF)


def start_all(copies, pending):
    for copy in copies:
        copy.start()
    pending.extend(copies)
    return copies


def reduce_first(plane, half, segments, held, result, pending, late=None):
    own, got, a1, b1, first_send, first_recv, first_local, ring_send, ring_recv = held
    quarter, part = half // 4, half // 16

    def keep(i, segment):
        ref, start, size, to = segment
        return pltpu.make_async_copy(
            ref.at[pl.ds(start, size), :], own.at[pl.ds(to, size), :], first_local.at[i]
        )

    def give(i, segment):
        ref, start, size, to = segment
        return remote(
            ref.at[pl.ds(start, size), :], got.at[pl.ds(to, size), :],
            first_send.at[i], first_recv.at[i], plane.partner,
        )

    for mine in range(2):

        @pl.when(plane.core == mine)
        def _():
            for i, segment in enumerate(segments[1 - mine]):
                give(i, segment).start()
            for i, segment in enumerate(segments[mine]):
                keep(i, segment).start()

    yield
    if late is not None:
        late()
    for mine in range(2):

        @pl.when(plane.core == mine)
        def _():
            for i, segment in enumerate(segments[mine]):
                keep(i, segment).wait()
                give(i, segment).wait_recv()
            for i, segment in enumerate(segments[1 - mine]):
                give(i, segment).wait_send()

    def add_rows(i, carry):
        span = rows(i * part, part)
        own[span, :] = (own[span, :].astype(F32) + got[span, :].astype(F32)).astype(BF)
        return carry

    lax.fori_loop(0, 16, add_rows, 0)
    started = []
    for k in (2, 1, 3):
        px, py = plane.x_of(k), plane.y_of(k)
        started.append(
            remote(
                own.at[rows(px * quarter, quarter), LEFT], a1.at[k - 1],
                ring_send.at[0, k - 1], ring_recv.at[0, k - 1], plane.at_x(px),
            )
        )
        started.append(
            remote(
                own.at[rows(py * quarter, quarter), RIGHT], b1.at[k - 1],
                ring_send.at[1, k - 1], ring_recv.at[1, k - 1], plane.at_y(py),
            )
        )
    start_all(started, pending)
    yield
    for copy in started:
        copy.wait_recv()
    result[0][...] = ring_total(own, LEFT, plane.x, quarter, a1)
    result[1][...] = ring_total(own, RIGHT, plane.y, quarter, b1)


def reduce_first_scratch(half, segments):
    dma = pltpu.SemaphoreType.DMA
    quarter = half // 4
    return [
        pltpu.VMEM((half, D), BF),
        pltpu.VMEM((half, D), BF),
        pltpu.VMEM((3, quarter, CUT), BF),
        pltpu.VMEM((3, quarter, D - CUT), BF),
        dma((segments,)), dma((segments,)), dma((segments,)), dma((2, 3)), dma((2, 3)),
    ]


def reduce_second(plane, half, partial, held, result, pending):
    sa, sb = partial
    a2, b2, ring_send, ring_recv = held
    part = half // 16
    started = []
    for k in (2, 1, 3):
        px, py = plane.x_of(k), plane.y_of(k)
        started.append(
            remote(
                sa.at[rows(py * part, part), :], a2.at[k - 1],
                ring_send.at[0, k - 1], ring_recv.at[0, k - 1], plane.at_y(py),
            )
        )
        started.append(
            remote(
                sb.at[rows(px * part, part), :], b2.at[k - 1],
                ring_send.at[1, k - 1], ring_recv.at[1, k - 1], plane.at_x(px),
            )
        )
    start_all(started, pending)
    yield
    for copy in started:
        copy.wait_recv()
    result[0][...] = ring_total(sa, slice(0, CUT), plane.y, part, a2)
    result[1][...] = ring_total(sb, slice(0, D - CUT), plane.x, part, b2)


def reduce_second_scratch(half):
    dma = pltpu.SemaphoreType.DMA
    part = half // 16
    return [
        pltpu.VMEM((3, part, CUT), BF), pltpu.VMEM((3, part, D - CUT), BF),
        dma((2, 3)), dma((2, 3)),
    ]


def reduced_shapes(count):
    return [((count, CUT), BF), ((count, D - CUT), BF)]


def spread_steps(plane, half, reduced, mine, theirs, sems, pending):
    red_a, red_b = reduced
    ring_send, ring_recv, pair_send, pair_recv = sems
    quarter, part = half // 4, half // 16
    x, y, x_of, y_of = plane.x, plane.y, plane.x_of, plane.y_of

    def piece_a(px, py):
        return mine.at[rows(px * quarter + py * part, part), LEFT]

    def piece_b(px, py):
        return mine.at[rows(py * quarter + px * part, part), RIGHT]

    def band_a(px):
        return mine.at[rows(px * quarter, quarter), LEFT]

    def band_b(py):
        return mine.at[rows(py * quarter, quarter), RIGHT]

    def sem(number, side, k):
        return ring_send.at[number, side, k - 1], ring_recv.at[number, side, k - 1]

    def pair(k):
        px, py = x_of(4 - k), y_of(4 - k)
        return [
            remote(
                band_a(px), theirs.at[rows(px * quarter, quarter), LEFT],
                pair_send.at[0, k], pair_recv.at[0, k], plane.partner,
            ),
            remote(
                band_b(py), theirs.at[rows(py * quarter, quarter), RIGHT],
                pair_send.at[1, k], pair_recv.at[1, k], plane.partner,
            ),
        ]

    piece_a(x, y)[...] = red_a[...]
    piece_b(x, y)[...] = red_b[...]
    started = []
    for k in (2, 1, 3):
        started.append(remote(red_a, piece_a(x, y), *sem(0, 0, k), plane.at_y(y_of(k))))
        started.append(remote(red_b, piece_b(x, y), *sem(0, 1, k), plane.at_x(x_of(k))))
    start_all(started, pending)
    yield
    for k in range(1, 4):
        there = y_of(4 - k)
        remote(red_a, piece_a(x, there), *sem(0, 0, k), plane.at_y(there)).wait_recv()
        there = x_of(4 - k)
        remote(red_b, piece_b(there, y), *sem(0, 1, k), plane.at_x(there)).wait_recv()
    started = []
    for k in (2, 1, 3):
        started.append(remote(band_a(x), band_a(x), *sem(1, 0, k), plane.at_x(x_of(k))))
        started.append(remote(band_b(y), band_b(y), *sem(1, 1, k), plane.at_y(y_of(k))))
    start_all(started + pair(0), pending)
    yield
    for k in (1, 3, 2):
        there = x_of(4 - k)
        remote(band_a(there), band_a(there), *sem(1, 0, k), plane.at_x(there)).wait_recv()
        there = y_of(4 - k)
        remote(band_b(there), band_b(there), *sem(1, 1, k), plane.at_y(there)).wait_recv()
        start_all(pair(k), pending)
    yield
    for k in range(4):
        for copy in pair(k):
            copy.wait_recv()


def spread_scratch():
    dma = pltpu.SemaphoreType.DMA
    return [dma((2, 2, 3)), dma((2, 2, 3)), dma((2, 4)), dma((2, 4))]


def take_turns(*generators):
    waiting = list(generators)
    while waiting:
        for generator in list(waiting):
            try:
                next(generator)
            except StopIteration:
                waiting.remove(generator)


def comm_call(body, collective_id, outs, args, specs, out_specs, scratch):
    return pl.pallas_call(
        body,
        out_shape=tuple(jax.ShapeDtypeStruct(shape, dtype) for shape, dtype in outs),
        in_specs=specs,
        out_specs=tuple(out_specs),
        scratch_shapes=scratch,
        compiler_params=pltpu.CompilerParams(
            collective_id=collective_id, has_side_effects=True, vmem_limit_bytes=VMEM_LIMIT
        ),
    )(*args)


def exchange_steps(to_workers, src, dst, send_sem, recv_sem, local_sem):
    me = lax.axis_index("ctx")

    def copy(k, peer, slot):
        return remote(src.at[peer], dst.at[slot], send_sem.at[k], recv_sem.at[k], {"ctx": peer})

    works = me < WORK
    for k in range(1, N_CTX):
        peer = lax.rem(me + k, N_CTX)
        pl.when(peer < WORK if to_workers else works)(copy(k, peer, me).start)
    own = pltpu.make_async_copy(src.at[me], dst.at[me], local_sem)
    pl.when(works)(own.start)
    yield
    pl.when(works)(own.wait)
    for k in range(1, N_CTX):
        peer = lax.rem(me + N_CTX - k, N_CTX)
        pl.when(works if to_workers else peer < WORK)(copy(k, peer, peer).wait_recv)
    for k in range(1, N_CTX):
        peer = lax.rem(me + k, N_CTX)
        pl.when(peer < WORK if to_workers else works)(copy(k, peer, me).wait_send)


def ctx_peers():
    me = lax.axis_index("ctx")
    return [{"ctx": lax.rem(me + k, N_CTX)} for k in range(1, N_CTX)]


def exchange_scratch():
    dma = pltpu.SemaphoreType.DMA
    return [dma((N_CTX,)), dma((N_CTX,)), dma]


def exchange_body(to_workers, src, dst, *sems):
    greet(ctx_peers())
    take_turns(exchange_steps(to_workers, src, dst, *sems))


def exchange(to_workers, collective_id, src):
    (moved,) = comm_call(
        functools.partial(exchange_body, to_workers),
        collective_id, [(src.shape, BF)], [src], [HB], [HB], exchange_scratch(),
    )
    return moved


def finish_sends(pending):
    for copy in pending:
        copy.wait_send()


def attn_sum_body(part, total, *scratch):
    greet(tp_peers())
    pending = []
    take_turns(tp_steps([part], [total], *scratch, pending))
    finish_sends(pending)


def gn2_sum_body(gn2_part, up, down, gn2, sum_a, sum_b, *scratch):
    plane = Plane()
    greet(plane.peers() + tp_peers())
    pending = []
    tp, weights = scratch[:3], scratch[3:]
    segments = (((up, 0, FIRST, 0),), ((down, 0, FIRST, 0),))
    take_turns(
        reduce_first(plane, FIRST, segments, weights, (sum_a, sum_b), pending),
        tp_steps([gn2_part], [gn2], *tp, pending),
    )
    finish_sends(pending)


def grad_exchange_body(src, sum_a, sum_b, dst, red_a, red_b, *scratch):
    greet(ctx_peers())
    pending = []
    take_turns(
        exchange_steps(True, src, dst, *scratch[:3]),
        reduce_second(Plane(), FIRST, (sum_a, sum_b), scratch[3:], (red_a, red_b), pending),
    )
    finish_sends(pending)


def attend_back_body(
    block_place, order, pieces, keys, keys_t, queries, out_t, lse, red_a, red_b, mlp_part,
    send, mine, theirs, mlp,
    grads, grad_q, dots, acc, packed, *scratch,
):
    plane = Plane()
    greet(plane.peers() + tp_peers())
    pending = []
    spread = spread_steps(plane, FIRST, (red_a, red_b), mine, theirs, scratch[3:], pending)
    total = tp_steps([mlp_part], [mlp], *scratch[:3], pending)
    next(spread)
    next(total)
    row_offset = lax.rem(lax.axis_index("ctx"), SPLIT) * STEP
    for p in range(N_CTX):
        share = unpack(pieces[order[p]])
        grads[p * SHARE : (p + 1) * SHARE, :] = jnp.concatenate(
            [jnp.zeros((SHARE, HD), BF), share], axis=1
        )
    for first in range(0, ROWS, GROUP):
        turned = grads[first : first + GROUP, :].astype(F32).T
        dots[:, first : first + GROUP] = jnp.sum(
            turned[HD:, :] * out_t[:, first : first + GROUP], axis=0, keepdims=True
        )
    acc[...] = jnp.zeros_like(acc)
    for first in range(0, ROWS, GROUP):
        low, high = group_keys(first)
        span = slice(first, first + GROUP)
        both = jnp.concatenate([queries[span, :], grads[span, :]], axis=0)
        grad_block = jnp.zeros((HD, GROUP), F32)
        for start, stop in ((0, low), (low, high)):
            if start == stop:
                continue
            scores = dot_nt(keys[start:stop, :], both)
            weights = jnp.exp(scores[:, :GROUP] - lse[:, span])
            if start == low:
                weights = jnp.where(allowed_keys(first, row_offset), weights, 0.0)
            grad_scores = (weights * (scores[:, GROUP:] - dots[:, span])).astype(BF)
            pair = jnp.concatenate([grad_scores, weights.astype(BF)], axis=1)
            blocks = slice(start // TOK, stop // TOK)
            acc[blocks] += dot(pair, both).reshape(-1, TOK, 2 * HD)
            grad_block = grad_block + dot(keys_t[:HD, start:stop], grad_scores)
        grad_q[:, span] = grad_block * (HD**-0.5)
        if first == 5 * GROUP:
            next(spread)
        if first == 8 * GROUP:
            next(total)
    for p in range(N_CTX):
        packed[p] = pack(grad_q[:, p * SHARE : (p + 1) * SHARE].T.astype(BF))
    next(spread)
    for b in range(N_CTX):
        place = block_place[b]
        send[b, :TOK, :] = acc[place].astype(BF)
        send[b, TOK:, :] = packed[place]
    take_turns(spread, total)
    finish_sends(pending)


VEC_AT = 2 * REST + HSLOT * HD + COLS


def gn1_sum_body(
    gn1_part, up, down, w_out, w_qkv_t, vec, gn1, red_a, red_b,
    vec_parts, vec_low, vec_got, vec_send, vec_recv, sum_a, sum_b, *scratch,
):
    plane = Plane()
    greet(plane.peers() + tp_peers())
    pending = []
    tp, weights, second = scratch[:3], scratch[3:12], scratch[12:]
    own, got = weights[:2]
    me = lax.axis_index("tp")

    vec_parts[me] = vec[...].astype(BF)
    for k in range(1, N_TP):
        copy = remote(
            vec_parts.at[me], vec_parts.at[me], vec_send.at[k], vec_recv.at[k],
            {"tp": lax.rem(me + k, N_TP)},
        )
        start_all([copy], pending)

    @pl.when(plane.core == 1)
    def _():
        own[SECOND - 128 :, :] = jnp.zeros((128, D), BF)
        got[SECOND - 128 :, :] = jnp.zeros((128, D), BF)

    def add_vectors():
        for k in range(1, N_TP):
            there = vec_parts.at[lax.rem(me + N_TP - k, N_TP)]
            remote(there, there, vec_send.at[k], vec_recv.at[k], plane.partner).wait_recv()
        over_tp = vec_parts[0].astype(F32)
        for t in range(1, N_TP):
            over_tp = over_tp + vec_parts[t].astype(F32)
        row = lax.broadcasted_iota(jnp.int32, (16, 1), 0)
        vec_low[...] = jnp.where(row < 2, over_tp, vec[...]).astype(BF)
        copy = remote(vec_low, vec_got, vec_send.at[0], vec_recv.at[0], plane.partner)
        start_all([copy], pending)
        copy.wait_recv()

        @pl.when(plane.core == 1)
        def _():
            own[SECOND - 128 : SECOND - 112, :] = vec_low[...]
            got[SECOND - 128 : SECOND - 112, :] = vec_got[...]

    segments = (
        (
            (up, FIRST, REST, 0),
            (down, FIRST, REST, REST),
            (w_out, 0, HSLOT * HD, 2 * REST),
            (w_qkv_t, 0, 320, 448),
        ),
        ((w_qkv_t, 320, 640, 0),),
    )

    def reduce():
        yield from reduce_first(
            plane, SECOND, segments, weights, (sum_a, sum_b), pending, late=add_vectors
        )
        yield from reduce_second(plane, SECOND, (sum_a, sum_b), second, (red_a, red_b), pending)

    take_turns(reduce(), tp_steps([gn1_part], [gn1], *tp, pending))
    finish_sends(pending)


def spread_body(red_a, red_b, mine, theirs, *scratch):
    plane = Plane()
    greet(plane.peers())
    pending = []
    take_turns(spread_steps(plane, SECOND, (red_a, red_b), mine, theirs, scratch, pending))
    finish_sends(pending)


def finish_body(
    tok, attn, mlp, gn1, grad_res, vecs, mine1, theirs1, mine2, theirs2,
    output_t, grad_tok_t, up_out, down_out, w_out_out, w_qkv_out, *rest,
):
    vec_outs, (up, down, w_out, w_qkv, out_sem) = rest[:8], rest[8:]
    top = 2 * REST + HSLOT * HD
    core = lax.axis_index("seq")
    copies = []

    def by_core(action):
        pl.when(core == 0)(lambda: action(mine1, theirs1, mine2, theirs2))
        pl.when(core == 1)(lambda: action(theirs1, mine1, theirs2, mine2))

    def write(src, dst):
        copies.append(pltpu.make_async_copy(src, dst, out_sem.at[len(copies)]))
        copies[-1].start()

    def cast_up(low1, high1, low2, high2):
        up[:FIRST, :] = low1[...].astype(F32)
        up[FIRST:, :] = low2[:REST, :].astype(F32)

    def cast_down(low1, high1, low2, high2):
        down[:FIRST, :] = high1[...].astype(F32)
        down[FIRST:, :] = low2[REST : 2 * REST, :].astype(F32)

    def cast_qkv(low1, high1, low2, high2):
        w_qkv[: SECOND - top, :] = low2[top:, :].astype(F32)
        w_qkv[SECOND - top :, :] = high2[: VEC_AT - SECOND, :].astype(F32)

    def cast_rest(low1, high1, low2, high2):
        w_out[...] = low2[2 * REST : top, :].astype(F32)
        vectors = high2[VEC_AT - SECOND : VEC_AT - SECOND + 16, :].astype(F32)
        for i, ref in enumerate(vec_outs):
            ref[...] = vectors[i, : ref.shape[0]]

    by_core(cast_up)
    write(up, up_out)
    by_core(cast_down)
    write(down, down_out)
    by_core(cast_qkv)
    write(w_qkv, w_qkv_out)
    by_core(cast_rest)
    write(w_out, w_out_out)
    inputs = tok[...].astype(F32)
    residual = inputs + (attn[...].astype(F32) + vecs[4:5, :])
    output_t[...] = (residual + (mlp[...].astype(F32) + vecs[5:6, :])).astype(BF).T
    normal, inverse = normalize(inputs)
    grad_norm = gn1[...].astype(F32)
    grad = grad_res[...] + norm_backward(grad_norm, normal, inverse, vecs[0:1, :])
    grad_tok_t[...] = grad.T
    for copy in copies:
        copy.wait()


def on_device(
    tokens, cotangent, block_place, head_count, ln1_gain, ln1_bias, w_qkv, b_qv, w_out, b_out,
    ln2_gain, ln2_bias, w_up, b_up, w_down, b_down,
):
    w_qkv_t = w_qkv.T
    send1, normed1, tok, cot, vecs = local_call(
        project_body,
        [
            ((N_CTX, PIECE, 2 * HD), BF),
            ((TOK, D), BF),
            ((TOK, D), BF),
            ((TOK, D), BF),
            ((8, D), F32),
        ],
        [tokens[0].T, cotangent[0].T, w_qkv_t]
        + [ln1_gain, ln1_bias, ln2_gain, ln2_bias, b_out, b_down, b_up, b_qv],
    )
    pieces1 = exchange(True, 1, send1)
    send2, keys, keys_t, queries, out_t, lse, order = local_call(
        attend_body,
        [
            ((N_CTX, HALF, 2 * HD), BF),
            ((N_CTX * TOK, 2 * HD), BF),
            ((2 * HD, N_CTX * TOK), BF),
            ((ROWS, 2 * HD), BF),
            ((HD, ROWS), F32),
            ((1, ROWS), F32),
            ((N_CTX,), jnp.int32),
        ],
        [block_place, head_count, pieces1],
        specs=[SM, SM, VM],
        out_specs=[VM] * 6 + [SM],
    )
    pieces2 = exchange(False, 2, send2)
    attended, attn_part = local_call(
        out_project_body, [((TOK, HSLOT * HD), BF), ((TOK, D), BF)], [pieces2, w_out]
    )
    (attn,) = comm_call(
        attn_sum_body, 3, [((TOK, D), BF)], [attn_part], [VM], [VM], tp_scratch(1)
    )
    mlp_part, gn2_part, gw_up, gw_down, sums_mlp = local_call(
        mlp_body,
        [((TOK, D), BF), ((TOK, D), BF), ((D, D), BF), ((D, D), BF), ((8, D), F32)],
        [tok, cot, attn, vecs, w_up, w_down],
    )
    gn2, sum1_a, sum1_b = comm_call(
        gn2_sum_body,
        4,
        [((TOK, D), BF)] + reduced_shapes(FIRST // 4),
        [gn2_part, gw_up, gw_down],
        [VM, HB, HB],
        [VM] * 3,
        tp_scratch(1) + reduce_first_scratch(FIRST, 1),
    )
    grad_res, gw_out, send3, sums_mid = local_call(
        middle_body,
        [
            ((TOK, D), F32),
            ((HSLOT * HD, D), BF),
            ((N_CTX, HALF, 2 * HD), BF),
            ((8, D), F32),
        ],
        [head_count, tok, cot, attn, gn2, vecs, w_out, attended],
        specs=[SM] + [VM] * 7,
    )
    pieces3, red1_a, red1_b = comm_call(
        grad_exchange_body,
        5,
        [(send3.shape, BF)] + reduced_shapes(FIRST // 16),
        [send3, sum1_a, sum1_b],
        [HB, VM, VM],
        [HB, VM, VM],
        exchange_scratch() + reduce_second_scratch(FIRST),
    )
    send4, mine1, theirs1, mlp = comm_call(
        attend_back_body,
        9,
        [
            ((N_CTX, PIECE, 2 * HD), BF),
            ((FIRST, D), BF),
            ((FIRST, D), BF),
            ((TOK, D), BF),
        ],
        [
            block_place, order, pieces3, keys, keys_t, queries, out_t, lse, red1_a, red1_b,
            mlp_part,
        ],
        [SM, SM] + [VM] * 9,
        [VM] * 4,
        [
            pltpu.VMEM((ROWS, 2 * HD), BF),
            pltpu.VMEM((HD, ROWS), F32),
            pltpu.VMEM((1, ROWS), F32),
            pltpu.VMEM((N_CTX, TOK, 2 * HD), F32),
            pltpu.VMEM((N_CTX, HALF, 2 * HD), BF),
        ]
        + tp_scratch(1)
        + spread_scratch(),
    )
    pieces4 = exchange(False, 6, send4)
    gw_qkv_t, gn1_part, vec = local_call(
        project_back_body,
        [((COLS, D), BF), ((TOK, D), BF), ((16, D), F32)],
        [pieces4, tok, normed1, w_qkv_t, sums_mid, sums_mlp],
    )
    dma = pltpu.SemaphoreType.DMA
    gn1, red2_a, red2_b = comm_call(
        gn1_sum_body,
        7,
        [((TOK, D), BF)] + reduced_shapes(SECOND // 16),
        [gn1_part, gw_up, gw_down, gw_out, gw_qkv_t, vec],
        [VM, HB, HB, HB, HB, VM],
        [VM] * 3,
        [
            pltpu.VMEM((N_TP, 16, D), BF),
            pltpu.VMEM((16, D), BF),
            pltpu.VMEM((16, D), BF),
            dma((N_TP,)),
            dma((N_TP,)),
            pltpu.VMEM((SECOND // 4, CUT), BF),
            pltpu.VMEM((SECOND // 4, D - CUT), BF),
        ]
        + tp_scratch(1)
        + reduce_first_scratch(SECOND, 4)
        + reduce_second_scratch(SECOND),
    )
    mine2, theirs2 = comm_call(
        spread_body,
        8,
        [((SECOND, D), BF), ((SECOND, D), BF)],
        [red2_a, red2_b],
        [VM, VM],
        [VM, VM],
        spread_scratch(),
    )
    output_t, grad_tok_t, g_up, g_down, g_out, g_qkv_t, *g = local_call(
        finish_body,
        [
            ((D, TOK), BF),
            ((D, TOK), F32),
            ((D, D), F32),
            ((D, D), F32),
            ((HSLOT * HD, D), F32),
            ((COLS, D), F32),
        ]
        + [((D,), F32)] * 7
        + [((HSLOT * 2 * HD,), F32)],
        [tok, attn, mlp, gn1, grad_res, vecs, mine1, theirs1, mine2, theirs2],
        out_specs=[VM, VM, HB, HB, HB, HB] + [VM] * 8,
        scratch=[
            pltpu.VMEM((D, D), F32),
            pltpu.VMEM((D, D), F32),
            pltpu.VMEM((HSLOT * HD, D), F32),
            pltpu.VMEM((COLS, D), F32),
            dma((4,)),
        ],
    )
    return (
        output_t.T[None],
        grad_tok_t.T[None],
        g[0],
        g[1],
        g_qkv_t.T,
        g[7],
        g_out,
        g[4],
        g[2],
        g[3],
        g_up,
        g[5],
        g_down,
        g[6],
    )


def solution(mesh):
    in_specs = (
        P("seq", "ctx", None), P("seq", "ctx", None), P(), P(), P(), P(), P(None, "tp"), P("tp"),
        P("tp", None), P(), P(), P(), P(None, "tp"), P("tp"), P("tp", None), P(),
    )
    out_specs = (
        P("seq", "ctx", None), P("seq", "ctx", None), P(), P(), P(None, "tp"), P("tp"),
        P("tp", None), P(), P(), P(), P(None, "tp"), P("tp"), P("tp", None), P(),
    )
    return jax.shard_map(
        on_device, mesh=mesh, in_specs=in_specs, out_specs=out_specs, check_vma=False
    )
```

```python
import functools

import jax
import jax.numpy as jnp
from jax import lax
from jax.experimental import pallas as pl
from jax.experimental.pallas import tpu as pltpu
from jax.sharding import PartitionSpec as P

HD = 64
HSLOT = 5
D = 1088
TOK = 256
N_CTX = 16
N_TP = 4
SPLIT = 3
STEP = 80
SHARE = 96
HALF = SHARE // 2
PIECE = TOK + HALF
ROWS = N_CTX * SHARE
GROUP = 128
WORK = HSLOT * SPLIT
COLS = HSLOT * 3 * HD
FIRST = 1024
REST = D - FIRST
SECOND = 768
CUT = 512
EPSILON = 1e-05
NEGATIVE = -1e30
BF = jnp.bfloat16
F32 = jnp.float32
MESH = pl.DeviceIdType.MESH
VMEM_LIMIT = 56 * 2**20

VM = pl.BlockSpec(memory_space=pltpu.VMEM)
SM = pl.BlockSpec(memory_space=pltpu.SMEM)
HB = pl.BlockSpec(memory_space=pl.ANY)


def dot(a, b):
    return jnp.dot(a, b, preferred_element_type=F32)


def dot_nt(a, b):
    return lax.dot_general(a, b, (((1,), (1,)), ((), ())), preferred_element_type=F32)


def dot_tn(a, b):
    return lax.dot_general(a, b, (((0,), (0,)), ((), ())), preferred_element_type=F32)


def pack(rows):
    return jnp.concatenate([rows[:HALF], rows[HALF:]], axis=1)


def unpack(packed):
    return jnp.concatenate([packed[:, :HD], packed[:, HD:]], axis=0)


def normalize(values):
    centered = values - jnp.mean(values, axis=-1, keepdims=True)
    inverse = lax.rsqrt(jnp.mean(centered * centered, axis=-1, keepdims=True) + EPSILON)
    return centered * inverse, inverse


def norm_backward(grad_out, normal, inverse, gain):
    grad_normal = grad_out * gain
    grad_mean = jnp.mean(grad_normal, axis=-1, keepdims=True)
    grad_along = jnp.mean(grad_normal * normal, axis=-1, keepdims=True)
    return inverse * (grad_normal - grad_mean - normal * grad_along)


def row_sum(values):
    return jnp.sum(values, axis=0, keepdims=True)


def local_call(body, outs, args, specs=None, scratch=(), out_specs=None):
    moved = sum(a.size * a.dtype.itemsize for a in args)
    return pl.pallas_call(
        body,
        out_shape=tuple(jax.ShapeDtypeStruct(shape, dtype) for shape, dtype in outs),
        in_specs=specs or [VM] * len(args),
        out_specs=tuple(out_specs or [VM] * len(outs)),
        scratch_shapes=list(scratch),
        compiler_params=pltpu.CompilerParams(vmem_limit_bytes=VMEM_LIMIT),
        cost_estimate=pl.CostEstimate(flops=0, bytes_accessed=moved, transcendentals=0),
    )(*args)


def join_shares(shares):
    return jnp.concatenate([shares[0], shares[1][16:], shares[2][16:]], axis=0)


def group_keys(first):
    low = first // SHARE
    high = (first + GROUP - 1) // SHARE
    return low * TOK, (high + 1) * TOK


def allowed_keys(first, row_offset):
    low, high = group_keys(first)
    row = first + lax.broadcasted_iota(jnp.int32, (1, GROUP), 1)
    place = jnp.full((1, GROUP), low // TOK, jnp.int32)
    for p in range(low // TOK + 1, high // TOK):
        place = place + (row >= p * SHARE).astype(jnp.int32)
    position = place * (TOK - SHARE) + row + row_offset
    key = low + lax.broadcasted_iota(jnp.int32, (high - low, GROUP), 0)
    return key <= position


def greet(peers):
    barrier = pltpu.get_barrier_semaphore()
    for peer in peers:
        pl.semaphore_signal(barrier, inc=1, device_id=peer, device_id_type=MESH)
    return lambda: pl.semaphore_wait(barrier, len(peers))


def remote(src, dst, send, recv, device):
    return pltpu.make_async_remote_copy(
        src_ref=src,
        dst_ref=dst,
        send_sem=send,
        recv_sem=recv,
        device_id=device,
        device_id_type=MESH,
    )


def rows(start, size):
    return pl.ds(pl.multiple_of(start, 16), size)


def tp_steps(parts, totals, held, send_sem, recv_sem, pending):
    me = lax.axis_index("tp")
    share = TOK // N_TP
    count = len(parts)
    started = {}
    for i in range(count):
        for k in (2, 1, 3):
            peer = lax.rem(me + k, N_TP)
            started[i, k] = remote(
                parts[i].at[rows(peer * share, share), :], held.at[i, k - 1],
                send_sem.at[0, i, k - 1], recv_sem.at[0, i, k - 1], {"tp": peer},
            )
            started[i, k].start()
    pending += started.values()
    yield
    own = rows(me * share, share)
    for i in range(count):
        total = parts[i][own, :].astype(F32)
        for k in range(1, N_TP):
            started[i, k].wait_recv()
            total = total + held[i, k - 1].astype(F32)
        totals[i][own, :] = total.astype(BF)
        for k in (2, 1, 3):
            copy = remote(
                totals[i].at[own, :], totals[i].at[own, :],
                send_sem.at[1, i, k - 1], recv_sem.at[1, i, k - 1],
                {"tp": lax.rem(me + k, N_TP)},
            )
            copy.start()
            pending.append(copy)
    yield
    for i in range(count):
        for k in range(1, N_TP):
            peer = lax.rem(me + N_TP - k, N_TP)
            there = totals[i].at[rows(peer * share, share), :]
            remote(
                there, there, send_sem.at[1, i, k - 1], recv_sem.at[1, i, k - 1], {"tp": peer}
            ).wait_recv()


def tp_scratch(count):
    return [
        pltpu.VMEM((count, N_TP - 1, TOK // N_TP, D), BF),
        pltpu.SemaphoreType.DMA((2, count, N_TP - 1)),
        pltpu.SemaphoreType.DMA((2, count, N_TP - 1)),
    ]


def tp_peers():
    me = lax.axis_index("tp")
    return [{"tp": lax.rem(me + k, N_TP)} for k in range(1, N_TP)]


class Plane:
    def __init__(self):
        ctx = lax.axis_index("ctx")
        self.core = lax.axis_index("seq")
        self.partner = {"seq": 1 - self.core}
        self.x, self.y = ctx // 4, lax.rem(ctx, 4)

    def x_of(self, k):
        return lax.rem(self.x + k, 4)

    def y_of(self, k):
        return lax.rem(self.y + k, 4)

    def at_x(self, place):
        return {"ctx": place * 4 + self.y}

    def at_y(self, place):
        return {"ctx": self.x * 4 + place}

    def peers(self):
        return (
            [self.partner]
            + [self.at_x(self.x_of(k)) for k in range(1, 4)]
            + [self.at_y(self.y_of(k)) for k in range(1, 4)]
        )


LEFT, RIGHT = slice(0, CUT), slice(CUT, D)


def ring_total(src, columns, place, size, arrived):
    value = src[rows(place * size, size), columns].astype(F32)
    for k in range(3):
        value = value + arrived[k].astype(F32)
    return value.astype(BF)


def start_all(copies, pending):
    for copy in copies:
        copy.start()
    pending.extend(copies)
    return copies


def reduce_first(plane, half, segments, held, result, pending, late=None):
    own, got, a1, b1, first_send, first_recv, first_local, ring_send, ring_recv = held
    quarter, part = half // 4, half // 16

    def keep(i, segment):
        ref, start, size, to = segment
        return pltpu.make_async_copy(
            ref.at[pl.ds(start, size), :], own.at[pl.ds(to, size), :], first_local.at[i]
        )

    def give(i, segment):
        ref, start, size, to = segment
        return remote(
            ref.at[pl.ds(start, size), :], got.at[pl.ds(to, size), :],
            first_send.at[i], first_recv.at[i], plane.partner,
        )

    for mine in range(2):

        @pl.when(plane.core == mine)
        def _():
            for i, segment in enumerate(segments[1 - mine]):
                give(i, segment).start()
            for i, segment in enumerate(segments[mine]):
                keep(i, segment).start()

    yield
    if late is not None:
        late()
    for mine in range(2):

        @pl.when(plane.core == mine)
        def _():
            for i, segment in enumerate(segments[mine]):
                keep(i, segment).wait()
                give(i, segment).wait_recv()
            for i, segment in enumerate(segments[1 - mine]):
                give(i, segment).wait_send()

    def add_rows(i, carry):
        span = rows(i * part, part)
        own[span, :] = (own[span, :].astype(F32) + got[span, :].astype(F32)).astype(BF)
        return carry

    lax.fori_loop(0, 16, add_rows, 0)
    started = []
    for k in (2, 1, 3):
        px, py = plane.x_of(k), plane.y_of(k)
        started.append(
            remote(
                own.at[rows(px * quarter, quarter), LEFT], a1.at[k - 1],
                ring_send.at[0, k - 1], ring_recv.at[0, k - 1], plane.at_x(px),
            )
        )
        started.append(
            remote(
                own.at[rows(py * quarter, quarter), RIGHT], b1.at[k - 1],
                ring_send.at[1, k - 1], ring_recv.at[1, k - 1], plane.at_y(py),
            )
        )
    start_all(started, pending)
    yield
    for copy in started:
        copy.wait_recv()
    result[0][...] = ring_total(own, LEFT, plane.x, quarter, a1)
    result[1][...] = ring_total(own, RIGHT, plane.y, quarter, b1)


def reduce_first_scratch(half, segments):
    dma = pltpu.SemaphoreType.DMA
    quarter = half // 4
    return [
        pltpu.VMEM((half, D), BF),
        pltpu.VMEM((half, D), BF),
        pltpu.VMEM((3, quarter, CUT), BF),
        pltpu.VMEM((3, quarter, D - CUT), BF),
        dma((segments,)), dma((segments,)), dma((segments,)), dma((2, 3)), dma((2, 3)),
    ]


def reduce_second(plane, half, partial, held, result, pending):
    sa, sb = partial
    a2, b2, ring_send, ring_recv = held
    part = half // 16
    started = []
    for k in (2, 1, 3):
        px, py = plane.x_of(k), plane.y_of(k)
        started.append(
            remote(
                sa.at[rows(py * part, part), :], a2.at[k - 1],
                ring_send.at[0, k - 1], ring_recv.at[0, k - 1], plane.at_y(py),
            )
        )
        started.append(
            remote(
                sb.at[rows(px * part, part), :], b2.at[k - 1],
                ring_send.at[1, k - 1], ring_recv.at[1, k - 1], plane.at_x(px),
            )
        )
    start_all(started, pending)
    yield
    for copy in started:
        copy.wait_recv()
    result[0][...] = ring_total(sa, slice(0, CUT), plane.y, part, a2)
    result[1][...] = ring_total(sb, slice(0, D - CUT), plane.x, part, b2)


def reduce_second_scratch(half):
    dma = pltpu.SemaphoreType.DMA
    part = half // 16
    return [
        pltpu.VMEM((3, part, CUT), BF), pltpu.VMEM((3, part, D - CUT), BF),
        dma((2, 3)), dma((2, 3)),
    ]


def reduced_shapes(count):
    return [((count, CUT), BF), ((count, D - CUT), BF)]


def spread_steps(plane, half, reduced, mine, theirs, sems, pending):
    red_a, red_b = reduced
    ring_send, ring_recv, pair_send, pair_recv = sems
    quarter, part = half // 4, half // 16
    x, y, x_of, y_of = plane.x, plane.y, plane.x_of, plane.y_of

    def piece_a(px, py):
        return mine.at[rows(px * quarter + py * part, part), LEFT]

    def piece_b(px, py):
        return mine.at[rows(py * quarter + px * part, part), RIGHT]

    def band_a(px):
        return mine.at[rows(px * quarter, quarter), LEFT]

    def band_b(py):
        return mine.at[rows(py * quarter, quarter), RIGHT]

    def sem(number, side, k):
        return ring_send.at[number, side, k - 1], ring_recv.at[number, side, k - 1]

    def pair(k):
        px, py = x_of(4 - k), y_of(4 - k)
        return [
            remote(
                band_a(px), theirs.at[rows(px * quarter, quarter), LEFT],
                pair_send.at[0, k], pair_recv.at[0, k], plane.partner,
            ),
            remote(
                band_b(py), theirs.at[rows(py * quarter, quarter), RIGHT],
                pair_send.at[1, k], pair_recv.at[1, k], plane.partner,
            ),
        ]

    piece_a(x, y)[...] = red_a[...]
    piece_b(x, y)[...] = red_b[...]
    started = []
    for k in (2, 1, 3):
        started.append(remote(red_a, piece_a(x, y), *sem(0, 0, k), plane.at_y(y_of(k))))
        started.append(remote(red_b, piece_b(x, y), *sem(0, 1, k), plane.at_x(x_of(k))))
    start_all(started, pending)
    yield
    for k in range(1, 4):
        there = y_of(4 - k)
        remote(red_a, piece_a(x, there), *sem(0, 0, k), plane.at_y(there)).wait_recv()
        there = x_of(4 - k)
        remote(red_b, piece_b(there, y), *sem(0, 1, k), plane.at_x(there)).wait_recv()
    started = []
    for k in (2, 1, 3):
        started.append(remote(band_a(x), band_a(x), *sem(1, 0, k), plane.at_x(x_of(k))))
        started.append(remote(band_b(y), band_b(y), *sem(1, 1, k), plane.at_y(y_of(k))))
    start_all(started + pair(0), pending)
    yield
    for k in (1, 3, 2):
        there = x_of(4 - k)
        remote(band_a(there), band_a(there), *sem(1, 0, k), plane.at_x(there)).wait_recv()
        there = y_of(4 - k)
        remote(band_b(there), band_b(there), *sem(1, 1, k), plane.at_y(there)).wait_recv()
        start_all(pair(k), pending)
    yield
    for k in range(4):
        for copy in pair(k):
            copy.wait_recv()


def spread_scratch():
    dma = pltpu.SemaphoreType.DMA
    return [dma((2, 2, 3)), dma((2, 2, 3)), dma((2, 4)), dma((2, 4))]


def take_turns(*generators):
    waiting = list(generators)
    while waiting:
        for generator in list(waiting):
            try:
                next(generator)
            except StopIteration:
                waiting.remove(generator)


def comm_call(body, collective_id, outs, args, specs, out_specs, scratch):
    return pl.pallas_call(
        body,
        out_shape=tuple(jax.ShapeDtypeStruct(shape, dtype) for shape, dtype in outs),
        in_specs=specs,
        out_specs=tuple(out_specs),
        scratch_shapes=scratch,
        compiler_params=pltpu.CompilerParams(
            collective_id=collective_id, has_side_effects=True, vmem_limit_bytes=VMEM_LIMIT
        ),
    )(*args)


def exchange_steps(to_workers, source, dst, sems, pending, prepare=None):
    send_sem, recv_sem, local_sem = sems
    me = lax.axis_index("ctx")
    works = me < WORK

    def copy(k, peer, slot):
        return remote(
            source(k, peer), dst.at[slot], send_sem.at[k], recv_sem.at[k], {"ctx": peer}
        )

    own = pltpu.make_async_copy(source(0, me), dst.at[me], local_sem)
    for k in EXCHANGE_ORDER:
        peer = lax.rem(me + k, N_CTX)
        if prepare is not None:
            prepare(k, peer)
        if k:
            pl.when(peer < WORK if to_workers else works)(copy(k, peer, me).start)
        else:
            pl.when(works)(own.start)
    yield
    pl.when(works)(own.wait)
    for k in range(1, N_CTX):
        peer = lax.rem(me + N_CTX - k, N_CTX)
        pl.when(works if to_workers else peer < WORK)(copy(k, peer, peer).wait_recv)
    yield
    for k in range(1, N_CTX):
        peer = lax.rem(me + k, N_CTX)
        pl.when(peer < WORK if to_workers else works)(copy(k, peer, me).wait_send)


EXCHANGE_ORDER = tuple(range(1, N_CTX)) + (0,)


def ctx_peers():
    me = lax.axis_index("ctx")
    return [{"ctx": lax.rem(me + k, N_CTX)} for k in range(1, N_CTX)]


def exchange_scratch():
    dma = pltpu.SemaphoreType.DMA
    return [dma((N_CTX,)), dma((N_CTX,)), dma]


def finish_sends(pending):
    for copy in pending:
        copy.wait_send()


def order_of(block_place):
    order = []
    for p in range(N_CTX):
        owner = jnp.int32(0)
        for i in range(1, N_CTX):
            owner = jnp.where(block_place[i] == p, i, owner)
        order.append(owner)
    return order


def project_body(tok_t, cot_t, w_t, *rest):
    rows_in, (pieces, normed_out, tok, cot, vecs, send, *sems) = rest[:8], rest[8:]
    greeted = greet(ctx_peers())
    pending = []
    tok[...] = tok_t[...].T
    for i, ref in enumerate(rows_in):
        vecs[i : i + 1, : ref.shape[0]] = ref[...].astype(F32).reshape(1, ref.shape[0])
    normal, _ = normalize(tok[...].astype(F32))
    normed = (normal * vecs[0:1, :] + vecs[1:2, :]).astype(BF)
    normed_out[...] = normed
    projected = dot_nt(normed, w_t[...])
    upper = lax.broadcasted_iota(jnp.int32, (1, 2 * HD), 1) >= HD
    for s in range(HSLOT):
        base = 3 * HD * s
        bias = vecs[7:8, 2 * HD * s : 2 * HD * (s + 1)]
        pair = projected[:, base + HD : base + 3 * HD] + jnp.where(upper, bias, 0.0)
        pair = pair.astype(BF)
        queries = (projected[:, base : base + HD] + bias[:, :HD]).astype(BF)
        queries = queries * jnp.asarray(HD**-0.5, BF)
        for j in range(SPLIT):
            send[SPLIT * s + j, :TOK, :] = pair
            send[SPLIT * s + j, TOK:, :] = pack(queries[STEP * j : STEP * j + SHARE])
    greeted()
    steps = exchange_steps(True, lambda k, peer: send.at[peer], pieces, sems, pending)
    next(steps)
    cot[...] = cot_t[...].T
    take_turns(steps)
    finish_sends(pending)


def attend_body(
    block_place, head_count, pieces, w_out,
    keys, keys_t, queries, out_t, lse, attended, attn,
    packed, stage, arrived, part, *scratch,
):
    greeted = greet(ctx_peers() + tp_peers())
    pending = []
    order = order_of(block_place)
    ctx = lax.axis_index("ctx")
    row_offset = lax.rem(ctx, SPLIT) * STEP
    live = (ctx // SPLIT < head_count[lax.axis_index("tp")]).astype(F32)
    for p in range(N_CTX):
        owner = order[p]
        pair = pieces[owner, :TOK, :]
        keys[p * TOK : (p + 1) * TOK, :] = pair
        keys_t[:, p * TOK : (p + 1) * TOK] = pair.T
        share = unpack(pieces[owner, TOK:, :])
        queries[p * SHARE : (p + 1) * SHARE, :] = jnp.concatenate(
            [share, jnp.zeros((SHARE, HD), BF)], axis=1
        )
    for first in range(0, ROWS, GROUP):
        low, high = group_keys(first)
        block = queries[first : first + GROUP, :]
        edge = jnp.where(
            allowed_keys(first, row_offset), dot_nt(keys[low:high, :], block), NEGATIVE
        )
        top = jnp.max(edge, axis=0, keepdims=True)
        if low:
            body = dot_nt(keys[:low, :], block)
            top = jnp.maximum(top, jnp.max(body, axis=0, keepdims=True))
        weights = jnp.exp(edge - top)
        total = jnp.sum(weights, axis=0, keepdims=True)
        mixed = dot(keys_t[HD:, low:high], weights.astype(BF))
        if low:
            weights = jnp.exp(body - top)
            total = total + jnp.sum(weights, axis=0, keepdims=True)
            mixed = mixed + dot(keys_t[HD:, :low], weights.astype(BF))
        out_t[:, first : first + GROUP] = mixed / total * live
        lse[:, first : first + GROUP] = top + jnp.log(total)
    for p in range(N_CTX):
        packed[p] = pack(out_t[:, p * SHARE : (p + 1) * SHARE].T.astype(BF))
    greeted()

    def prepare(k, peer):
        stage[k] = packed[block_place[peer]]

    steps = exchange_steps(
        False, lambda k, peer: stage.at[k], arrived, scratch[:3], pending, prepare
    )
    next(steps)
    next(steps)
    heads = []
    for s in range(HSLOT):
        heads.append(join_shares([unpack(arrived[SPLIT * s + j]) for j in range(SPLIT)]))
    joined = jnp.concatenate(heads, axis=1)
    attended[...] = joined
    part[...] = dot(joined, w_out[...]).astype(BF)
    take_turns(tp_steps([part], [attn], *scratch[3:], pending))
    take_turns(steps)
    finish_sends(pending)


def mlp_body(
    tok, cot, attn, vecs, w_up, w_down,
    mlp_part, gn2, sum_a, sum_b, rest_up, rest_down, sums,
    gn2_part, gw_up, gw_down, *scratch,
):
    plane = Plane()
    greeted = greet(plane.peers() + tp_peers())
    pending = []
    residual = tok[...].astype(F32) + (attn[...].astype(F32) + vecs[4:5, :])
    normal, _ = normalize(residual)
    normed = (normal * vecs[2:3, :] + vecs[3:4, :]).astype(BF)
    hidden = dot(normed, w_up[...]) + vecs[6:7, :]
    cdf = 0.5 * (1.0 + lax.erf(hidden * (0.5**0.5)))
    cot_low = cot[...]
    grad_act = dot_nt(cot_low, w_down[...])
    slope = cdf + hidden * jnp.exp(-0.5 * hidden * hidden) * 0.3989422804014327
    grad_hidden = (grad_act * slope).astype(BF)
    gn2_part[...] = dot_nt(grad_hidden, w_up[...]).astype(BF)
    greeted()
    total = tp_steps([gn2_part], [gn2], *scratch[:3], pending)
    next(total)
    activated = (hidden * cdf).astype(BF)
    gw_down[...] = dot_tn(activated, cot_low).astype(BF)
    gw_up[...] = dot_tn(normed, grad_hidden).astype(BF)
    segments = (((gw_up, 0, FIRST, 0),), ((gw_down, 0, FIRST, 0),))
    weights = reduce_first(plane, FIRST, segments, scratch[3:], (sum_a, sum_b), pending)
    next(weights)
    mlp_part[...] = dot(activated, w_down[...]).astype(BF)
    rest_up[...] = gw_up[FIRST:, :]
    rest_down[...] = gw_down[FIRST:, :]
    sums[...] = jnp.zeros_like(sums)
    sums[0:1, :] = row_sum(grad_hidden.astype(F32))
    sums[1:2, :] = row_sum(cot_low.astype(F32))
    take_turns(weights, total)
    finish_sends(pending)


def attend_back_body(
    block_place, head_count, tok, cot, attn, gn2, vecs, w_out, attended,
    keys, keys_t, queries, out_t, lse, sum_a, sum_b, mlp_part,
    grad_res, gw_out, sums, mine, theirs, mlp, pieces4,
    send3, pieces3, red_a, red_b, grads, grad_q, dots, acc, packed, stage, *scratch,
):
    plane = Plane()
    greeted = greet(ctx_peers() + tp_peers() + [plane.partner])
    pending = []
    scatter_sems, gather_sems, tp, second, ring = (
        scratch[:3], scratch[3:6], scratch[6:9], scratch[9:13], scratch[13:],
    )
    order = order_of(block_place)
    greeted()
    reduce = reduce_second(plane, FIRST, (sum_a, sum_b), second, (red_a, red_b), pending)
    total = tp_steps([mlp_part], [mlp], *tp, pending)
    next(reduce)
    next(total)

    residual = tok[...].astype(F32) + (attn[...].astype(F32) + vecs[4:5, :])
    normal, inverse = normalize(residual)
    grad_norm = gn2[...].astype(F32)
    grad = cot[...].astype(F32) + norm_backward(grad_norm, normal, inverse, vecs[2:3, :])
    grad_low = grad.astype(BF)
    live_lanes = head_count[lax.axis_index("tp")] * HD
    lane = lax.broadcasted_iota(jnp.int32, (1, HSLOT * HD), 1)
    live = (lane < live_lanes).astype(F32)
    grad_att = (dot_nt(grad_low, w_out[...]) * live).astype(BF)
    for s in range(HSLOT):
        head = grad_att[:, HD * s : HD * (s + 1)]
        for j in range(SPLIT):
            share = head[STEP * j : STEP * j + SHARE]
            if j:
                share = jnp.concatenate([jnp.zeros((16, HD), BF), share[16:]], axis=0)
            send3[SPLIT * s + j] = pack(share)
    scatter = exchange_steps(
        True, lambda k, peer: send3.at[peer], pieces3, scatter_sems, pending
    )
    next(scatter)
    take_turns(reduce)
    spread = spread_steps(plane, FIRST, (red_a, red_b), mine, theirs, ring, pending)
    next(spread)
    grad_res[...] = grad
    gw_out[...] = dot_tn(attended[...], grad_low).astype(BF)
    sums[...] = jnp.zeros_like(sums)
    sums[0:1, :] = row_sum(grad_norm * normal)
    sums[1:2, :] = row_sum(grad_norm)
    sums[2:3, :] = row_sum(grad_low.astype(F32))
    acc[...] = jnp.zeros_like(acc)
    next(scatter)
    next(spread)
    next(total)

    row_offset = lax.rem(lax.axis_index("ctx"), SPLIT) * STEP
    for p in range(N_CTX):
        share = unpack(pieces3[order[p]])
        grads[p * SHARE : (p + 1) * SHARE, :] = jnp.concatenate(
            [jnp.zeros((SHARE, HD), BF), share], axis=1
        )
    for first in range(0, ROWS, GROUP):
        turned = grads[first : first + GROUP, :].astype(F32).T
        dots[:, first : first + GROUP] = jnp.sum(
            turned[HD:, :] * out_t[:, first : first + GROUP], axis=0, keepdims=True
        )
    for first in range(0, ROWS, GROUP):
        low, high = group_keys(first)
        span = slice(first, first + GROUP)
        both = jnp.concatenate([queries[span, :], grads[span, :]], axis=0)
        grad_block = jnp.zeros((HD, GROUP), F32)
        for start, stop in ((0, low), (low, high)):
            if start == stop:
                continue
            scores = dot_nt(keys[start:stop, :], both)
            weights = jnp.exp(scores[:, :GROUP] - lse[:, span])
            if start == low:
                weights = jnp.where(allowed_keys(first, row_offset), weights, 0.0)
            grad_scores = (weights * (scores[:, GROUP:] - dots[:, span])).astype(BF)
            pair = jnp.concatenate([grad_scores, weights.astype(BF)], axis=1)
            blocks = slice(start // TOK, stop // TOK)
            acc[blocks] += dot(pair, both).reshape(-1, TOK, 2 * HD)
            grad_block = grad_block + dot(keys_t[:HD, start:stop], grad_scores)
        grad_q[:, span] = grad_block * (HD**-0.5)
    for p in range(N_CTX):
        packed[p] = pack(grad_q[:, p * SHARE : (p + 1) * SHARE].T.astype(BF))

    def prepare(k, peer):
        place = block_place[peer]
        stage[k, :TOK, :] = acc[place].astype(BF)
        stage[k, TOK:, :] = packed[place]

    gather = exchange_steps(
        False, lambda k, peer: stage.at[k], pieces4, gather_sems, pending, prepare
    )
    take_turns(gather, spread, total, scatter)
    finish_sends(pending)


VEC_AT = 2 * REST + HSLOT * HD + COLS


def project_back_body(
    pieces, tok, normed, w_t, sums_mid, sums_mlp, up, down, w_out,
    gn1, mine, theirs,
    gw_qkv_t, part, vec, vec_parts, vec_low, vec_got, vec_send, vec_recv,
    sum_a, sum_b, red_a, red_b, *scratch,
):
    plane = Plane()
    greeted = greet(plane.peers() + tp_peers())
    pending = []
    tp, weights, second, ring = scratch[:3], scratch[3:12], scratch[12:16], scratch[16:]
    own, got = weights[:2]
    me = lax.axis_index("tp")

    @pl.when(plane.core == 1)
    def _():
        own[SECOND - 128 :, :] = jnp.zeros((128, D), BF)
        got[SECOND - 128 :, :] = jnp.zeros((128, D), BF)

    columns, biases = [], []
    for s in range(HSLOT):
        shares = [pieces[SPLIT * s + j] for j in range(SPLIT)]
        pair = shares[0][:TOK].astype(F32)
        for piece in shares[1:]:
            pair = pair + piece[:TOK].astype(F32)
        pair = pair.astype(BF)
        queries = join_shares([unpack(piece[TOK:]) for piece in shares])
        columns += [queries, pair]
        biases += [row_sum(queries.astype(F32)), row_sum(pair.astype(F32))[:, HD:]]
    grads = jnp.concatenate(columns, axis=1)
    gw_qkv_t[...] = dot_tn(grads, normed[...]).astype(BF)
    greeted()

    def add_vectors():
        for k in range(1, N_TP):
            there = vec_parts.at[lax.rem(me + N_TP - k, N_TP)]
            remote(there, there, vec_send.at[k], vec_recv.at[k], plane.partner).wait_recv()
        over_tp = vec_parts[0].astype(F32)
        for t in range(1, N_TP):
            over_tp = over_tp + vec_parts[t].astype(F32)
        row = lax.broadcasted_iota(jnp.int32, (16, 1), 0)
        vec_low[...] = jnp.where(row < 2, over_tp, vec[...]).astype(BF)
        copy = remote(vec_low, vec_got, vec_send.at[0], vec_recv.at[0], plane.partner)
        start_all([copy], pending)
        copy.wait_recv()

        @pl.when(plane.core == 1)
        def _():
            own[SECOND - 128 : SECOND - 112, :] = vec_low[...]
            got[SECOND - 128 : SECOND - 112, :] = vec_got[...]

    segments = (
        (
            (up, 0, REST, 0),
            (down, 0, REST, REST),
            (w_out, 0, HSLOT * HD, 2 * REST),
            (gw_qkv_t, 0, 320, 448),
        ),
        ((gw_qkv_t, 320, 640, 0),),
    )

    def all_weights():
        yield from reduce_first(
            plane, SECOND, segments, weights, (sum_a, sum_b), pending, late=add_vectors
        )
        yield from reduce_second(plane, SECOND, (sum_a, sum_b), second, (red_a, red_b), pending)
        yield from spread_steps(plane, SECOND, (red_a, red_b), mine, theirs, ring, pending)

    steps = all_weights()
    next(steps)
    product = dot(grads, w_t[...])
    part[...] = product.astype(BF)
    total = tp_steps([part], [gn1], *tp, pending)
    normal, _ = normalize(tok[...].astype(F32))
    vec[0:1, :] = row_sum(product * normal)
    vec[1:2, :] = row_sum(product)
    vec[2:5, :] = sums_mid[0:3, :]
    vec[5:7, :] = sums_mlp[0:2, :]
    vec[7:8, : HSLOT * 2 * HD] = jnp.concatenate(biases, axis=1)
    vec[7:8, HSLOT * 2 * HD :] = jnp.zeros((1, D - HSLOT * 2 * HD), F32)
    vec[8:, :] = jnp.zeros((8, D), F32)
    vec_parts[me] = vec[...].astype(BF)
    for k in range(1, N_TP):
        copy = remote(
            vec_parts.at[me], vec_parts.at[me], vec_send.at[k], vec_recv.at[k],
            {"tp": lax.rem(me + k, N_TP)},
        )
        start_all([copy], pending)
    next(total)
    take_turns(steps, total)
    finish_sends(pending)


def finish_body(
    tok, attn, mlp, gn1, grad_res, vecs, mine1, theirs1, mine2, theirs2,
    output_t, grad_tok_t, up_out, down_out, w_out_out, w_qkv_out, *rest,
):
    vec_outs, (up, down, w_out, w_qkv, out_sem) = rest[:8], rest[8:]
    top = 2 * REST + HSLOT * HD
    core = lax.axis_index("seq")
    copies = []

    def by_core(action):
        pl.when(core == 0)(lambda: action(mine1, theirs1, mine2, theirs2))
        pl.when(core == 1)(lambda: action(theirs1, mine1, theirs2, mine2))

    def write(src, dst):
        copies.append(pltpu.make_async_copy(src, dst, out_sem.at[len(copies)]))
        copies[-1].start()

    def cast_up(low1, high1, low2, high2):
        up[:FIRST, :] = low1[...].astype(F32)
        up[FIRST:, :] = low2[:REST, :].astype(F32)

    def cast_down(low1, high1, low2, high2):
        down[:FIRST, :] = high1[...].astype(F32)
        down[FIRST:, :] = low2[REST : 2 * REST, :].astype(F32)

    def cast_qkv(low1, high1, low2, high2):
        w_qkv[: SECOND - top, :] = low2[top:, :].astype(F32)
        w_qkv[SECOND - top :, :] = high2[: VEC_AT - SECOND, :].astype(F32)

    def cast_rest(low1, high1, low2, high2):
        w_out[...] = low2[2 * REST : top, :].astype(F32)
        vectors = high2[VEC_AT - SECOND : VEC_AT - SECOND + 16, :].astype(F32)
        for i, ref in enumerate(vec_outs):
            ref[...] = vectors[i, : ref.shape[0]]

    by_core(cast_up)
    write(up, up_out)
    by_core(cast_down)
    write(down, down_out)
    by_core(cast_qkv)
    write(w_qkv, w_qkv_out)
    by_core(cast_rest)
    write(w_out, w_out_out)
    inputs = tok[...].astype(F32)
    residual = inputs + (attn[...].astype(F32) + vecs[4:5, :])
    output_t[...] = (residual + (mlp[...].astype(F32) + vecs[5:6, :])).astype(BF).T
    normal, inverse = normalize(inputs)
    grad_norm = gn1[...].astype(F32)
    grad = grad_res[...] + norm_backward(grad_norm, normal, inverse, vecs[0:1, :])
    grad_tok_t[...] = grad.T
    for copy in copies:
        copy.wait()


def on_device(
    tokens, cotangent, block_place, head_count, ln1_gain, ln1_bias, w_qkv, b_qv, w_out, b_out,
    ln2_gain, ln2_bias, w_up, b_up, w_down, b_down,
):
    w_qkv_t = w_qkv.T
    dma = pltpu.SemaphoreType.DMA
    row_shape, piece_shape, half_shape = (
        ((TOK, D), BF), ((N_CTX, PIECE, 2 * HD), BF), ((N_CTX, HALF, 2 * HD), BF),
    )

    def buffer(shaped):
        return pltpu.VMEM(*shaped)

    pieces1, normed1, tok, cot, vecs = comm_call(
        project_body,
        1,
        [piece_shape, row_shape, row_shape, row_shape, ((8, D), F32)],
        [tokens[0].T, cotangent[0].T, w_qkv_t]
        + [ln1_gain, ln1_bias, ln2_gain, ln2_bias, b_out, b_down, b_up, b_qv],
        [VM] * 11,
        [VM] * 5,
        [buffer(piece_shape)] + exchange_scratch(),
    )
    keys, keys_t, queries, out_t, lse, attended, attn = comm_call(
        attend_body,
        2,
        [
            ((N_CTX * TOK, 2 * HD), BF),
            ((2 * HD, N_CTX * TOK), BF),
            ((ROWS, 2 * HD), BF),
            ((HD, ROWS), F32),
            ((1, ROWS), F32),
            ((TOK, HSLOT * HD), BF),
            row_shape,
        ],
        [block_place, head_count, pieces1, w_out],
        [SM, SM, VM, VM],
        [VM] * 7,
        [buffer(half_shape), buffer(half_shape), buffer(half_shape), buffer(row_shape)]
        + exchange_scratch()
        + tp_scratch(1),
    )
    mlp_part, gn2, sum1_a, sum1_b, rest_up, rest_down, sums_mlp = comm_call(
        mlp_body,
        3,
        [row_shape, row_shape]
        + reduced_shapes(FIRST // 4)
        + [((REST, D), BF), ((REST, D), BF), ((8, D), F32)],
        [tok, cot, attn, vecs, w_up, w_down],
        [VM] * 6,
        [VM] * 7,
        [buffer(row_shape), pltpu.VMEM((D, D), BF), pltpu.VMEM((D, D), BF)]
        + tp_scratch(1)
        + reduce_first_scratch(FIRST, 1),
    )
    grad_res, gw_out, sums_mid, mine1, theirs1, mlp, pieces4 = comm_call(
        attend_back_body,
        4,
        [
            ((TOK, D), F32),
            ((HSLOT * HD, D), BF),
            ((8, D), F32),
            ((FIRST, D), BF),
            ((FIRST, D), BF),
            row_shape,
            piece_shape,
        ],
        [
            block_place, head_count, tok, cot, attn, gn2, vecs, w_out, attended,
            keys, keys_t, queries, out_t, lse, sum1_a, sum1_b, mlp_part,
        ],
        [SM, SM] + [VM] * 15,
        [VM] * 7,
        [buffer(half_shape), buffer(half_shape)]
        + [buffer(s) for s in reduced_shapes(FIRST // 16)]
        + [
            pltpu.VMEM((ROWS, 2 * HD), BF),
            pltpu.VMEM((HD, ROWS), F32),
            pltpu.VMEM((1, ROWS), F32),
            pltpu.VMEM((N_CTX, TOK, 2 * HD), F32),
            buffer(half_shape),
            buffer(piece_shape),
        ]
        + exchange_scratch()
        + exchange_scratch()
        + tp_scratch(1)
        + reduce_second_scratch(FIRST)
        + spread_scratch(),
    )
    gn1, mine2, theirs2 = comm_call(
        project_back_body,
        5,
        [row_shape, ((SECOND, D), BF), ((SECOND, D), BF)],
        [pieces4, tok, normed1, w_qkv_t, sums_mid, sums_mlp, rest_up, rest_down, gw_out],
        [VM] * 9,
        [VM] * 3,
        [
            pltpu.VMEM((COLS, D), BF),
            buffer(row_shape),
            pltpu.VMEM((16, D), F32),
            pltpu.VMEM((N_TP, 16, D), BF),
            pltpu.VMEM((16, D), BF),
            pltpu.VMEM((16, D), BF),
            dma((N_TP,)),
            dma((N_TP,)),
        ]
        + [buffer(s) for s in reduced_shapes(SECOND // 4) + reduced_shapes(SECOND // 16)]
        + tp_scratch(1)
        + reduce_first_scratch(SECOND, 4)
        + reduce_second_scratch(SECOND)
        + spread_scratch(),
    )
    output_t, grad_tok_t, g_up, g_down, g_out, g_qkv_t, *g = local_call(
        finish_body,
        [
            ((D, TOK), BF),
            ((D, TOK), F32),
            ((D, D), F32),
            ((D, D), F32),
            ((HSLOT * HD, D), F32),
            ((COLS, D), F32),
        ]
        + [((D,), F32)] * 7
        + [((HSLOT * 2 * HD,), F32)],
        [tok, attn, mlp, gn1, grad_res, vecs, mine1, theirs1, mine2, theirs2],
        out_specs=[VM, VM, HB, HB, HB, HB] + [VM] * 8,
        scratch=[
            pltpu.VMEM((D, D), F32),
            pltpu.VMEM((D, D), F32),
            pltpu.VMEM((HSLOT * HD, D), F32),
            pltpu.VMEM((COLS, D), F32),
            dma((4,)),
        ],
    )
    return (
        output_t.T[None],
        grad_tok_t.T[None],
        g[0],
        g[1],
        g_qkv_t.T,
        g[7],
        g_out,
        g[4],
        g[2],
        g[3],
        g_up,
        g[5],
        g_down,
        g[6],
    )


def solution(mesh):
    in_specs = (
        P("seq", "ctx", None), P("seq", "ctx", None), P(), P(), P(), P(), P(None, "tp"), P("tp"),
        P("tp", None), P(), P(), P(), P(None, "tp"), P("tp"), P("tp", None), P(),
    )
    out_specs = (
        P("seq", "ctx", None), P("seq", "ctx", None), P(), P(), P(None, "tp"), P("tp"),
        P("tp", None), P(), P(), P(), P(None, "tp"), P("tp"), P("tp", None), P(),
    )
    return jax.shard_map(
        on_device, mesh=mesh, in_specs=in_specs, out_specs=out_specs, check_vma=False
    )
```

```python
import functools

import jax
import jax.numpy as jnp
from jax import lax
from jax.experimental import pallas as pl
from jax.experimental.pallas import tpu as pltpu
from jax.sharding import PartitionSpec as P

HD = 64
HSLOT = 5
D = 1088
TOK = 256
N_CTX = 16
N_TP = 4
SPLIT = 3
STEP = 80
SHARE = 96
HALF = SHARE // 2
PIECE = TOK + HALF
ROWS = N_CTX * SHARE
GROUP = 128
WORK = HSLOT * SPLIT
COLS = HSLOT * 3 * HD
FIRST = 1024
REST = D - FIRST
SECOND = 768
CUT = 512
EPSILON = 1e-05
NEGATIVE = -1e30
BF = jnp.bfloat16
F32 = jnp.float32
MESH = pl.DeviceIdType.MESH
MIB = 2**20
LIMITS = (56, 20, 20, 20, 20, 24)

VM = pl.BlockSpec(memory_space=pltpu.VMEM)
SM = pl.BlockSpec(memory_space=pltpu.SMEM)
HB = pl.BlockSpec(memory_space=pl.ANY)


def dot(a, b):
    return jnp.dot(a, b, preferred_element_type=F32)


def dot_nt(a, b):
    return lax.dot_general(a, b, (((1,), (1,)), ((), ())), preferred_element_type=F32)


def dot_tn(a, b):
    return lax.dot_general(a, b, (((0,), (0,)), ((), ())), preferred_element_type=F32)


def pack(rows):
    return jnp.concatenate([rows[:HALF], rows[HALF:]], axis=1)


def unpack(packed):
    return jnp.concatenate([packed[:, :HD], packed[:, HD:]], axis=0)


def normalize(values):
    centered = values - jnp.mean(values, axis=-1, keepdims=True)
    inverse = lax.rsqrt(jnp.mean(centered * centered, axis=-1, keepdims=True) + EPSILON)
    return centered * inverse, inverse


def norm_backward(grad_out, normal, inverse, gain):
    grad_normal = grad_out * gain
    grad_mean = jnp.mean(grad_normal, axis=-1, keepdims=True)
    grad_along = jnp.mean(grad_normal * normal, axis=-1, keepdims=True)
    return inverse * (grad_normal - grad_mean - normal * grad_along)


def row_sum(values):
    return jnp.sum(values, axis=0, keepdims=True)


def local_call(body, index, outs, args, specs=None, scratch=(), out_specs=None):
    moved = sum(a.size * a.dtype.itemsize for a in args)
    return pl.pallas_call(
        body,
        out_shape=tuple(jax.ShapeDtypeStruct(shape, dtype) for shape, dtype in outs),
        in_specs=specs or [VM] * len(args),
        out_specs=tuple(out_specs or [VM] * len(outs)),
        scratch_shapes=list(scratch),
        compiler_params=pltpu.CompilerParams(vmem_limit_bytes=LIMITS[index] * MIB),
        cost_estimate=pl.CostEstimate(flops=0, bytes_accessed=moved, transcendentals=0),
    )(*args)


def join_shares(shares):
    return jnp.concatenate([shares[0], shares[1][16:], shares[2][16:]], axis=0)


def group_keys(first):
    low = first // SHARE
    high = (first + GROUP - 1) // SHARE
    return low * TOK, (high + 1) * TOK


def allowed_keys(first, row_offset):
    low, high = group_keys(first)
    row = first + lax.broadcasted_iota(jnp.int32, (1, GROUP), 1)
    place = jnp.full((1, GROUP), low // TOK, jnp.int32)
    for p in range(low // TOK + 1, high // TOK):
        place = place + (row >= p * SHARE).astype(jnp.int32)
    position = place * (TOK - SHARE) + row + row_offset
    key = low + lax.broadcasted_iota(jnp.int32, (high - low, GROUP), 0)
    return key <= position


def greet(peers):
    barrier = pltpu.get_barrier_semaphore()
    for peer in peers:
        pl.semaphore_signal(barrier, inc=1, device_id=peer, device_id_type=MESH)
    return lambda: pl.semaphore_wait(barrier, len(peers))


def remote(src, dst, send, recv, device):
    return pltpu.make_async_remote_copy(
        src_ref=src,
        dst_ref=dst,
        send_sem=send,
        recv_sem=recv,
        device_id=device,
        device_id_type=MESH,
    )


def rows(start, size):
    return pl.ds(pl.multiple_of(start, 16), size)


def tp_steps(parts, totals, held, send_sem, recv_sem, pending):
    me = lax.axis_index("tp")
    share = TOK // N_TP
    count = len(parts)
    started = {}
    for i in range(count):
        for k in (2, 1, 3):
            peer = lax.rem(me + k, N_TP)
            started[i, k] = remote(
                parts[i].at[rows(peer * share, share), :], held.at[i, k - 1],
                send_sem.at[0, i, k - 1], recv_sem.at[0, i, k - 1], {"tp": peer},
            )
            started[i, k].start()
    pending += started.values()
    yield
    own = rows(me * share, share)
    for i in range(count):
        total = parts[i][own, :].astype(F32)
        for k in range(1, N_TP):
            started[i, k].wait_recv()
            total = total + held[i, k - 1].astype(F32)
        totals[i][own, :] = total.astype(BF)
        for k in (2, 1, 3):
            copy = remote(
                totals[i].at[own, :], totals[i].at[own, :],
                send_sem.at[1, i, k - 1], recv_sem.at[1, i, k - 1],
                {"tp": lax.rem(me + k, N_TP)},
            )
            copy.start()
            pending.append(copy)
    yield
    for i in range(count):
        for k in range(1, N_TP):
            peer = lax.rem(me + N_TP - k, N_TP)
            there = totals[i].at[rows(peer * share, share), :]
            remote(
                there, there, send_sem.at[1, i, k - 1], recv_sem.at[1, i, k - 1], {"tp": peer}
            ).wait_recv()


def tp_scratch(count):
    return [
        pltpu.VMEM((count, N_TP - 1, TOK // N_TP, D), BF),
        pltpu.SemaphoreType.DMA((2, count, N_TP - 1)),
        pltpu.SemaphoreType.DMA((2, count, N_TP - 1)),
    ]


def tp_peers():
    me = lax.axis_index("tp")
    return [{"tp": lax.rem(me + k, N_TP)} for k in range(1, N_TP)]


class Plane:
    def __init__(self):
        ctx = lax.axis_index("ctx")
        self.core = lax.axis_index("seq")
        self.partner = {"seq": 1 - self.core}
        self.x, self.y = ctx // 4, lax.rem(ctx, 4)

    def place(self, axis, k=0):
        return lax.rem((self.x, self.y)[axis] + k, 4)

    def device(self, axis, place):
        return {"ctx": self.x * 4 + place if axis else place * 4 + self.y}

    def peers(self):
        return [self.partner] + [
            self.device(axis, self.place(axis, k)) for axis in range(2) for k in range(1, 4)
        ]


SIDES = {
    FIRST: ((0, FIRST // 2, slice(0, D)), (FIRST // 2, FIRST // 2, slice(0, D))),
    SECOND: ((0, SECOND, slice(0, CUT)), (0, SECOND, slice(CUT, D))),
}


def side_shapes(half, pieces, lead=()):
    return [
        (lead + (count // pieces, columns.stop - columns.start), BF)
        for _, count, columns in SIDES[half]
    ]


def buffers(shapes):
    return [pltpu.VMEM(*shape) for shape in shapes]


def start_all(copies, pending):
    for copy in copies:
        copy.start()
    pending.extend(copies)
    return copies


def plus(*refs):
    value = refs[0][...].astype(F32)
    for ref in refs[1:]:
        value = value + ref[...].astype(F32)
    return value.astype(BF)


def reduce_first(plane, half, segments, held, result, pending, late=None, staged=False):
    own, got, near_a, near_b, full_a, full_b, first_send, first_recv, first_local = held[:9]
    ring_send, ring_recv = held[9:]
    near, full = (near_a, near_b), (full_a, full_b)

    def keep(i, segment):
        ref, start, size, to = segment
        return pltpu.make_async_copy(
            ref.at[pl.ds(start, size), :], own.at[pl.ds(to, size), :], first_local.at[i]
        )

    def give(i, segment):
        ref, start, size, to = segment
        return remote(
            ref.at[pl.ds(start, size), :], got.at[pl.ds(to, size), :],
            first_send.at[i], first_recv.at[i], plane.partner,
        )

    for mine in (1, 0):

        @pl.when(plane.core == 1 - mine)
        def _():
            for i, segment in enumerate(segments[mine]):
                give(i, segment).start()

        @pl.when(plane.core == mine)
        def _():
            for i, segment in enumerate(segments[mine]):
                keep(i, segment).start()

        if staged and mine:
            yield
    yield
    if late is not None:
        late()
    for mine in range(2):

        @pl.when(plane.core == mine)
        def _():
            for i, segment in enumerate(segments[mine]):
                keep(i, segment).wait()
                give(i, segment).wait_recv()
            for i, segment in enumerate(segments[1 - mine]):
                give(i, segment).wait_send()

    part = half // 16

    def add_rows(i, carry):
        span = rows(i * part, part)
        own[span, :] = (own[span, :].astype(F32) + got[span, :].astype(F32)).astype(BF)
        return carry

    lax.fori_loop(0, 16, add_rows, 0)

    def chunk(side, k, piece=None):
        first, count, columns = SIDES[half][side]
        size = count // 4
        start = first + plane.place(side, k) * size
        if piece is not None:
            size = size // 2
            start = start + piece * size
        return own.at[rows(start, size), columns]

    def to(side, direction, stage, src, dst):
        sems = ring_send.at[side, stage, direction], ring_recv.at[side, stage, direction]
        there = plane.device(side, plane.place(side, 3 if direction else 1))
        return remote(src, dst, *sems, there)

    def both(stage, src, dst):
        return [
            to(side, direction, stage, src(side, direction), dst(side, direction))
            for direction in range(2)
            for side in range(2)
        ]

    farthest = start_all(
        both(0, lambda s, d: chunk(s, 2, d), lambda s, d: near[s].at[d]), pending
    )
    yield
    nearest = both(1, lambda s, d: chunk(s, 3 if d else 1), lambda s, d: full[s].at[d])
    for copy, onward, (direction, side) in zip(
        farthest, nearest, ((d, s) for d in range(2) for s in range(2))
    ):
        copy.wait_recv()
        passing = chunk(side, 3 if direction else 1, direction)
        passing[...] = plus(passing, near[side].at[direction])
        start_all([onward], pending)
    yield
    for copy in nearest:
        copy.wait_recv()
    for side in range(2):
        result[side][...] = plus(chunk(side, 0), full[side].at[0], full[side].at[1])


def reduce_first_scratch(half, segments):
    dma = pltpu.SemaphoreType.DMA
    return (
        [pltpu.VMEM((half, D), BF), pltpu.VMEM((half, D), BF)]
        + buffers(side_shapes(half, 8, (2,)) + side_shapes(half, 4, (2,)))
        + [dma((segments,)), dma((segments,)), dma((segments,)), dma((2, 2, 2)), dma((2, 2, 2))]
    )


def reduce_second(plane, half, partial, held, result, pending):
    arrived, (ring_send, ring_recv) = held[:2], held[2:]

    def piece(side, k):
        size = SIDES[half][side][1] // 16
        return partial[side].at[rows(plane.place(1 - side, k) * size, size), :]

    started = []
    for k in (2, 1, 3):
        for side in range(2):
            started.append(
                remote(
                    piece(side, k), arrived[side].at[k - 1],
                    ring_send.at[side, k - 1], ring_recv.at[side, k - 1],
                    plane.device(1 - side, plane.place(1 - side, k)),
                )
            )
    start_all(started, pending)
    yield
    for copy in started:
        copy.wait_recv()
    for side in range(2):
        result[side][...] = plus(piece(side, 0), *(arrived[side].at[k] for k in range(3)))


def reduce_second_scratch(half):
    dma = pltpu.SemaphoreType.DMA
    return buffers(side_shapes(half, 16, (3,))) + [dma((2, 3)), dma((2, 3))]


def spread_steps(plane, half, reduced, mine, theirs, sems, pending):
    part_send, part_recv, ring_send, ring_recv, pair_send, pair_recv = sems

    def piece(side, k):
        first, count, columns = SIDES[half][side]
        start = first + plane.place(side) * (count // 4) + plane.place(1 - side, k) * (count // 16)
        return mine.at[rows(start, count // 16), columns]

    def band(ref, side, k, piece=None):
        first, count, columns = SIDES[half][side]
        size = count // 4
        start = first + plane.place(side, k) * size
        if piece is not None:
            size = size // 2
            start = start + piece * size
        return ref.at[rows(start, size), columns]

    def to(side, direction, stage, k, piece=None):
        there = plane.device(side, plane.place(side, 3 if direction else 1))
        here = band(mine, side, k, piece)
        sems = ring_send.at[side, stage, direction], ring_recv.at[side, stage, direction]
        return remote(here, here, *sems, there)

    def pair(side, k):
        return remote(
            band(mine, side, k), band(theirs, side, k),
            pair_send.at[side, k], pair_recv.at[side, k], plane.partner,
        )

    started = []
    for side in range(2):
        piece(side, 0)[...] = reduced[side][...]
    for k in (2, 1, 3):
        for side in range(2):
            started.append(
                remote(
                    reduced[side], piece(side, 0),
                    part_send.at[side, k - 1], part_recv.at[side, k - 1],
                    plane.device(1 - side, plane.place(1 - side, k)),
                )
            )
    start_all(started, pending)
    yield
    for k in range(1, 4):
        for side in range(2):
            there = plane.place(1 - side, 4 - k)
            remote(
                reduced[side], piece(side, 4 - k),
                part_send.at[side, k - 1], part_recv.at[side, k - 1],
                plane.device(1 - side, there),
            ).wait_recv()
    for side in range(2):
        start_all([to(side, 0, 0, 0), to(side, 1, 0, 0)], pending)
    start_all([pair(0, 0), pair(1, 0)], pending)
    yield
    for direction in range(2):
        came = 1 if direction else 3
        for side in range(2):
            to(side, direction, 0, came).wait_recv()
            start_all([to(side, direction, 1, came, direction), pair(side, came)], pending)
    yield
    for direction in range(2):
        for side in range(2):
            to(side, direction, 1, 2, direction).wait_recv()
    start_all([pair(0, 2), pair(1, 2)], pending)
    yield
    for k in range(4):
        for side in range(2):
            pair(side, k).wait_recv()


def spread_scratch():
    dma = pltpu.SemaphoreType.DMA
    return [
        dma((2, 3)), dma((2, 3)), dma((2, 2, 2)), dma((2, 2, 2)), dma((2, 4)), dma((2, 4)),
    ]


def take_turns(*generators):
    waiting = list(generators)
    while waiting:
        for generator in list(waiting):
            try:
                next(generator)
            except StopIteration:
                waiting.remove(generator)


def comm_call(body, collective_id, outs, args, specs, out_specs, scratch):
    return pl.pallas_call(
        body,
        out_shape=tuple(jax.ShapeDtypeStruct(shape, dtype) for shape, dtype in outs),
        in_specs=specs,
        out_specs=tuple(out_specs),
        scratch_shapes=scratch,
        compiler_params=pltpu.CompilerParams(
            collective_id=collective_id,
            has_side_effects=True,
            vmem_limit_bytes=LIMITS[collective_id - 1] * MIB,
        ),
    )(*args)


def exchange_steps(to_workers, source, dst, sems, pending, prepare=None):
    send_sem, recv_sem, local_sem = sems
    me = lax.axis_index("ctx")
    works = me < WORK

    def copy(k, peer, slot):
        return remote(
            source(k, peer), dst.at[slot], send_sem.at[k], recv_sem.at[k], {"ctx": peer}
        )

    own = pltpu.make_async_copy(source(0, me), dst.at[me], local_sem)
    for k in EXCHANGE_ORDER:
        peer = moved(me, k, 1)
        if prepare is not None:
            prepare(k, peer)
        if k:
            pl.when(peer < WORK if to_workers else works)(copy(k, peer, me).start)
        else:
            pl.when(works)(own.start)
    yield
    pl.when(works)(own.wait)
    for k in EXCHANGE_ORDER[:-1]:
        peer = moved(me, k, -1)
        pl.when(works if to_workers else peer < WORK)(copy(k, peer, peer).wait_recv)
    yield
    for k in EXCHANGE_ORDER[:-1]:
        peer = moved(me, k, 1)
        pl.when(peer < WORK if to_workers else works)(copy(k, peer, me).wait_send)


EXCHANGE_ORDER = (10, 4, 1, 12, 3, 6, 14, 9, 11, 2, 8, 5, 15, 7, 13, 0)


def moved(me, k, sign):
    x, y = me // 4, lax.rem(me, 4)
    return lax.rem(x + 4 + sign * (k // 4), 4) * 4 + lax.rem(y + 4 + sign * (k % 4), 4)


def ctx_peers():
    me = lax.axis_index("ctx")
    return [{"ctx": lax.rem(me + k, N_CTX)} for k in range(1, N_CTX)]


def exchange_scratch():
    dma = pltpu.SemaphoreType.DMA
    return [dma((N_CTX,)), dma((N_CTX,)), dma]


def finish_sends(pending):
    for copy in pending:
        copy.wait_send()


def order_of(block_place):
    order = []
    for p in range(N_CTX):
        owner = jnp.int32(0)
        for i in range(1, N_CTX):
            owner = jnp.where(block_place[i] == p, i, owner)
        order.append(owner)
    return order


def project_body(tok_t, cot_t, w_t, *rest):
    rows_in, (pieces, normed_out, tok, cot, vecs, send, *sems) = rest[:8], rest[8:]
    greeted = greet(ctx_peers())
    pending = []
    tok[...] = tok_t[...].T
    for i, ref in enumerate(rows_in):
        vecs[i : i + 1, : ref.shape[0]] = ref[...].astype(F32).reshape(1, ref.shape[0])
    normal, _ = normalize(tok[...].astype(F32))
    normed = (normal * vecs[0:1, :] + vecs[1:2, :]).astype(BF)
    normed_out[...] = normed
    projected = dot_nt(normed, w_t[...])
    upper = lax.broadcasted_iota(jnp.int32, (1, 2 * HD), 1) >= HD
    for s in range(HSLOT):
        base = 3 * HD * s
        bias = vecs[7:8, 2 * HD * s : 2 * HD * (s + 1)]
        pair = projected[:, base + HD : base + 3 * HD] + jnp.where(upper, bias, 0.0)
        pair = pair.astype(BF)
        queries = (projected[:, base : base + HD] + bias[:, :HD]).astype(BF)
        queries = queries * jnp.asarray(HD**-0.5, BF)
        for j in range(SPLIT):
            send[SPLIT * s + j, :TOK, :] = pair
            send[SPLIT * s + j, TOK:, :] = pack(queries[STEP * j : STEP * j + SHARE])
    greeted()
    steps = exchange_steps(True, lambda k, peer: send.at[peer], pieces, sems, pending)
    next(steps)
    cot[...] = cot_t[...].T
    take_turns(steps)
    finish_sends(pending)


def attend_body(
    block_place, head_count, pieces, w_out,
    keys, keys_t, queries, out_t, lse, attended, attn,
    packed, stage, arrived, part, *scratch,
):
    greeted = greet(ctx_peers() + tp_peers())
    pending = []
    order = order_of(block_place)
    ctx = lax.axis_index("ctx")
    row_offset = lax.rem(ctx, SPLIT) * STEP
    live = (ctx // SPLIT < head_count[lax.axis_index("tp")]).astype(F32)
    for p in range(N_CTX):
        owner = order[p]
        pair = pieces[owner, :TOK, :]
        keys[p * TOK : (p + 1) * TOK, :] = pair
        keys_t[:, p * TOK : (p + 1) * TOK] = pair.T
        share = unpack(pieces[owner, TOK:, :])
        queries[p * SHARE : (p + 1) * SHARE, :] = jnp.concatenate(
            [share, jnp.zeros((SHARE, HD), BF)], axis=1
        )
    for first in range(0, ROWS, GROUP):
        low, high = group_keys(first)
        block = queries[first : first + GROUP, :]
        edge = jnp.where(
            allowed_keys(first, row_offset), dot_nt(keys[low:high, :], block), NEGATIVE
        )
        top = jnp.max(edge, axis=0, keepdims=True)
        if low:
            body = dot_nt(keys[:low, :], block)
            top = jnp.maximum(top, jnp.max(body, axis=0, keepdims=True))
        weights = jnp.exp(edge - top)
        total = jnp.sum(weights, axis=0, keepdims=True)
        mixed = dot(keys_t[HD:, low:high], weights.astype(BF))
        if low:
            weights = jnp.exp(body - top)
            total = total + jnp.sum(weights, axis=0, keepdims=True)
            mixed = mixed + dot(keys_t[HD:, :low], weights.astype(BF))
        out_t[:, first : first + GROUP] = mixed / total * live
        lse[:, first : first + GROUP] = top + jnp.log(total)
    for p in range(N_CTX):
        packed[p] = pack(out_t[:, p * SHARE : (p + 1) * SHARE].T.astype(BF))
    greeted()

    def prepare(k, peer):
        stage[k] = packed[block_place[peer]]

    steps = exchange_steps(
        False, lambda k, peer: stage.at[k], arrived, scratch[:3], pending, prepare
    )
    next(steps)
    next(steps)
    heads = []
    for s in range(HSLOT):
        heads.append(join_shares([unpack(arrived[SPLIT * s + j]) for j in range(SPLIT)]))
    joined = jnp.concatenate(heads, axis=1)
    attended[...] = joined
    part[...] = dot(joined, w_out[...]).astype(BF)
    take_turns(tp_steps([part], [attn], *scratch[3:], pending))
    take_turns(steps)
    finish_sends(pending)


def mlp_body(
    tok, cot, attn, vecs, w_up, w_down,
    mlp_part, gn2, sum_a, sum_b, rest_up, rest_down, sums,
    gn2_part, gw_up, gw_down, *scratch,
):
    plane = Plane()
    greeted = greet(plane.peers() + tp_peers())
    pending = []
    residual = tok[...].astype(F32) + (attn[...].astype(F32) + vecs[4:5, :])
    normal, _ = normalize(residual)
    normed = (normal * vecs[2:3, :] + vecs[3:4, :]).astype(BF)
    hidden = dot(normed, w_up[...]) + vecs[6:7, :]
    cdf = 0.5 * (1.0 + lax.erf(hidden * (0.5**0.5)))
    activated = (hidden * cdf).astype(BF)
    cot_low = cot[...]
    gw_down[...] = dot_tn(activated, cot_low).astype(BF)
    greeted()
    segments = (((gw_up, 0, FIRST, 0),), ((gw_down, 0, FIRST, 0),))
    weights = reduce_first(
        plane, FIRST, segments, scratch[3:], (sum_a, sum_b), pending, staged=True
    )
    next(weights)
    grad_act = dot_nt(cot_low, w_down[...])
    slope = cdf + hidden * jnp.exp(-0.5 * hidden * hidden) * 0.3989422804014327
    grad_hidden = (grad_act * slope).astype(BF)
    gn2_part[...] = dot_nt(grad_hidden, w_up[...]).astype(BF)
    total = tp_steps([gn2_part], [gn2], *scratch[:3], pending)
    next(total)
    gw_up[...] = dot_tn(normed, grad_hidden).astype(BF)
    next(weights)
    mlp_part[...] = dot(activated, w_down[...]).astype(BF)
    rest_up[...] = gw_up[FIRST:, :]
    rest_down[...] = gw_down[FIRST:, :]
    sums[...] = jnp.zeros_like(sums)
    sums[0:1, :] = row_sum(grad_hidden.astype(F32))
    sums[1:2, :] = row_sum(cot_low.astype(F32))
    take_turns(weights, total)
    finish_sends(pending)


def attend_back_body(
    block_place, head_count, tok, cot, attn, gn2, vecs, w_out, attended,
    keys, keys_t, queries, out_t, lse, sum_a, sum_b, mlp_part,
    grad_res, gw_out, sums, mine, theirs, mlp, pieces4,
    send3, pieces3, red_a, red_b, grads, grad_q, dots, acc, packed, stage, *scratch,
):
    plane = Plane()
    greeted = greet(ctx_peers() + tp_peers() + [plane.partner])
    pending = []
    scatter_sems, gather_sems, tp, second, ring = (
        scratch[:3], scratch[3:6], scratch[6:9], scratch[9:13], scratch[13:],
    )
    order = order_of(block_place)
    greeted()
    reduce = reduce_second(plane, FIRST, (sum_a, sum_b), second, (red_a, red_b), pending)
    total = tp_steps([mlp_part], [mlp], *tp, pending)
    next(reduce)
    next(total)

    residual = tok[...].astype(F32) + (attn[...].astype(F32) + vecs[4:5, :])
    normal, inverse = normalize(residual)
    grad_norm = gn2[...].astype(F32)
    grad = cot[...].astype(F32) + norm_backward(grad_norm, normal, inverse, vecs[2:3, :])
    grad_low = grad.astype(BF)
    live_lanes = head_count[lax.axis_index("tp")] * HD
    lane = lax.broadcasted_iota(jnp.int32, (1, HSLOT * HD), 1)
    live = (lane < live_lanes).astype(F32)
    grad_att = (dot_nt(grad_low, w_out[...]) * live).astype(BF)
    for s in range(HSLOT):
        head = grad_att[:, HD * s : HD * (s + 1)]
        for j in range(SPLIT):
            share = head[STEP * j : STEP * j + SHARE]
            if j:
                share = jnp.concatenate([jnp.zeros((16, HD), BF), share[16:]], axis=0)
            send3[SPLIT * s + j] = pack(share)
    scatter = exchange_steps(
        True, lambda k, peer: send3.at[peer], pieces3, scatter_sems, pending
    )
    next(scatter)
    take_turns(reduce)
    spread = spread_steps(plane, FIRST, (red_a, red_b), mine, theirs, ring, pending)
    next(spread)
    grad_res[...] = grad
    gw_out[...] = dot_tn(attended[...], grad_low).astype(BF)
    sums[...] = jnp.zeros_like(sums)
    sums[0:1, :] = row_sum(grad_norm * normal)
    sums[1:2, :] = row_sum(grad_norm)
    sums[2:3, :] = row_sum(grad_low.astype(F32))
    acc[...] = jnp.zeros_like(acc)
    next(scatter)
    next(spread)
    next(total)

    row_offset = lax.rem(lax.axis_index("ctx"), SPLIT) * STEP
    for p in range(N_CTX):
        share = unpack(pieces3[order[p]])
        grads[p * SHARE : (p + 1) * SHARE, :] = jnp.concatenate(
            [jnp.zeros((SHARE, HD), BF), share], axis=1
        )
    for first in range(0, ROWS, GROUP):
        turned = grads[first : first + GROUP, :].astype(F32).T
        dots[:, first : first + GROUP] = jnp.sum(
            turned[HD:, :] * out_t[:, first : first + GROUP], axis=0, keepdims=True
        )
    for first in range(0, ROWS, GROUP):
        low, high = group_keys(first)
        span = slice(first, first + GROUP)
        both = jnp.concatenate([queries[span, :], grads[span, :]], axis=0)
        grad_block = jnp.zeros((HD, GROUP), F32)
        for start, stop in ((0, low), (low, high)):
            if start == stop:
                continue
            scores = dot_nt(keys[start:stop, :], both)
            weights = jnp.exp(scores[:, :GROUP] - lse[:, span])
            if start == low:
                weights = jnp.where(allowed_keys(first, row_offset), weights, 0.0)
            grad_scores = (weights * (scores[:, GROUP:] - dots[:, span])).astype(BF)
            pair = jnp.concatenate([grad_scores, weights.astype(BF)], axis=1)
            blocks = slice(start // TOK, stop // TOK)
            acc[blocks] += dot(pair, both).reshape(-1, TOK, 2 * HD)
            grad_block = grad_block + dot(keys_t[:HD, start:stop], grad_scores)
        grad_q[:, span] = grad_block * (HD**-0.5)
        if first == 8 * GROUP:
            next(spread)
    for p in range(N_CTX):
        packed[p] = pack(grad_q[:, p * SHARE : (p + 1) * SHARE].T.astype(BF))

    def prepare(k, peer):
        place = block_place[peer]
        stage[k, :TOK, :] = acc[place].astype(BF)
        stage[k, TOK:, :] = packed[place]

    gather = exchange_steps(
        False, lambda k, peer: stage.at[k], pieces4, gather_sems, pending, prepare
    )
    take_turns(gather, spread, total, scatter)
    finish_sends(pending)


VEC_AT = 2 * REST + HSLOT * HD + COLS


def project_back_body(
    pieces, tok, normed, w_t, sums_mid, sums_mlp, up, down, w_out,
    gn1, mine, theirs,
    gw_qkv_t, part, vec, vec_parts, vec_low, vec_got, vec_send, vec_recv,
    sum_a, sum_b, red_a, red_b, *scratch,
):
    plane = Plane()
    greeted = greet(plane.peers() + tp_peers())
    pending = []
    tp, weights, second, ring = scratch[:3], scratch[3:14], scratch[14:18], scratch[18:]
    own, got = weights[:2]
    me = lax.axis_index("tp")

    @pl.when(plane.core == 1)
    def _():
        own[SECOND - 128 :, :] = jnp.zeros((128, D), BF)
        got[SECOND - 128 :, :] = jnp.zeros((128, D), BF)

    columns, biases = [], []
    for s in range(HSLOT):
        shares = [pieces[SPLIT * s + j] for j in range(SPLIT)]
        pair = shares[0][:TOK].astype(F32)
        for piece in shares[1:]:
            pair = pair + piece[:TOK].astype(F32)
        pair = pair.astype(BF)
        queries = join_shares([unpack(piece[TOK:]) for piece in shares])
        columns += [queries, pair]
        biases += [row_sum(queries.astype(F32)), row_sum(pair.astype(F32))[:, HD:]]
    grads = jnp.concatenate(columns, axis=1)
    gw_qkv_t[...] = dot_tn(grads, normed[...]).astype(BF)
    greeted()

    def add_vectors():
        for k in range(1, N_TP):
            there = vec_parts.at[lax.rem(me + N_TP - k, N_TP)]
            remote(there, there, vec_send.at[k], vec_recv.at[k], plane.partner).wait_recv()
        over_tp = vec_parts[0].astype(F32)
        for t in range(1, N_TP):
            over_tp = over_tp + vec_parts[t].astype(F32)
        row = lax.broadcasted_iota(jnp.int32, (16, 1), 0)
        vec_low[...] = jnp.where(row < 2, over_tp, vec[...]).astype(BF)
        copy = remote(vec_low, vec_got, vec_send.at[0], vec_recv.at[0], plane.partner)
        start_all([copy], pending)
        copy.wait_recv()

        @pl.when(plane.core == 1)
        def _():
            own[SECOND - 128 : SECOND - 112, :] = vec_low[...]
            got[SECOND - 128 : SECOND - 112, :] = vec_got[...]

    segments = (
        (
            (up, 0, REST, 0),
            (down, 0, REST, REST),
            (w_out, 0, HSLOT * HD, 2 * REST),
            (gw_qkv_t, 0, 320, 448),
        ),
        ((gw_qkv_t, 320, 640, 0),),
    )

    def all_weights():
        yield from reduce_first(
            plane, SECOND, segments, weights, (sum_a, sum_b), pending, late=add_vectors
        )
        yield from reduce_second(plane, SECOND, (sum_a, sum_b), second, (red_a, red_b), pending)
        yield from spread_steps(plane, SECOND, (red_a, red_b), mine, theirs, ring, pending)

    steps = all_weights()
    next(steps)
    product = dot(grads, w_t[...])
    part[...] = product.astype(BF)
    total = tp_steps([part], [gn1], *tp, pending)
    normal, _ = normalize(tok[...].astype(F32))
    vec[0:1, :] = row_sum(product * normal)
    vec[1:2, :] = row_sum(product)
    vec[2:5, :] = sums_mid[0:3, :]
    vec[5:7, :] = sums_mlp[0:2, :]
    vec[7:8, : HSLOT * 2 * HD] = jnp.concatenate(biases, axis=1)
    vec[7:8, HSLOT * 2 * HD :] = jnp.zeros((1, D - HSLOT * 2 * HD), F32)
    vec[8:, :] = jnp.zeros((8, D), F32)
    vec_parts[me] = vec[...].astype(BF)
    for k in range(1, N_TP):
        copy = remote(
            vec_parts.at[me], vec_parts.at[me], vec_send.at[k], vec_recv.at[k],
            {"tp": lax.rem(me + k, N_TP)},
        )
        start_all([copy], pending)
    next(total)
    take_turns(steps, total)
    finish_sends(pending)


def finish_body(
    tok, attn, mlp, gn1, grad_res, vecs, mine1, theirs1, mine2, theirs2,
    output_t, grad_tok_t, up_out, down_out, w_out_out, w_qkv_out, *rest,
):
    vec_outs, (up, down, w_out, w_qkv, out_sem) = rest[:8], rest[8:]
    top = 2 * REST + HSLOT * HD
    core = lax.axis_index("seq")
    copies = []

    def by_core(action):
        pl.when(core == 0)(lambda: action(mine1, theirs1, mine2, theirs2))
        pl.when(core == 1)(lambda: action(theirs1, mine1, theirs2, mine2))

    def write(src, dst):
        copies.append(pltpu.make_async_copy(src, dst, out_sem.at[len(copies)]))
        copies[-1].start()

    def cast_up(low1, high1, low2, high2):
        up[:FIRST, :] = low1[...].astype(F32)
        up[FIRST:, :] = low2[:REST, :].astype(F32)

    def cast_down(low1, high1, low2, high2):
        down[:FIRST, :] = high1[...].astype(F32)
        down[FIRST:, :] = low2[REST : 2 * REST, :].astype(F32)

    def cast_qkv(low1, high1, low2, high2):
        w_qkv[: SECOND - top, :] = low2[top:, :].astype(F32)
        w_qkv[SECOND - top :, :] = high2[: VEC_AT - SECOND, :].astype(F32)

    def cast_rest(low1, high1, low2, high2):
        w_out[...] = low2[2 * REST : top, :].astype(F32)
        vectors = high2[VEC_AT - SECOND : VEC_AT - SECOND + 16, :].astype(F32)
        for i, ref in enumerate(vec_outs):
            ref[...] = vectors[i, : ref.shape[0]]

    by_core(cast_up)
    write(up, up_out)
    by_core(cast_down)
    write(down, down_out)
    by_core(cast_qkv)
    write(w_qkv, w_qkv_out)
    by_core(cast_rest)
    write(w_out, w_out_out)
    inputs = tok[...].astype(F32)
    residual = inputs + (attn[...].astype(F32) + vecs[4:5, :])
    output_t[...] = (residual + (mlp[...].astype(F32) + vecs[5:6, :])).astype(BF).T
    normal, inverse = normalize(inputs)
    grad_norm = gn1[...].astype(F32)
    grad = grad_res[...] + norm_backward(grad_norm, normal, inverse, vecs[0:1, :])
    grad_tok_t[...] = grad.T
    for copy in copies:
        copy.wait()


def on_device(
    tokens, cotangent, block_place, head_count, ln1_gain, ln1_bias, w_qkv, b_qv, w_out, b_out,
    ln2_gain, ln2_bias, w_up, b_up, w_down, b_down,
):
    w_qkv_t = w_qkv.T
    dma = pltpu.SemaphoreType.DMA
    row_shape, piece_shape, half_shape = (
        ((TOK, D), BF), ((N_CTX, PIECE, 2 * HD), BF), ((N_CTX, HALF, 2 * HD), BF),
    )

    def buffer(shaped):
        return pltpu.VMEM(*shaped)

    pieces1, normed1, tok, cot, vecs = comm_call(
        project_body,
        1,
        [piece_shape, row_shape, row_shape, row_shape, ((8, D), F32)],
        [tokens[0].T, cotangent[0].T, w_qkv_t]
        + [ln1_gain, ln1_bias, ln2_gain, ln2_bias, b_out, b_down, b_up, b_qv],
        [VM] * 11,
        [VM] * 5,
        [buffer(piece_shape)] + exchange_scratch(),
    )
    keys, keys_t, queries, out_t, lse, attended, attn = comm_call(
        attend_body,
        2,
        [
            ((N_CTX * TOK, 2 * HD), BF),
            ((2 * HD, N_CTX * TOK), BF),
            ((ROWS, 2 * HD), BF),
            ((HD, ROWS), F32),
            ((1, ROWS), F32),
            ((TOK, HSLOT * HD), BF),
            row_shape,
        ],
        [block_place, head_count, pieces1, w_out],
        [SM, SM, VM, VM],
        [VM] * 7,
        [buffer(half_shape), buffer(half_shape), buffer(half_shape), buffer(row_shape)]
        + exchange_scratch()
        + tp_scratch(1),
    )
    mlp_part, gn2, sum1_a, sum1_b, rest_up, rest_down, sums_mlp = comm_call(
        mlp_body,
        3,
        [row_shape, row_shape]
        + side_shapes(FIRST, 4)
        + [((REST, D), BF), ((REST, D), BF), ((8, D), F32)],
        [tok, cot, attn, vecs, w_up, w_down],
        [VM] * 6,
        [VM] * 7,
        [buffer(row_shape), pltpu.VMEM((D, D), BF), pltpu.VMEM((D, D), BF)]
        + tp_scratch(1)
        + reduce_first_scratch(FIRST, 1),
    )
    grad_res, gw_out, sums_mid, mine1, theirs1, mlp, pieces4 = comm_call(
        attend_back_body,
        4,
        [
            ((TOK, D), F32),
            ((HSLOT * HD, D), BF),
            ((8, D), F32),
            ((FIRST, D), BF),
            ((FIRST, D), BF),
            row_shape,
            piece_shape,
        ],
        [
            block_place, head_count, tok, cot, attn, gn2, vecs, w_out, attended,
            keys, keys_t, queries, out_t, lse, sum1_a, sum1_b, mlp_part,
        ],
        [SM, SM] + [VM] * 15,
        [VM] * 7,
        [buffer(half_shape), buffer(half_shape)]
        + buffers(side_shapes(FIRST, 16))
        + [
            pltpu.VMEM((ROWS, 2 * HD), BF),
            pltpu.VMEM((HD, ROWS), F32),
            pltpu.VMEM((1, ROWS), F32),
            pltpu.VMEM((N_CTX, TOK, 2 * HD), F32),
            buffer(half_shape),
            buffer(piece_shape),
        ]
        + exchange_scratch()
        + exchange_scratch()
        + tp_scratch(1)
        + reduce_second_scratch(FIRST)
        + spread_scratch(),
    )
    gn1, mine2, theirs2 = comm_call(
        project_back_body,
        5,
        [row_shape, ((SECOND, D), BF), ((SECOND, D), BF)],
        [pieces4, tok, normed1, w_qkv_t, sums_mid, sums_mlp, rest_up, rest_down, gw_out],
        [VM] * 9,
        [VM] * 3,
        [
            pltpu.VMEM((COLS, D), BF),
            buffer(row_shape),
            pltpu.VMEM((16, D), F32),
            pltpu.VMEM((N_TP, 16, D), BF),
            pltpu.VMEM((16, D), BF),
            pltpu.VMEM((16, D), BF),
            dma((N_TP,)),
            dma((N_TP,)),
        ]
        + buffers(side_shapes(SECOND, 4) + side_shapes(SECOND, 16))
        + tp_scratch(1)
        + reduce_first_scratch(SECOND, 4)
        + reduce_second_scratch(SECOND)
        + spread_scratch(),
    )
    output_t, grad_tok_t, g_up, g_down, g_out, g_qkv_t, *g = local_call(
        finish_body,
        5,
        [
            ((D, TOK), BF),
            ((D, TOK), F32),
            ((D, D), F32),
            ((D, D), F32),
            ((HSLOT * HD, D), F32),
            ((COLS, D), F32),
        ]
        + [((D,), F32)] * 7
        + [((HSLOT * 2 * HD,), F32)],
        [tok, attn, mlp, gn1, grad_res, vecs, mine1, theirs1, mine2, theirs2],
        out_specs=[VM, VM, HB, HB, HB, HB] + [VM] * 8,
        scratch=[
            pltpu.VMEM((D, D), F32),
            pltpu.VMEM((D, D), F32),
            pltpu.VMEM((HSLOT * HD, D), F32),
            pltpu.VMEM((COLS, D), F32),
            dma((4,)),
        ],
    )
    return (
        output_t.T[None],
        grad_tok_t.T[None],
        g[0],
        g[1],
        g_qkv_t.T,
        g[7],
        g_out,
        g[4],
        g[2],
        g[3],
        g_up,
        g[5],
        g_down,
        g[6],
    )


def solution(mesh):
    in_specs = (
        P("seq", "ctx", None), P("seq", "ctx", None), P(), P(), P(), P(), P(None, "tp"), P("tp"),
        P("tp", None), P(), P(), P(), P(None, "tp"), P("tp"), P("tp", None), P(),
    )
    out_specs = (
        P("seq", "ctx", None), P("seq", "ctx", None), P(), P(), P(None, "tp"), P("tp"),
        P("tp", None), P(), P(), P(), P(None, "tp"), P("tp"), P("tp", None), P(),
    )
    return jax.shard_map(
        on_device, mesh=mesh, in_specs=in_specs, out_specs=out_specs, check_vma=False
    )
```

```python
import functools

import jax
import jax.numpy as jnp
from jax import lax
from jax.experimental import pallas as pl
from jax.experimental.pallas import tpu as pltpu
from jax.sharding import PartitionSpec as P

HD = 64
HSLOT = 5
D = 1088
TOK = 256
N_CTX = 16
N_TP = 4
SPLIT = 3
STEP = 80
SHARE = 96
HALF = SHARE // 2
PIECE = TOK + HALF
ROWS = N_CTX * SHARE
GROUP = 128
WORK = HSLOT * SPLIT
COLS = HSLOT * 3 * HD
FIRST = 1024
REST = D - FIRST
SECOND = 256
THIRD = 512
VEC_AT = COLS - THIRD
OUT_LOW = SECOND - 2 * REST
CUT = 512
EPSILON = 1e-05
NEGATIVE = -1e30
BF = jnp.bfloat16
F32 = jnp.float32
MESH = pl.DeviceIdType.MESH
MIB = 2**20
FLOPS = (16, 24, 60, 48)
LIMITS = (56, 20, 30, 20, 24)

VM = pl.BlockSpec(memory_space=pltpu.VMEM)
SM = pl.BlockSpec(memory_space=pltpu.SMEM)
HB = pl.BlockSpec(memory_space=pl.ANY)
OUTSIDE = pl.BlockSpec(memory_space=pltpu.HBM)


def dot(a, b):
    return jnp.dot(a, b, preferred_element_type=F32)


def dot_nt(a, b):
    return lax.dot_general(a, b, (((1,), (1,)), ((), ())), preferred_element_type=F32)


def dot_tn(a, b):
    return lax.dot_general(a, b, (((0,), (0,)), ((), ())), preferred_element_type=F32)


def pack(rows):
    return jnp.concatenate([rows[:HALF], rows[HALF:]], axis=1)


def unpack(packed):
    return jnp.concatenate([packed[:, :HD], packed[:, HD:]], axis=0)


def normalize(values):
    centered = values - jnp.mean(values, axis=-1, keepdims=True)
    inverse = lax.rsqrt(jnp.mean(centered * centered, axis=-1, keepdims=True) + EPSILON)
    return centered * inverse, inverse


def norm_backward(grad_out, normal, inverse, gain):
    grad_normal = grad_out * gain
    grad_mean = jnp.mean(grad_normal, axis=-1, keepdims=True)
    grad_along = jnp.mean(grad_normal * normal, axis=-1, keepdims=True)
    return inverse * (grad_normal - grad_mean - normal * grad_along)


def row_sum(values):
    return jnp.sum(values, axis=0, keepdims=True)


def local_call(body, index, outs, args, specs=None, scratch=(), out_specs=None):
    moved = sum(a.size * a.dtype.itemsize for a in args)
    return pl.pallas_call(
        body,
        out_shape=tuple(jax.ShapeDtypeStruct(shape, dtype) for shape, dtype in outs),
        in_specs=specs or [VM] * len(args),
        out_specs=tuple(out_specs or [VM] * len(outs)),
        scratch_shapes=list(scratch),
        compiler_params=pltpu.CompilerParams(vmem_limit_bytes=LIMITS[index] * MIB),
        cost_estimate=pl.CostEstimate(flops=0, bytes_accessed=moved, transcendentals=0),
    )(*args)


def join_shares(shares):
    return jnp.concatenate([shares[0], shares[1][16:], shares[2][16:]], axis=0)


def group_keys(first):
    low = first // SHARE
    high = (first + GROUP - 1) // SHARE
    return low * TOK, (high + 1) * TOK


def allowed_keys(first, row_offset):
    low, high = group_keys(first)
    row = first + lax.broadcasted_iota(jnp.int32, (1, GROUP), 1)
    place = jnp.full((1, GROUP), low // TOK, jnp.int32)
    for p in range(low // TOK + 1, high // TOK):
        place = place + (row >= p * SHARE).astype(jnp.int32)
    position = place * (TOK - SHARE) + row + row_offset
    key = low + lax.broadcasted_iota(jnp.int32, (high - low, GROUP), 0)
    return key <= position


def greet(peers):
    barrier = pltpu.get_barrier_semaphore()
    for peer in peers:
        pl.semaphore_signal(barrier, inc=1, device_id=peer, device_id_type=MESH)
    return lambda: pl.semaphore_wait(barrier, len(peers))


def remote(src, dst, send, recv, device):
    return pltpu.make_async_remote_copy(
        src_ref=src,
        dst_ref=dst,
        send_sem=send,
        recv_sem=recv,
        device_id=device,
        device_id_type=MESH,
    )


def rows(start, size):
    return pl.ds(pl.multiple_of(start, 16), size)


def tp_steps(parts, totals, held, send_sem, recv_sem, pending):
    me = lax.axis_index("tp")
    share = TOK // N_TP
    size = share // TP_PIECES
    work = [(i, j) for i in range(len(parts)) for j in range(TP_PIECES)]

    def cut(ref, peer, j):
        return ref.at[rows(peer * share + j * size, size), :]

    started = {}
    for i, j in work:
        for k in (2, 1, 3):
            peer = lax.rem(me + k, N_TP)
            started[i, j, k] = remote(
                cut(parts[i], peer, j), held.at[i, k - 1, pl.ds(j * size, size), :],
                send_sem.at[0, i, j, k - 1], recv_sem.at[0, i, j, k - 1], {"tp": peer},
            )
            started[i, j, k].start()
    pending += started.values()
    yield
    for i, j in work:
        for k in range(1, N_TP):
            started[i, j, k].wait_recv()
        own = cut(totals[i], me, j)
        own[...] = plus(
            cut(parts[i], me, j),
            *(held.at[i, k, pl.ds(j * size, size), :] for k in range(N_TP - 1)),
        )
        for k in (2, 1, 3):
            copy = remote(
                own, own, send_sem.at[1, i, j, k - 1], recv_sem.at[1, i, j, k - 1],
                {"tp": lax.rem(me + k, N_TP)},
            )
            start_all([copy], pending)
    yield
    for i, j in work:
        for k in range(1, N_TP):
            peer = lax.rem(me + N_TP - k, N_TP)
            there = cut(totals[i], peer, j)
            remote(
                there, there, send_sem.at[1, i, j, k - 1], recv_sem.at[1, i, j, k - 1],
                {"tp": peer},
            ).wait_recv()


TP_PIECES = 2


def tp_scratch(count):
    return [
        pltpu.VMEM((count, N_TP - 1, TOK // N_TP, D), BF),
        pltpu.SemaphoreType.DMA((2, count, TP_PIECES, N_TP - 1)),
        pltpu.SemaphoreType.DMA((2, count, TP_PIECES, N_TP - 1)),
    ]


def tp_peers():
    me = lax.axis_index("tp")
    return [{"tp": lax.rem(me + k, N_TP)} for k in range(1, N_TP)]


class Plane:
    def __init__(self):
        ctx = lax.axis_index("ctx")
        self.core = lax.axis_index("seq")
        self.partner = {"seq": 1 - self.core}
        self.x, self.y = ctx // 4, lax.rem(ctx, 4)

    def place(self, axis, k=0):
        return lax.rem((self.x, self.y)[axis] + k, 4)

    def device(self, axis, place):
        return {"ctx": self.x * 4 + place if axis else place * 4 + self.y}

    def peers(self):
        return [self.partner] + [
            self.device(axis, self.place(axis, k)) for axis in range(2) for k in range(1, 4)
        ]


SIDES = {
    FIRST: ((0, FIRST // 2, slice(0, D)), (FIRST // 2, FIRST // 2, slice(0, D))),
    SECOND: ((0, SECOND, slice(0, CUT)), (0, SECOND, slice(CUT, D))),
    THIRD: ((0, THIRD // 2, slice(0, D)), (THIRD // 2, THIRD // 2, slice(0, D))),
}


def side_shapes(half, pieces, lead=()):
    return [
        (lead + (count // pieces, columns.stop - columns.start), BF)
        for _, count, columns in SIDES[half]
    ]


def buffers(shapes):
    return [pltpu.VMEM(*shape) for shape in shapes]


def start_all(copies, pending):
    for copy in copies:
        copy.start()
    pending.extend(copies)
    return copies


def plus(*refs):
    value = refs[0][...].astype(F32)
    for ref in refs[1:]:
        value = value + ref[...].astype(F32)
    return value.astype(BF)


def reduce_first(plane, half, segments, held, result, pending, late=None, staged=False):
    own, got, near_a, near_b, full_a, full_b, first_send, first_recv, first_local = held[:9]
    ring_send, ring_recv = held[9:]
    near, full = (near_a, near_b), (full_a, full_b)

    def keep(i, segment):
        ref, start, size, to = segment
        return pltpu.make_async_copy(
            ref.at[pl.ds(start, size), :], own.at[pl.ds(to, size), :], first_local.at[i]
        )

    def give(i, segment):
        ref, start, size, to = segment
        return remote(
            ref.at[pl.ds(start, size), :], got.at[pl.ds(to, size), :],
            first_send.at[i], first_recv.at[i], plane.partner,
        )

    for mine in (1, 0):

        @pl.when(plane.core == 1 - mine)
        def _():
            for i, segment in enumerate(segments[mine]):
                give(i, segment).start()

        @pl.when(plane.core == mine)
        def _():
            for i, segment in enumerate(segments[mine]):
                keep(i, segment).start()

        if staged and mine:
            yield
    yield
    if late is not None:
        late()
    for mine in range(2):

        @pl.when(plane.core == mine)
        def _():
            for i, segment in enumerate(segments[mine]):
                keep(i, segment).wait()
                give(i, segment).wait_recv()
            for i, segment in enumerate(segments[1 - mine]):
                give(i, segment).wait_send()

    part = half // 16

    def add_rows(i, carry):
        span = rows(i * part, part)
        own[span, :] = (own[span, :].astype(F32) + got[span, :].astype(F32)).astype(BF)
        return carry

    lax.fori_loop(0, 16, add_rows, 0)

    def chunk(side, k, piece=None):
        first, count, columns = SIDES[half][side]
        size = count // 4
        start = first + plane.place(side, k) * size
        if piece is not None:
            size = size // 2
            start = start + piece * size
        return own.at[rows(start, size), columns]

    def to(side, direction, stage, src, dst):
        sems = ring_send.at[side, stage, direction], ring_recv.at[side, stage, direction]
        there = plane.device(side, plane.place(side, 3 if direction else 1))
        return remote(src, dst, *sems, there)

    def both(stage, src, dst):
        return [
            to(side, direction, stage, src(side, direction), dst(side, direction))
            for direction in range(2)
            for side in range(2)
        ]

    farthest = start_all(
        both(0, lambda s, d: chunk(s, 2, d), lambda s, d: near[s].at[d]), pending
    )
    yield
    nearest = both(1, lambda s, d: chunk(s, 3 if d else 1), lambda s, d: full[s].at[d])
    for copy, onward, (direction, side) in zip(
        farthest, nearest, ((d, s) for d in range(2) for s in range(2))
    ):
        copy.wait_recv()
        passing = chunk(side, 3 if direction else 1, direction)
        passing[...] = plus(passing, near[side].at[direction])
        start_all([onward], pending)
    yield
    for copy in nearest:
        copy.wait_recv()
    for side in range(2):
        result[side][...] = plus(chunk(side, 0), full[side].at[0], full[side].at[1])


def reduce_first_scratch(half, segments):
    dma = pltpu.SemaphoreType.DMA
    return (
        [pltpu.VMEM((half, D), BF), pltpu.VMEM((half, D), BF)]
        + buffers(side_shapes(half, 8, (2,)) + side_shapes(half, 4, (2,)))
        + [dma((segments,)), dma((segments,)), dma((segments,)), dma((2, 2, 2)), dma((2, 2, 2))]
    )


def reduce_second(plane, half, partial, held, result, pending):
    arrived, (ring_send, ring_recv) = held[:2], held[2:]

    def piece(side, k):
        size = SIDES[half][side][1] // 16
        return partial[side].at[rows(plane.place(1 - side, k) * size, size), :]

    started = []
    for k in (2, 1, 3):
        for side in range(2):
            started.append(
                remote(
                    piece(side, k), arrived[side].at[k - 1],
                    ring_send.at[side, k - 1], ring_recv.at[side, k - 1],
                    plane.device(1 - side, plane.place(1 - side, k)),
                )
            )
    start_all(started, pending)
    yield
    for copy in started:
        copy.wait_recv()
    for side in range(2):
        result[side][...] = plus(piece(side, 0), *(arrived[side].at[k] for k in range(3)))


def reduce_second_scratch(half):
    dma = pltpu.SemaphoreType.DMA
    return buffers(side_shapes(half, 16, (3,))) + [dma((2, 3)), dma((2, 3))]


def spread_steps(plane, half, reduced, mine, theirs, sems, pending):
    part_send, part_recv, ring_send, ring_recv, pair_send, pair_recv = sems

    def piece(side, k):
        first, count, columns = SIDES[half][side]
        start = first + plane.place(side) * (count // 4) + plane.place(1 - side, k) * (count // 16)
        return mine.at[rows(start, count // 16), columns]

    def band(ref, side, k, piece=None):
        first, count, columns = SIDES[half][side]
        size = count // 4
        start = first + plane.place(side, k) * size
        if piece is not None:
            size = size // 2
            start = start + piece * size
        return ref.at[rows(start, size), columns]

    def to(side, direction, stage, k, piece=None):
        there = plane.device(side, plane.place(side, 3 if direction else 1))
        here = band(mine, side, k, piece)
        sems = ring_send.at[side, stage, direction], ring_recv.at[side, stage, direction]
        return remote(here, here, *sems, there)

    def pair(side, k):
        return remote(
            band(mine, side, k), band(theirs, side, k),
            pair_send.at[side, k], pair_recv.at[side, k], plane.partner,
        )

    started = []
    for side in range(2):
        piece(side, 0)[...] = reduced[side][...]
    for k in (2, 1, 3):
        for side in range(2):
            started.append(
                remote(
                    reduced[side], piece(side, 0),
                    part_send.at[side, k - 1], part_recv.at[side, k - 1],
                    plane.device(1 - side, plane.place(1 - side, k)),
                )
            )
    start_all(started, pending)
    yield
    for k in range(1, 4):
        for side in range(2):
            there = plane.place(1 - side, 4 - k)
            remote(
                reduced[side], piece(side, 4 - k),
                part_send.at[side, k - 1], part_recv.at[side, k - 1],
                plane.device(1 - side, there),
            ).wait_recv()
    for side in range(2):
        start_all([to(side, 0, 0, 0), to(side, 1, 0, 0)], pending)
    start_all([pair(0, 0), pair(1, 0)], pending)
    yield
    for direction in range(2):
        came = 1 if direction else 3
        for side in range(2):
            to(side, direction, 0, came).wait_recv()
            start_all([to(side, direction, 1, came, direction), pair(side, came)], pending)
    yield
    for direction in range(2):
        for side in range(2):
            to(side, direction, 1, 2, direction).wait_recv()
    start_all([pair(0, 2), pair(1, 2)], pending)
    yield
    for k in range(4):
        for side in range(2):
            pair(side, k).wait_recv()


def spread_scratch():
    dma = pltpu.SemaphoreType.DMA
    return [
        dma((2, 3)), dma((2, 3)), dma((2, 2, 2)), dma((2, 2, 2)), dma((2, 4)), dma((2, 4)),
    ]


def take_turns(*generators):
    waiting = list(generators)
    while waiting:
        for generator in list(waiting):
            try:
                next(generator)
            except StopIteration:
                waiting.remove(generator)


def comm_call(body, collective_id, outs, args, specs, out_specs, scratch):
    return pl.pallas_call(
        body,
        out_shape=tuple(jax.ShapeDtypeStruct(shape, dtype) for shape, dtype in outs),
        in_specs=specs,
        out_specs=tuple(out_specs),
        scratch_shapes=scratch,
        cost_estimate=pl.CostEstimate(
            flops=FLOPS[collective_id - 1] * 10**9, bytes_accessed=10**7, transcendentals=0
        ),
        compiler_params=pltpu.CompilerParams(
            collective_id=collective_id,
            has_side_effects=True,
            vmem_limit_bytes=LIMITS[collective_id - 1] * MIB,
        ),
    )(*args)


def exchange_steps(to_workers, source, dst, sems, pending, prepare=None):
    send_sem, recv_sem, local_sem = sems
    me = lax.axis_index("ctx")
    works = me < WORK

    def copy(k, peer, slot):
        return remote(
            source(k, peer), dst.at[slot], send_sem.at[k], recv_sem.at[k], {"ctx": peer}
        )

    own = pltpu.make_async_copy(source(0, me), dst.at[me], local_sem)
    for k in EXCHANGE_ORDER:
        peer = moved(me, k, 1)
        if prepare is not None:
            prepare(k, peer)
        if k:
            pl.when(peer < WORK if to_workers else works)(copy(k, peer, me).start)
        else:
            pl.when(works)(own.start)
    yield
    pl.when(works)(own.wait)
    for k in EXCHANGE_ORDER[:-1]:
        peer = moved(me, k, -1)
        pl.when(works if to_workers else peer < WORK)(copy(k, peer, peer).wait_recv)
    yield
    for k in EXCHANGE_ORDER[:-1]:
        peer = moved(me, k, 1)
        pl.when(peer < WORK if to_workers else works)(copy(k, peer, me).wait_send)


EXCHANGE_ORDER = (10, 4, 1, 12, 3, 6, 14, 9, 11, 2, 8, 5, 15, 7, 13, 0)


def moved(me, k, sign):
    x, y = me // 4, lax.rem(me, 4)
    return lax.rem(x + 4 + sign * (k // 4), 4) * 4 + lax.rem(y + 4 + sign * (k % 4), 4)


def ctx_peers():
    me = lax.axis_index("ctx")
    return [{"ctx": lax.rem(me + k, N_CTX)} for k in range(1, N_CTX)]


def exchange_scratch():
    dma = pltpu.SemaphoreType.DMA
    return [dma((N_CTX,)), dma((N_CTX,)), dma]


def finish_sends(pending):
    for copy in pending:
        copy.wait_send()


def order_of(block_place):
    order = []
    for p in range(N_CTX):
        owner = jnp.int32(0)
        for i in range(1, N_CTX):
            owner = jnp.where(block_place[i] == p, i, owner)
        order.append(owner)
    return order


def project_body(*refs):
    outside, (pieces, normed_out, tok, cot, vecs) = refs[:11], refs[11:16]
    inside, (load_sem, send, *sems) = refs[16:27], refs[27:]
    greeted = greet(ctx_peers())
    pending = []
    loads = []
    for i, (src, dst) in enumerate(zip(outside, inside)):
        loads.append(pltpu.make_async_copy(src, dst, load_sem.at[i]))
        loads[-1].start()
    (tok_t, cot_t, w_t), rows_in = inside[:3], inside[3:]
    loads[0].wait()
    tok[...] = tok_t[...].T
    for load in loads[3:]:
        load.wait()
    for i, ref in enumerate(rows_in):
        vecs[i : i + 1, : ref.shape[0]] = ref[...].astype(F32).reshape(1, ref.shape[0])
    normal, _ = normalize(tok[...].astype(F32))
    normed = (normal * vecs[0:1, :] + vecs[1:2, :]).astype(BF)
    normed_out[...] = normed
    loads[2].wait()
    projected = dot_nt(normed, w_t[...])
    upper = lax.broadcasted_iota(jnp.int32, (1, 2 * HD), 1) >= HD
    for s in range(HSLOT):
        base = 3 * HD * s
        bias = vecs[7:8, 2 * HD * s : 2 * HD * (s + 1)]
        pair = projected[:, base + HD : base + 3 * HD] + jnp.where(upper, bias, 0.0)
        pair = pair.astype(BF)
        queries = (projected[:, base : base + HD] + bias[:, :HD]).astype(BF)
        queries = queries * jnp.asarray(HD**-0.5, BF)
        for j in range(SPLIT):
            send[SPLIT * s + j, :TOK, :] = pair
            send[SPLIT * s + j, TOK:, :] = pack(queries[STEP * j : STEP * j + SHARE])
    greeted()
    steps = exchange_steps(True, lambda k, peer: send.at[peer], pieces, sems, pending)
    next(steps)
    loads[1].wait()
    cot[...] = cot_t[...].T
    take_turns(steps)
    finish_sends(pending)


def attend_body(
    block_place, head_count, pieces, w_out,
    keys, keys_t, queries, out_t, lse, attended, attn,
    packed, stage, arrived, part, *scratch,
):
    greeted = greet(ctx_peers() + tp_peers())
    pending = []
    order = order_of(block_place)
    ctx = lax.axis_index("ctx")
    row_offset = lax.rem(ctx, SPLIT) * STEP
    live = (ctx // SPLIT < head_count[lax.axis_index("tp")]).astype(F32)
    for p in range(N_CTX):
        owner = order[p]
        pair = pieces[owner, :TOK, :]
        keys[p * TOK : (p + 1) * TOK, :] = pair
        keys_t[:, p * TOK : (p + 1) * TOK] = pair.T
        share = unpack(pieces[owner, TOK:, :])
        queries[p * SHARE : (p + 1) * SHARE, :] = jnp.concatenate(
            [share, jnp.zeros((SHARE, HD), BF)], axis=1
        )
    for first in range(0, ROWS, GROUP):
        low, high = group_keys(first)
        block = queries[first : first + GROUP, :]
        edge = jnp.where(
            allowed_keys(first, row_offset), dot_nt(keys[low:high, :], block), NEGATIVE
        )
        top = jnp.max(edge, axis=0, keepdims=True)
        if low:
            body = dot_nt(keys[:low, :], block)
            top = jnp.maximum(top, jnp.max(body, axis=0, keepdims=True))
        weights = jnp.exp(edge - top)
        total = jnp.sum(weights, axis=0, keepdims=True)
        mixed = dot(keys_t[HD:, low:high], weights.astype(BF))
        if low:
            weights = jnp.exp(body - top)
            total = total + jnp.sum(weights, axis=0, keepdims=True)
            mixed = mixed + dot(keys_t[HD:, :low], weights.astype(BF))
        out_t[:, first : first + GROUP] = mixed / total * live
        lse[:, first : first + GROUP] = top + jnp.log(total)
    for p in range(N_CTX):
        packed[p] = pack(out_t[:, p * SHARE : (p + 1) * SHARE].T.astype(BF))
    greeted()

    def prepare(k, peer):
        stage[k] = packed[block_place[peer]]

    steps = exchange_steps(
        False, lambda k, peer: stage.at[k], arrived, scratch[:3], pending, prepare
    )
    next(steps)
    next(steps)
    heads = []
    for s in range(HSLOT):
        heads.append(join_shares([unpack(arrived[SPLIT * s + j]) for j in range(SPLIT)]))
    joined = jnp.concatenate(heads, axis=1)
    attended[...] = joined
    part[...] = dot(joined, w_out[...]).astype(BF)
    take_turns(tp_steps([part], [attn], *scratch[3:], pending))
    take_turns(steps)
    finish_sends(pending)


def middle_body(
    block_place, head_count, tok, cot, attn, vecs, w_up, w_down_outside, w_out, attended,
    keys, keys_t, queries, out_t, lse,
    rest_up, rest_down, sums_mlp, grad_res, gw_out, sums, mine, theirs, mlp, pieces4,
    gn2_part, gn2, mlp_part, gw_up, gw_down, w_down, load_sem, sum_a, sum_b, red_a, red_b,
    send3, pieces3, grads, grad_q, dots, acc, packed, stage, *scratch,
):
    load = pltpu.make_async_copy(w_down_outside, w_down, load_sem)
    load.start()
    plane = Plane()
    greeted = greet(ctx_peers() + tp_peers() + [plane.partner])
    pending = []
    scatter_sems, gather_sems, tp, tp_mlp = (
        scratch[:3], scratch[3:6], scratch[6:9], scratch[9:12],
    )
    first_held, second_held, ring = scratch[12:23], scratch[23:27], scratch[27:]
    order = order_of(block_place)

    residual = tok[...].astype(F32) + (attn[...].astype(F32) + vecs[4:5, :])
    normal, inverse = normalize(residual)
    normed = (normal * vecs[2:3, :] + vecs[3:4, :]).astype(BF)
    hidden = dot(normed, w_up[...]) + vecs[6:7, :]
    cdf = 0.5 * (1.0 + lax.erf(hidden * (0.5**0.5)))
    activated = (hidden * cdf).astype(BF)
    cot_low = cot[...]
    gw_down[...] = dot_tn(activated, cot_low).astype(BF)
    greeted()

    def first_batch():
        segments = (((gw_up, 0, FIRST, 0),), ((gw_down, 0, FIRST, 0),))
        yield from reduce_first(
            plane, FIRST, segments, first_held, (sum_a, sum_b), pending, staged=True
        )
        yield from reduce_second(
            plane, FIRST, (sum_a, sum_b), second_held, (red_a, red_b), pending
        )
        yield from spread_steps(plane, FIRST, (red_a, red_b), mine, theirs, ring, pending)

    weight = first_batch()
    next(weight)
    load.wait()
    grad_act = dot_nt(cot_low, w_down[...])
    slope = cdf + hidden * jnp.exp(-0.5 * hidden * hidden) * 0.3989422804014327
    grad_hidden = (grad_act * slope).astype(BF)
    gn2_part[...] = dot_nt(grad_hidden, w_up[...]).astype(BF)
    total = tp_steps([gn2_part], [gn2], *tp, pending)
    next(total)
    gw_up[...] = dot_tn(normed, grad_hidden).astype(BF)
    next(weight)
    mlp_part[...] = dot(activated, w_down[...]).astype(BF)
    rest_up[...] = gw_up[FIRST:, :]
    rest_down[...] = gw_down[FIRST:, :]
    sums_mlp[...] = jnp.zeros_like(sums_mlp)
    sums_mlp[0:1, :] = row_sum(grad_hidden.astype(F32))
    sums_mlp[1:2, :] = row_sum(cot_low.astype(F32))
    next(weight)
    next(total)
    next(weight)
    take_turns(total)

    total = tp_steps([mlp_part], [mlp], *tp_mlp, pending)
    normal, inverse = normalize(tok[...].astype(F32) + (attn[...].astype(F32) + vecs[4:5, :]))
    grad_norm = gn2[...].astype(F32)
    grad = cot[...].astype(F32) + norm_backward(grad_norm, normal, inverse, vecs[2:3, :])
    grad_low = grad.astype(BF)
    live_lanes = head_count[lax.axis_index("tp")] * HD
    lane = lax.broadcasted_iota(jnp.int32, (1, HSLOT * HD), 1)
    live = (lane < live_lanes).astype(F32)
    grad_att = (dot_nt(grad_low, w_out[...]) * live).astype(BF)
    for s in range(HSLOT):
        head = grad_att[:, HD * s : HD * (s + 1)]
        for j in range(SPLIT):
            share = head[STEP * j : STEP * j + SHARE]
            if j:
                share = jnp.concatenate([jnp.zeros((16, HD), BF), share[16:]], axis=0)
            send3[SPLIT * s + j] = pack(share)
    scatter = exchange_steps(
        True, lambda k, peer: send3.at[peer], pieces3, scatter_sems, pending
    )
    next(scatter)
    next(weight)
    next(total)
    grad_res[...] = grad
    gw_out[...] = dot_tn(attended[...], grad_low).astype(BF)
    sums[...] = jnp.zeros_like(sums)
    sums[0:1, :] = row_sum(grad_norm * normal)
    sums[1:2, :] = row_sum(grad_norm)
    sums[2:3, :] = row_sum(grad_low.astype(F32))
    acc[...] = jnp.zeros_like(acc)
    next(weight)
    next(scatter)

    row_offset = lax.rem(lax.axis_index("ctx"), SPLIT) * STEP
    for p in range(N_CTX):
        share = unpack(pieces3[order[p]])
        grads[p * SHARE : (p + 1) * SHARE, :] = jnp.concatenate(
            [jnp.zeros((SHARE, HD), BF), share], axis=1
        )
    for first in range(0, ROWS, GROUP):
        turned = grads[first : first + GROUP, :].astype(F32).T
        dots[:, first : first + GROUP] = jnp.sum(
            turned[HD:, :] * out_t[:, first : first + GROUP], axis=0, keepdims=True
        )
    for first in range(0, ROWS, GROUP):
        low, high = group_keys(first)
        span = slice(first, first + GROUP)
        both = jnp.concatenate([queries[span, :], grads[span, :]], axis=0)
        grad_block = jnp.zeros((HD, GROUP), F32)
        for start, stop in ((0, low), (low, high)):
            if start == stop:
                continue
            scores = dot_nt(keys[start:stop, :], both)
            weights = jnp.exp(scores[:, :GROUP] - lse[:, span])
            if start == low:
                weights = jnp.where(allowed_keys(first, row_offset), weights, 0.0)
            grad_scores = (weights * (scores[:, GROUP:] - dots[:, span])).astype(BF)
            pair = jnp.concatenate([grad_scores, weights.astype(BF)], axis=1)
            blocks = slice(start // TOK, stop // TOK)
            acc[blocks] += dot(pair, both).reshape(-1, TOK, 2 * HD)
            grad_block = grad_block + dot(keys_t[:HD, start:stop], grad_scores)
        grad_q[:, span] = grad_block * (HD**-0.5)
        if first in (3 * GROUP, 9 * GROUP):
            next(weight)
        if first == 5 * GROUP:
            next(total)
    for p in range(N_CTX):
        packed[p] = pack(grad_q[:, p * SHARE : (p + 1) * SHARE].T.astype(BF))

    def prepare(k, peer):
        place = block_place[peer]
        stage[k, :TOK, :] = acc[place].astype(BF)
        stage[k, TOK:, :] = packed[place]

    gather = exchange_steps(
        False, lambda k, peer: stage.at[k], pieces4, gather_sems, pending, prepare
    )
    take_turns(gather, weight, total, scatter)
    finish_sends(pending)


def project_back_body(
    pieces, tok, normed, w_t, sums_mid, sums_mlp, up, down, w_out,
    gn1, mine2, theirs2, mine3, theirs3,
    gw_qkv_t, part, vec, vec_parts, vec_low, vec_got, vec_send, vec_recv, *scratch,
):
    plane = Plane()
    greeted = greet(plane.peers() + tp_peers())
    pending = []
    tp = scratch[:3]
    held2, held3 = scratch[3:28], scratch[28:]
    own3, got3 = held3[4:6]
    me = lax.axis_index("tp")

    @pl.when(plane.core == 1)
    def _():
        for ref in held2[4:6]:
            ref[HSLOT * HD - OUT_LOW :, :] = jnp.zeros((SECOND + OUT_LOW - HSLOT * HD, D), BF)
        for ref in held3[4:6]:
            ref[VEC_AT:, :] = jnp.zeros((THIRD - VEC_AT, D), BF)

    def batch(half, segments, held, mine, theirs, late=None):
        sums, reds = held[:2], held[2:4]
        yield from reduce_first(plane, half, segments, held[4:15], sums, pending, late=late)
        yield from reduce_second(plane, half, sums, held[15:19], reds, pending)
        yield from spread_steps(plane, half, reds, mine, theirs, held[19:], pending)

    second = batch(
        SECOND,
        (
            ((up, 0, REST, 0), (down, 0, REST, REST), (w_out, 0, OUT_LOW, 2 * REST)),
            ((w_out, OUT_LOW, HSLOT * HD - OUT_LOW, 0),),
        ),
        held2, mine2, theirs2,
    )
    greeted()
    next(second)
    columns, biases = [], []
    for s in range(HSLOT):
        shares = [pieces[SPLIT * s + j] for j in range(SPLIT)]
        pair = shares[0][:TOK].astype(F32)
        for piece in shares[1:]:
            pair = pair + piece[:TOK].astype(F32)
        pair = pair.astype(BF)
        queries = join_shares([unpack(piece[TOK:]) for piece in shares])
        columns += [queries, pair]
        biases += [row_sum(queries.astype(F32)), row_sum(pair.astype(F32))[:, HD:]]
    grads = jnp.concatenate(columns, axis=1)
    def add_vectors():
        for k in range(1, N_TP):
            there = vec_parts.at[lax.rem(me + N_TP - k, N_TP)]
            remote(there, there, vec_send.at[k], vec_recv.at[k], plane.partner).wait_recv()
        over_tp = vec_parts[0].astype(F32)
        for t in range(1, N_TP):
            over_tp = over_tp + vec_parts[t].astype(F32)
        row = lax.broadcasted_iota(jnp.int32, (16, 1), 0)
        vec_low[...] = jnp.where(row < 2, over_tp, vec[...]).astype(BF)
        copy = remote(vec_low, vec_got, vec_send.at[0], vec_recv.at[0], plane.partner)
        start_all([copy], pending)
        copy.wait_recv()

        @pl.when(plane.core == 1)
        def _():
            own3[VEC_AT : VEC_AT + 16, :] = vec_low[...]
            got3[VEC_AT : VEC_AT + 16, :] = vec_got[...]

    product = dot(grads, w_t[...])
    part[...] = product.astype(BF)
    total = tp_steps([part], [gn1], *tp, pending)
    next(total)
    next(second)
    normal, _ = normalize(tok[...].astype(F32))
    vec[0:1, :] = row_sum(product * normal)
    vec[1:2, :] = row_sum(product)
    vec[2:5, :] = sums_mid[0:3, :]
    vec[5:7, :] = sums_mlp[0:2, :]
    vec[7:8, : HSLOT * 2 * HD] = jnp.concatenate(biases, axis=1)
    vec[7:8, HSLOT * 2 * HD :] = jnp.zeros((1, D - HSLOT * 2 * HD), F32)
    vec[8:, :] = jnp.zeros((8, D), F32)
    vec_parts[me] = vec[...].astype(BF)
    for k in range(1, N_TP):
        copy = remote(
            vec_parts.at[me], vec_parts.at[me], vec_send.at[k], vec_recv.at[k],
            {"tp": lax.rem(me + k, N_TP)},
        )
        start_all([copy], pending)
    next(second)
    gw_qkv_t[...] = dot_tn(grads, normed[...]).astype(BF)
    third = batch(
        THIRD,
        (((gw_qkv_t, 0, THIRD, 0),), ((gw_qkv_t, THIRD, VEC_AT, 0),)),
        held3, mine3, theirs3, late=add_vectors,
    )
    next(third)
    next(second)
    take_turns(second, third, total)
    finish_sends(pending)


def finish_body(
    tok, attn, mlp, gn1, grad_res, vecs, mine1, theirs1, mine2, theirs2, mine3, theirs3,
    output_t, grad_tok_t, up_out, down_out, w_out_out, w_qkv_out, *rest,
):
    vec_outs, (up, down, w_out, w_qkv, out_sem) = rest[:8], rest[8:]
    core = lax.axis_index("seq")
    copies = []

    def by_core(action):
        pl.when(core == 0)(lambda: action(mine1, theirs1, mine2, theirs2, mine3, theirs3))
        pl.when(core == 1)(lambda: action(theirs1, mine1, theirs2, mine2, theirs3, mine3))

    def write(src, dst):
        copies.append(pltpu.make_async_copy(src, dst, out_sem.at[len(copies)]))
        copies[-1].start()

    def cast_up(low1, high1, low2, high2, low3, high3):
        up[:FIRST, :] = low1[...].astype(F32)
        up[FIRST:, :] = low2[:REST, :].astype(F32)

    def cast_down(low1, high1, low2, high2, low3, high3):
        down[:FIRST, :] = high1[...].astype(F32)
        down[FIRST:, :] = low2[REST : 2 * REST, :].astype(F32)

    def cast_qkv(low1, high1, low2, high2, low3, high3):
        w_qkv[:THIRD, :] = low3[...].astype(F32)
        w_qkv[THIRD:, :] = high3[:VEC_AT, :].astype(F32)

    def cast_rest(low1, high1, low2, high2, low3, high3):
        w_out[:OUT_LOW, :] = low2[2 * REST :, :].astype(F32)
        w_out[OUT_LOW:, :] = high2[: HSLOT * HD - OUT_LOW, :].astype(F32)
        vectors = high3[VEC_AT : VEC_AT + 16, :].astype(F32)
        for i, ref in enumerate(vec_outs):
            ref[...] = vectors[i, : ref.shape[0]]

    by_core(cast_up)
    write(up, up_out)
    by_core(cast_down)
    write(down, down_out)
    by_core(cast_qkv)
    write(w_qkv, w_qkv_out)
    by_core(cast_rest)
    write(w_out, w_out_out)
    inputs = tok[...].astype(F32)
    residual = inputs + (attn[...].astype(F32) + vecs[4:5, :])
    output_t[...] = (residual + (mlp[...].astype(F32) + vecs[5:6, :])).astype(BF).T
    normal, inverse = normalize(inputs)
    grad_norm = gn1[...].astype(F32)
    grad = grad_res[...] + norm_backward(grad_norm, normal, inverse, vecs[0:1, :])
    grad_tok_t[...] = grad.T
    for copy in copies:
        copy.wait()


def on_device(
    tokens, cotangent, block_place, head_count, ln1_gain, ln1_bias, w_qkv, b_qv, w_out, b_out,
    ln2_gain, ln2_bias, w_up, b_up, w_down, b_down,
):
    w_qkv_t = w_qkv.T
    dma = pltpu.SemaphoreType.DMA
    row_shape, piece_shape, half_shape = (
        ((TOK, D), BF), ((N_CTX, PIECE, 2 * HD), BF), ((N_CTX, HALF, 2 * HD), BF),
    )

    def buffer(shaped):
        return pltpu.VMEM(*shaped)

    pieces1, normed1, tok, cot, vecs = comm_call(
        project_body,
        1,
        [piece_shape, row_shape, row_shape, row_shape, ((8, D), F32)],
        [tokens[0].T, cotangent[0].T, w_qkv_t]
        + [ln1_gain, ln1_bias, ln2_gain, ln2_bias, b_out, b_down, b_up, b_qv],
        [OUTSIDE] * 11,
        [VM] * 5,
        [pltpu.VMEM((D, TOK), BF), pltpu.VMEM((D, TOK), BF), pltpu.VMEM((COLS, D), BF)]
        + [pltpu.VMEM((D,), BF)] * 7
        + [pltpu.VMEM((HSLOT * 2 * HD,), BF), dma((11,)), buffer(piece_shape)]
        + exchange_scratch(),
    )
    keys, keys_t, queries, out_t, lse, attended, attn = comm_call(
        attend_body,
        2,
        [
            ((N_CTX * TOK, 2 * HD), BF),
            ((2 * HD, N_CTX * TOK), BF),
            ((ROWS, 2 * HD), BF),
            ((HD, ROWS), F32),
            ((1, ROWS), F32),
            ((TOK, HSLOT * HD), BF),
            row_shape,
        ],
        [block_place, head_count, pieces1, w_out],
        [SM, SM, VM, VM],
        [VM] * 7,
        [buffer(half_shape), buffer(half_shape), buffer(half_shape), buffer(row_shape)]
        + exchange_scratch()
        + tp_scratch(1),
    )
    (
        rest_up, rest_down, sums_mlp, grad_res, gw_out, sums_mid, mine1, theirs1, mlp, pieces4
    ) = comm_call(
        middle_body,
        3,
        [
            ((REST, D), BF),
            ((REST, D), BF),
            ((8, D), F32),
            ((TOK, D), F32),
            ((HSLOT * HD, D), BF),
            ((8, D), F32),
            ((FIRST, D), BF),
            ((FIRST, D), BF),
            row_shape,
            piece_shape,
        ],
        [
            block_place, head_count, tok, cot, attn, vecs, w_up, w_down, w_out, attended,
            keys, keys_t, queries, out_t, lse,
        ],
        [SM, SM] + [VM] * 5 + [OUTSIDE] + [VM] * 7,
        [VM] * 10,
        [buffer(row_shape)] * 3
        + [pltpu.VMEM((D, D), BF)] * 3
        + [dma]
        + buffers(side_shapes(FIRST, 4) + side_shapes(FIRST, 16))
        + [buffer(half_shape), buffer(half_shape)]
        + [
            pltpu.VMEM((ROWS, 2 * HD), BF),
            pltpu.VMEM((HD, ROWS), F32),
            pltpu.VMEM((1, ROWS), F32),
            pltpu.VMEM((N_CTX, TOK, 2 * HD), F32),
            buffer(half_shape),
            buffer(piece_shape),
        ]
        + exchange_scratch()
        + exchange_scratch()
        + tp_scratch(1)
        + tp_scratch(1)
        + reduce_first_scratch(FIRST, 1)
        + reduce_second_scratch(FIRST)
        + spread_scratch(),
    )
    gn1, mine2, theirs2, mine3, theirs3 = comm_call(
        project_back_body,
        4,
        [row_shape] + [((SECOND, D), BF)] * 2 + [((THIRD, D), BF)] * 2,
        [pieces4, tok, normed1, w_qkv_t, sums_mid, sums_mlp, rest_up, rest_down, gw_out],
        [VM] * 9,
        [VM] * 5,
        [
            pltpu.VMEM((COLS, D), BF),
            buffer(row_shape),
            pltpu.VMEM((16, D), F32),
            pltpu.VMEM((N_TP, 16, D), BF),
            pltpu.VMEM((16, D), BF),
            pltpu.VMEM((16, D), BF),
            dma((N_TP,)),
            dma((N_TP,)),
        ]
        + tp_scratch(1)
        + [
            held
            for half, segments in ((SECOND, 3), (THIRD, 1))
            for held in buffers(side_shapes(half, 4) + side_shapes(half, 16))
            + reduce_first_scratch(half, segments)
            + reduce_second_scratch(half)
            + spread_scratch()
        ],
    )
    output_t, grad_tok_t, g_up, g_down, g_out, g_qkv_t, *g = local_call(
        finish_body,
        4,
        [
            ((D, TOK), BF),
            ((D, TOK), F32),
            ((D, D), F32),
            ((D, D), F32),
            ((HSLOT * HD, D), F32),
            ((COLS, D), F32),
        ]
        + [((D,), F32)] * 7
        + [((HSLOT * 2 * HD,), F32)],
        [
            tok, attn, mlp, gn1, grad_res, vecs, mine1, theirs1, mine2, theirs2, mine3, theirs3,
        ],
        out_specs=[VM, VM, HB, HB, HB, HB] + [VM] * 8,
        scratch=[
            pltpu.VMEM((D, D), F32),
            pltpu.VMEM((D, D), F32),
            pltpu.VMEM((HSLOT * HD, D), F32),
            pltpu.VMEM((COLS, D), F32),
            dma((4,)),
        ],
    )
    return (
        output_t.T[None],
        grad_tok_t.T[None],
        g[0],
        g[1],
        g_qkv_t.T,
        g[7],
        g_out,
        g[4],
        g[2],
        g[3],
        g_up,
        g[5],
        g_down,
        g[6],
    )


def solution(mesh):
    in_specs = (
        P("seq", "ctx", None), P("seq", "ctx", None), P(), P(), P(), P(), P(None, "tp"), P("tp"),
        P("tp", None), P(), P(), P(), P(None, "tp"), P("tp"), P("tp", None), P(),
    )
    out_specs = (
        P("seq", "ctx", None), P("seq", "ctx", None), P(), P(), P(None, "tp"), P("tp"),
        P("tp", None), P(), P(), P(), P(None, "tp"), P("tp"), P("tp", None), P(),
    )
    return jax.shard_map(
        on_device, mesh=mesh, in_specs=in_specs, out_specs=out_specs, check_vma=False
    )
```
